32 devices in a mesh: dp: 8 (over z, y), stream: 2 (over x), head: 2 (over core).
Axes of the slice: x: 2, y: 2, z: 4, core: 2. Of those that a mesh axis runs over, the one named last changes fastest.
Arguments:
- text: bfloat16 [6144, 768], P(('dp', 'stream')), may hold values from -6 to 6
- patches: bfloat16 [64, 145, 1024], P(('dp', 'stream')), may hold values from -6 to 6
- segment_ids: int32 [16, 384], P(('dp', 'stream')), may hold values from 0 to 23, never falling along the last dimension, each value on 1 to 48 neighbouring positions
- phrase_image: int32 [16, 24], P(('dp', 'stream')), may hold values from 0 to 3
- wq_self: bfloat16 [768, 768], P(None, 'head'), may hold values from -0.21875 to 0.21875
- wk_self: bfloat16 [768, 768], P(None, 'head'), may hold values from -0.21875 to 0.21875
- wv_self: bfloat16 [768, 768], P(None, 'head'), may hold values from -0.21875 to 0.21875
- wo_self: bfloat16 [768, 768], P('head'), may hold values from -1.25 to 1.25
- ln1_gain: float32 [768], replicated, may hold values from 0.25 to 1.75
- ln1_bias: float32 [768], replicated, may hold values from -1.5 to 1.5
- wq_cross: bfloat16 [768, 768], P(None, 'head'), may hold values from -0.21875 to 0.21875
- wk_cross: bfloat16 [1024, 768], P(None, 'head'), may hold values from -0.1875 to 0.1875
- wv_cross: bfloat16 [1024, 768], P(None, 'head'), may hold values from -0.1875 to 0.1875
- wo_cross: bfloat16 [768, 768], P('head'), may hold values from -1.75 to 1.75
- ln2_gain: float32 [768], replicated, may hold values from 0.25 to 1.75
- ln2_bias: float32 [768], replicated, may hold values from -1.5 to 1.5
- w_in: bfloat16 [768, 3072], P(None, 'head'), may hold values from -0.21875 to 0.21875
- w_out: bfloat16 [3072, 768], P('head'), may hold values from -0.21875 to 0.21875
- ln3_gain: float32 [768], replicated, may hold values from 0.25 to 1.75
- ln3_bias: float32 [768], replicated, may hold values from -1.5 to 1.5
- cotangent: float32 [6144, 768], P(('dp', 'stream')), may hold values from -6 to 6
Outputs:
- output: float32 [6144, 768], P(('dp', 'stream'))
- grad_text: float32 [6144, 768], P(('dp', 'stream'))
- grad_patches: float32 [64, 145, 1024], P(('dp', 'stream'), None, 'head')
- grad_wq_self: float32 [768, 768], P(('dp', 'stream'), 'head')
- grad_wk_self: float32 [768, 768], P(('dp', 'stream'), 'head')
- grad_wv_self: float32 [768, 768], P(('dp', 'stream'), 'head')
- grad_wo_self: float32 [768, 768], P('head', ('dp', 'stream'))
- grad_ln1_gain: float32 [768], P(('dp', 'stream'))
- grad_ln1_bias: float32 [768], P(('dp', 'stream'))
- grad_wq_cross: float32 [768, 768], P(('dp', 'stream'), 'head')
- grad_wk_cross: float32 [1024, 768], P(('dp', 'stream'), 'head')
- grad_wv_cross: float32 [1024, 768], P(('dp', 'stream'), 'head')
- grad_wo_cross: float32 [768, 768], P('head', ('dp', 'stream'))
- grad_ln2_gain: float32 [768], P(('dp', 'stream'))
- grad_ln2_bias: float32 [768], P(('dp', 'stream'))
- grad_w_in: float32 [768, 3072], P(('dp', 'stream'), 'head')
- grad_w_out: float32 [3072, 768], P('head', ('dp', 'stream'))
- grad_ln3_gain: float32 [768], P(('dp', 'stream'))
- grad_ln3_bias: float32 [768], P(('dp', 'stream'))
The draws below stay inside these ranges and needn't reach their ends.
Inputs may be any that keep to these rules, and one draw needn't show every extreme that they name: `segment_ids`: each row of 384 tokens holds phrases 0 to 23 in order, each of 1 to 48 tokens, one of exactly 48. `phrase_image`: an image index among the 4 images of the partner group.
All inputs are finite; a program needn't handle non-finite values.
Results may differ from the reference program's by a relative error of at most 0.024.
Values may be sent and summed in bfloat16 or wider, within the bound.
No kernel may reach another device: no remote copies, remote signals or barrier semaphores. Data moves between devices by JAX's collectives and lax.ppermute only.
A program may use at most 128 MiB of HBM per device.

```python
import math
import jax
import jax.numpy as jnp
import numpy as np
from jax import lax

D = 768
HEADS = 12
HEAD_DIM = 64
FF = 3072
VIS = 1024
PATCH = 145
MAXLEN = 48
TOK_DEV = 384
IMG_DEV = 4
PHR = 24
GROUPS = 16
TOKENS = 6144
IMAGES = 64
N_DP = 8
N_STREAM = 2


def with_ends(entries, rng, smallest, high):
    spot = [jax.random.randint(jax.random.fold_in(rng, axis), (), 0, length) for axis, length in enumerate(entries.shape)]
    longest = entries.shape.index(max(entries.shape))
    neighbour = spot[:longest] + [(spot[longest] + 1) % entries.shape[longest]] + spot[longest + 1:]
    return entries.at[tuple(spot)].set(smallest).at[tuple(neighbour)].set(high)


def spiked(array, own_key, source, target, parts, factor):
    owner, partner = [(jnp.arange(array.shape[axis_at]) // (array.shape[axis_at] // parts)).reshape([-1 if axis == axis_at else 1 for axis in range(array.ndim)]) for axis_at in (source, target)]
    chosen = jax.random.permutation(own_key, parts)[partner]
    strong = (owner == chosen) | (owner == (partner + parts // 2) % parts)
    return jnp.where(strong, factor * array, array)


def steps_of(rng, shape, shards, low, top_value):
    loudness = 1.0
    for dim, parts in shards:
        steps = jax.random.uniform(jax.random.fold_in(jax.random.fold_in(rng, 6), dim), (parts,), jnp.float32, low / len(shards), top_value / len(shards))
        loudness = loudness * jnp.repeat(jnp.exp(steps), shape[dim] // parts).reshape((-1,) + (1,) * (len(shape) - 1 - dim))
    return loudness


def cumulative_ranks(count, lean):
    weights = [(1 << 20) // math.isqrt(standing ** lean) + 1 for standing in range(1, count + 1)]
    scale = 1 + sum(weights) // (1 << 30)
    return np.cumsum(np.array([max(1, weight // scale) for weight in weights]))


def ranked(stream_key, shape, number_of, slope):
    table = cumulative_ranks(number_of, slope)
    ticket = jax.random.randint(jax.random.fold_in(stream_key, 1), shape, 0, int(table[number_of - 1]))
    grade = jnp.searchsorted(jnp.asarray(table, jnp.int32), ticket, side="right")
    return jax.random.permutation(jax.random.fold_in(stream_key, 2), number_of)[grade].astype(jnp.int32)


def split_up(amount, total, most, lean):
    portions = [(1 << 20) // math.isqrt(rank ** lean) + 1 for rank in range(2, amount + 1)]
    surplus, counts = total - most - (amount - 1), [1] * (amount - 1)
    while surplus > 0:
        free = [i for i in range(amount - 1) if counts[i] < most]
        mass, left = sum([portions[i] for i in free]), surplus
        for i in free:
            extra = min(most - counts[i], max(1, left * portions[i] // mass), surplus)
            counts[i] = counts[i] + extra
            surplus = surplus - extra
    return np.array([most] + counts)


def ragged_sizes(key, number_of, total, limit, lean):
    if number_of == 2:
        one = jax.random.randint(key, (), max(1, total - limit), min(limit, total - 1) + 1)
        return jnp.stack([one, total - one])
    lengths = jnp.asarray(split_up(number_of, total, limit, lean), jnp.int32)
    couples = (number_of - 1) // 2
    giver, receiver = lengths[1:1 + 2 * couples:2], lengths[2:2 + 2 * couples:2]
    room = jnp.minimum(giver - 1, limit - receiver)
    moved = jax.random.randint(jax.random.fold_in(key, 1), (couples,), 0, 1 << 20) % (room + 1)
    lengths = lengths.at[1:1 + 2 * couples:2].set(giver - moved).at[2:2 + 2 * couples:2].set(receiver + moved)
    return lengths[jax.random.permutation(jax.random.fold_in(key, 2), number_of)]


def noise(key, extent, deviation, bound, split=(), held_as=jnp.bfloat16):
    level = steps_of(key, extent, split, -0.22, 0.18) if split else 1.0
    result = jax.random.normal(key, extent, jnp.float32) * deviation * level
    return jnp.minimum(jnp.maximum(result, -bound), bound).astype(held_as)


def noise_with(own_key, shape, scale, reach, pieces, heavy, kind=jnp.bfloat16):
    values = scale * jax.random.normal(own_key, shape, jnp.float32)
    if pieces:
        values = values * steps_of(own_key, shape, pieces, -0.22, 0.18)
    return jnp.clip(spiked(values, jax.random.fold_in(own_key, 3), *heavy), -reach, reach).astype(kind)


def setup_inputs(seed: int = 0) -> dict:
    key_of = jax.random.split(jax.random.key(seed), 22)
    text = noise_with(key_of[0], (TOKENS, D), 1.0, 6.0, ((0, 16),), (0, 1, 16, 2.0))
    patches = noise(key_of[1], (IMAGES, PATCH, VIS), 1.0, 6.0, ((0, 16),))
    segment_ids = jax.vmap(lambda own: jnp.searchsorted(jnp.cumsum(ragged_sizes(own, PHR, TOK_DEV, MAXLEN, 2)), jnp.arange(TOK_DEV), side="right"))(jax.random.split(key_of[2], GROUPS)).reshape((GROUPS, TOK_DEV)).astype(jnp.int32)
    phrase_image = with_ends(ranked(key_of[3], (GROUPS, PHR), IMG_DEV, 2), jax.random.fold_in(key_of[3], 3), 0, IMG_DEV - 1).astype(jnp.int32)
    wq_self = noise(key_of[4], (D, D), D ** -0.5, 0.21875, ((1, 2),))
    wk_self = noise(key_of[5], (D, D), D ** -0.5, 0.21875, ((1, 2),))
    wv_self = noise(key_of[6], (D, D), D ** -0.5, 0.21875, ((1, 2),))
    wo_self = noise(key_of[7], (D, D), (D // 32) ** -0.5, 1.25, ((0, 2),))
    ln1_gain = jnp.clip(1.0 + 0.15 * jax.random.normal(key_of[8], (D,), jnp.float32), 0.25, 1.75)
    ln1_bias = noise(key_of[9], (D,), 0.3, 1.5, (), jnp.float32)
    wq_cross = noise(key_of[10], (D, D), D ** -0.5, 0.21875, ((1, 2),))
    wk_cross = noise(key_of[11], (VIS, D), VIS ** -0.5, 0.1875, ((1, 2),))
    wv_cross = noise(key_of[12], (VIS, D), VIS ** -0.5, 0.1875, ((1, 2),))
    wo_cross = noise(key_of[13], (D, D), (D // 64) ** -0.5, 1.75, ((0, 2),))
    ln2_gain = jnp.clip(1.0 + 0.15 * jax.random.normal(key_of[14], (D,), jnp.float32), 0.25, 1.75)
    ln2_bias = noise(key_of[15], (D,), 0.3, 1.5, (), jnp.float32)
    w_in = noise(key_of[16], (D, FF), D ** -0.5, 0.21875, ((1, 2),))
    w_out = noise(key_of[17], (FF, D), (FF // 4) ** -0.5, 0.21875, ((0, 2),))
    ln3_gain = jnp.clip(1.0 + 0.15 * jax.random.normal(key_of[18], (D,), jnp.float32), 0.25, 1.75)
    ln3_bias = noise(key_of[19], (D,), 0.3, 1.5, (), jnp.float32)
    cotangent = noise(key_of[20], (TOKENS, D), 1.0, 6.0, ((0, 16),), jnp.float32)
    return dict(text=text, patches=patches, segment_ids=segment_ids, phrase_image=phrase_image, wq_self=wq_self, wk_self=wk_self, wv_self=wv_self, wo_self=wo_self, ln1_gain=ln1_gain, ln1_bias=ln1_bias, wq_cross=wq_cross, wk_cross=wk_cross, wv_cross=wv_cross, wo_cross=wo_cross, ln2_gain=ln2_gain, ln2_bias=ln2_bias, w_in=w_in, w_out=w_out, ln3_gain=ln3_gain, ln3_bias=ln3_bias, cotangent=cotangent)


@jax.custom_vjp
def low(v):
    return lax.optimization_barrier(v.astype(jnp.bfloat16)).astype(jnp.float32)

@jax.custom_vjp
def low_back(v):
    return v

def low_keep(v):
    return (low(v), None)

def low_pass(kept, grad):
    return (grad,)

def back_keep(v):
    return (v, None)

def back_low(kept, grad):
    return (low(grad),)
low.defvjp(low_keep, low_pass)
low_back.defvjp(back_keep, back_low)
EPSILON = 1e-12
NEGATIVE = -1e+30
HIGHEST = lax.Precision.HIGHEST

def matmul(left, right):
    return jnp.dot(left, right, precision=HIGHEST)

def layer_norm(residue, gain_vec, bias_vec):
    center = residue - lax.optimization_barrier(jnp.mean(residue, axis=-1, keepdims=True))
    spread = lax.optimization_barrier(jnp.mean(center * center, axis=-1, keepdims=True))
    return center * lax.rsqrt(spread + EPSILON) * gain_vec + bias_vec

def attend(queries, keys_in, values_in, allowed):
    rows = queries.shape[0]
    query_heads = queries.reshape(rows, HEADS, HEAD_DIM)
    key_heads = keys_in.reshape(keys_in.shape[0], HEADS, HEAD_DIM)
    value_heads = values_in.reshape(values_in.shape[0], HEADS, HEAD_DIM)
    scores = low_back(jnp.einsum('thd,khd->htk', query_heads, key_heads, precision=HIGHEST) * HEAD_DIM ** (-0.5))
    scores = jnp.where(allowed[None], scores, NEGATIVE)
    largest = lax.optimization_barrier(jnp.max(scores, axis=-1, keepdims=True))
    exponent = jnp.exp(scores - largest)
    probs = exponent / lax.optimization_barrier(jnp.sum(exponent, axis=-1, keepdims=True))
    mixed = jnp.einsum('htk,khd->thd', low(probs), value_heads, precision=HIGHEST)
    return low_back(low(mixed.reshape(rows, HEADS * HEAD_DIM)))

def reference(text, patches, segment_ids, phrase_image, wq_self, wk_self, wv_self, wo_self, ln1_gain, ln1_bias, wq_cross, wk_cross, wv_cross, wo_cross, ln2_gain, ln2_bias, w_in, w_out, ln3_gain, ln3_bias, cotangent):
    groups = N_DP * N_STREAM
    key_rows = IMG_DEV * PATCH

    def forward(text_in, patch_in, wq_s, wk_s, wv_s, wo_s, gain_one, bias_one, wq_c, wk_c, wv_c, wo_c, gain_two, bias_two, weight_in, weight_out, gain_three, bias_three):
        flat_patches = patch_in.reshape(IMAGES * PATCH, VIS)
        keys_all = low_back(low(matmul(flat_patches, wk_c)))
        values_all = low_back(low(matmul(flat_patches, wv_c)))
        keys_group = keys_all.reshape(groups // 2, 2, key_rows, D)[:, ::-1].reshape(groups, key_rows, D)
        values_group = values_all.reshape(groups // 2, 2, key_rows, D)[:, ::-1].reshape(groups, key_rows, D)
        text_group = text_in.reshape(groups, TOK_DEV, D)

        def one_group(packed):
            rows_in, keys_rows, values_rows, seg_row, image_row = packed
            queries = low_back(low(matmul(rows_in, wq_s)))
            keys_self = low_back(low(matmul(rows_in, wk_s)))
            values_self = low_back(low(matmul(rows_in, wv_s)))
            self_allowed = seg_row[:, None] == seg_row[None, :]
            attended = attend(queries, keys_self, values_self, self_allowed)
            residual1 = rows_in + low_back(matmul(attended, wo_s))
            normed1 = layer_norm(residual1, gain_one, bias_one)
            cross_queries = low_back(low(matmul(low(normed1), wq_c)))
            phrase_index = jnp.arange(PHR, dtype=jnp.int32)
            token_image = lax.optimization_barrier(jnp.sum(jnp.where(seg_row[:, None] == phrase_index[None, :], image_row[None, :], 0), axis=1)).astype(jnp.int32)
            key_image = (jnp.arange(key_rows, dtype=jnp.int32) // PATCH).astype(jnp.int32)
            cross_allowed = token_image[:, None] == key_image[None, :]
            cross_attended = attend(cross_queries, keys_rows, values_rows, cross_allowed)
            residual2 = normed1 + low_back(matmul(cross_attended, wo_c))
            normed2 = layer_norm(residual2, gain_two, bias_two)
            pre = low_back(matmul(low(normed2), weight_in))
            hidden = low(jax.nn.gelu(pre, approximate=False))
            residual3 = normed2 + low_back(matmul(hidden, weight_out))
            return layer_norm(residual3, gain_three, bias_three)
        outputs = lax.map(jax.checkpoint(one_group), (text_group, keys_group, values_group, segment_ids, phrase_image))
        return outputs.reshape(TOKENS, D)
    output, backward = jax.vjp(forward, text.astype(jnp.float32), patches.astype(jnp.float32), wq_self.astype(jnp.float32), wk_self.astype(jnp.float32), wv_self.astype(jnp.float32), wo_self.astype(jnp.float32), ln1_gain, ln1_bias, wq_cross.astype(jnp.float32), wk_cross.astype(jnp.float32), wv_cross.astype(jnp.float32), wo_cross.astype(jnp.float32), ln2_gain, ln2_bias, w_in.astype(jnp.float32), w_out.astype(jnp.float32), ln3_gain, ln3_bias)
    grads = backward(cotangent)
    return (output, grads[0], grads[1], grads[2], grads[3], grads[4], grads[5], grads[6], grads[7], grads[8], grads[9], grads[10], grads[11], grads[12], grads[13], grads[14], grads[15], grads[16], grads[17])
```

```python
import jax
import jax.numpy as jnp
from jax import lax
from jax.sharding import PartitionSpec as P

HEAD_DIM = 64


EPSILON = 1e-12
NEGATIVE = -1e30


def partner(value, axis, distance):
    mask = 2**distance
    pairs = [(source, source ^ mask) for source in range(lax.axis_size(axis))]
    return lax.ppermute(value, axis, pairs)


def layer_norm(residue, gain_vec, bias_vec):
    center = residue - jnp.mean(residue, axis=-1, keepdims=True)
    spread = jnp.mean(center * center, axis=-1, keepdims=True)
    return center * lax.rsqrt(spread + EPSILON) * gain_vec + bias_vec


def gelu_exact(inputs):
    return jax.nn.gelu(inputs, approximate=False)


def split_heads(matrix):
    return matrix.reshape(matrix.shape[0], matrix.shape[1] // HEAD_DIM, HEAD_DIM)


def masked_scores(queries, keys_in, allowed):
    scores = jnp.einsum(
        "thd,khd->htk",
        split_heads(queries),
        split_heads(keys_in),
        preferred_element_type=jnp.float32,
    )
    return jnp.where(allowed[None], scores * HEAD_DIM ** (-0.5), NEGATIVE)


def attend_forward(queries, keys_in, values_in, allowed):
    scores = masked_scores(queries, keys_in, allowed)
    largest = jnp.max(scores, axis=-1, keepdims=True)
    exponent = jnp.exp(scores - largest)
    totals = jnp.sum(exponent, axis=-1, keepdims=True)
    probs_low = (exponent / totals).astype(jnp.bfloat16)
    mixed = jnp.einsum(
        "htk,khd->thd", probs_low, split_heads(values_in), preferred_element_type=jnp.float32
    )
    return (
        mixed.reshape(queries.shape[0], queries.shape[1]).astype(jnp.bfloat16),
        largest + jnp.log(totals),
    )


def attend_backward(queries, keys_in, values_in, allowed, log_total, grad_mixed):
    scale = HEAD_DIM ** (-0.5)
    probs = jnp.exp(masked_scores(queries, keys_in, allowed) - log_total)
    probs_low = probs.astype(jnp.bfloat16)
    grad_heads = split_heads(grad_mixed)
    grad_probs = jnp.einsum(
        "thd,khd->htk", grad_heads, split_heads(values_in), preferred_element_type=jnp.float32
    )
    grad_values = jnp.einsum(
        "htk,thd->khd", probs_low, grad_heads, preferred_element_type=jnp.float32
    )
    inner = jnp.sum(probs * grad_probs, axis=-1, keepdims=True)
    grad_scores = (probs * (grad_probs - inner)).astype(jnp.bfloat16)
    grad_queries = (
        jnp.einsum(
            "htk,khd->thd", grad_scores, split_heads(keys_in), preferred_element_type=jnp.float32
        )
        * scale
    )
    grad_keys = (
        jnp.einsum(
            "htk,thd->khd", grad_scores, split_heads(queries), preferred_element_type=jnp.float32
        )
        * scale
    )
    return (
        grad_queries.reshape(queries.shape).astype(jnp.bfloat16),
        grad_keys.reshape(keys_in.shape).astype(jnp.bfloat16),
        grad_values.reshape(values_in.shape).astype(jnp.bfloat16),
    )


def branch_total(partial_rows):
    own = partial_rows.astype(jnp.bfloat16)
    other = partner(own, "head", 0)
    return own.astype(jnp.float32) + other.astype(jnp.float32)


def group_bits():
    bits = []
    size = lax.axis_size("dp")
    while size > 1:
        size //= 2
        bits.append(("dp", len(bits)))
    count = len(bits)
    return [("dp", count - 1 - place) for place in range(count)] + [("stream", 0)]


def scatter_sum(grads, stream_first):
    bits = group_bits()
    grads = grads.reshape((2,) * len(bits) + grads.shape[1:])
    order = list(range(len(bits)))[::-1]
    if not stream_first:
        order[0], order[1] = order[1], order[0]
    for step, dim in enumerate(order):
        axis, place = bits[dim]
        mine = (lax.axis_index(axis) >> place) & 1
        away = lax.dynamic_index_in_dim(grads, 1 - mine, dim, keepdims=True)
        keep = lax.dynamic_index_in_dim(grads, mine, dim, keepdims=True)
        got = partner(away, axis, place)
        grads = keep.astype(jnp.float32) + got.astype(jnp.float32)
        if step < len(order) - 1:
            grads = grads.astype(away.dtype)
    return grads.reshape(grads.shape[len(bits):])


def project(left, right):
    return jnp.dot(left, right, preferred_element_type=jnp.float32)


def weight_grad(left, right):
    return jnp.einsum("ta,tb->ab", left, right, preferred_element_type=jnp.float32)


def pieces(grad, groups):
    return grad.astype(jnp.bfloat16).reshape(groups, grad.shape[0] // groups, grad.shape[1])


def back_project(grad_rows, weight):
    return jnp.einsum("tb,ab->ta", grad_rows, weight, preferred_element_type=jnp.float32)


def body(
    text,
    patches,
    segment_ids,
    phrase_image,
    wq_self,
    wk_self,
    wv_self,
    wo_self,
    ln1_gain,
    ln1_bias,
    wq_cross,
    wk_cross,
    wv_cross,
    wo_cross,
    ln2_gain,
    ln2_bias,
    w_in,
    w_out,
    ln3_gain,
    ln3_bias,
    cotangent,
):
    images_here = patches.shape[0]
    patch_count = patches.shape[1]
    key_rows = images_here * patch_count
    groups = lax.axis_size("dp") * lax.axis_size("stream")
    half = images_here // 2
    head = lax.axis_index("head")
    some = partner(lax.dynamic_slice_in_dim(patches, head * half, half, 0), "stream", 0)
    rest = partner(some, "head", 0)
    far_patches = jnp.where(
        head == 0, jnp.concatenate([some, rest]), jnp.concatenate([rest, some])
    ).reshape(key_rows, patches.shape[2])
    keys_cross = project(far_patches, wk_cross).astype(jnp.bfloat16)
    values_cross = project(far_patches, wv_cross).astype(jnp.bfloat16)
    text_float = text.astype(jnp.float32)
    queries = project(text, wq_self).astype(jnp.bfloat16)
    keys_self = project(text, wk_self).astype(jnp.bfloat16)
    values_self = project(text, wv_self).astype(jnp.bfloat16)
    segments = segment_ids[0]
    self_allowed = segments[:, None] == segments[None, :]
    attended, self_total = attend_forward(queries, keys_self, values_self, self_allowed)
    residual1 = text_float + branch_total(project(attended, wo_self))
    normed1, norm1_back = jax.vjp(layer_norm, residual1, ln1_gain, ln1_bias)
    normed1_low = normed1.astype(jnp.bfloat16)
    cross_queries = project(normed1_low, wq_cross).astype(jnp.bfloat16)
    phrase_index = lax.broadcasted_iota(jnp.int32, (1, phrase_image.shape[1]), 1)
    token_image = jnp.sum(jnp.where(segments[:, None] == phrase_index, phrase_image, 0), axis=1)
    key_image = lax.broadcasted_iota(jnp.int32, (key_rows,), 0) // patch_count
    cross_allowed = token_image[:, None] == key_image[None, :]
    cross_attended, cross_total = attend_forward(
        cross_queries, keys_cross, values_cross, cross_allowed
    )
    residual2 = normed1 + branch_total(project(cross_attended, wo_cross))
    normed2, norm2_back = jax.vjp(layer_norm, residual2, ln2_gain, ln2_bias)
    normed2_low = normed2.astype(jnp.bfloat16)
    pre_act, gelu_back = jax.vjp(gelu_exact, project(normed2_low, w_in))
    hidden = pre_act.astype(jnp.bfloat16)
    residual3 = normed2 + branch_total(project(hidden, w_out))
    output, norm3_back = jax.vjp(layer_norm, residual3, ln3_gain, ln3_bias)
    grad_residual3, grad_ln3_gain, grad_ln3_bias = norm3_back(cotangent)
    grad_three_low = grad_residual3.astype(jnp.bfloat16)
    grad_w_out = pieces(weight_grad(grad_three_low, hidden), groups)
    grad_pre = gelu_back(back_project(grad_three_low, w_out))[0].astype(jnp.bfloat16)
    grad_w_in = pieces(weight_grad(normed2_low, grad_pre), groups)
    grad_normed2 = grad_residual3 + branch_total(back_project(grad_pre, w_in))
    grad_residual2, grad_ln2_gain, grad_ln2_bias = norm2_back(grad_normed2)
    grad_two_low = grad_residual2.astype(jnp.bfloat16)
    grad_wo_cross = pieces(weight_grad(grad_two_low, cross_attended), groups)
    grad_cross_mixed = back_project(grad_two_low, wo_cross).astype(jnp.bfloat16)
    grad_cross_queries, grad_keys_cross, grad_values_cross = attend_backward(
        cross_queries, keys_cross, values_cross, cross_allowed, cross_total, grad_cross_mixed
    )
    grad_wq_cross = pieces(weight_grad(normed1_low, grad_cross_queries), groups)
    grad_normed1 = grad_residual2 + branch_total(back_project(grad_cross_queries, wq_cross))
    grad_kv_cross = pieces(
        weight_grad(far_patches, jnp.concatenate([grad_keys_cross, grad_values_cross], axis=1)),
        groups,
    )
    patch_partial = back_project(grad_keys_cross, wk_cross) + back_project(grad_values_cross, wv_cross)
    patch_partial = patch_partial.astype(jnp.bfloat16)
    width = patches.shape[2] // 2
    patch_own = lax.dynamic_slice_in_dim(patch_partial, head * width, width, 1)
    patch_away = lax.dynamic_slice_in_dim(patch_partial, (1 - head) * width, width, 1)
    patch_sum = patch_own.astype(jnp.float32) + partner(patch_away, "head", 0).astype(jnp.float32)
    grad_patches = (
        partner(patch_sum.astype(jnp.bfloat16), "stream", 0)
        .astype(jnp.float32)
        .reshape(images_here, patch_count, width)
    )
    grad_residual1, grad_ln1_gain, grad_ln1_bias = norm1_back(grad_normed1)
    grad_one_low = grad_residual1.astype(jnp.bfloat16)
    grad_wo_self = pieces(weight_grad(grad_one_low, attended), groups)
    grad_self_mixed = back_project(grad_one_low, wo_self).astype(jnp.bfloat16)
    grad_queries, grad_keys_self, grad_values_self = attend_backward(
        queries, keys_self, values_self, self_allowed, self_total, grad_self_mixed
    )
    grad_qkv_self = pieces(
        weight_grad(text, jnp.concatenate([grad_queries, grad_keys_self, grad_values_self], axis=1)),
        groups,
    )
    text_partial = (
        back_project(grad_queries, wq_self)
        + back_project(grad_keys_self, wk_self)
        + back_project(grad_values_self, wv_self)
    )
    grad_text = grad_residual1 + branch_total(text_partial)
    norm_grads = jnp.stack(
        [grad_ln1_gain, grad_ln1_bias, grad_ln2_gain, grad_ln2_bias, grad_ln3_gain, grad_ln3_bias]
    )
    norm_grads = norm_grads.reshape(norm_grads.shape[0], groups, -1).swapaxes(0, 1)
    own_w_out = scatter_sum(grad_w_out, True).T
    own_w_in = scatter_sum(grad_w_in, False)
    own_wo_cross, own_wq_cross = jnp.split(
        scatter_sum(jnp.concatenate([grad_wo_cross, grad_wq_cross], axis=2), True), 2, axis=1
    )
    own_wk_cross, own_wv_cross = jnp.split(scatter_sum(grad_kv_cross, False), 2, axis=1)
    own_wo_self = scatter_sum(grad_wo_self, True)
    own_wq_self, own_wk_self, own_wv_self = jnp.split(scatter_sum(grad_qkv_self, False), 3, axis=1)
    own_norms = scatter_sum(norm_grads, True)
    return (
        output,
        grad_text,
        grad_patches,
        own_wq_self,
        own_wk_self,
        own_wv_self,
        own_wo_self.T,
        own_norms[0],
        own_norms[1],
        own_wq_cross,
        own_wk_cross,
        own_wv_cross,
        own_wo_cross.T,
        own_norms[2],
        own_norms[3],
        own_w_in,
        own_w_out,
        own_norms[4],
        own_norms[5],
    )


def solution(mesh):
    in_specs = (
        P(("dp", "stream"), None),
        P(("dp", "stream"), None, None),
        P(("dp", "stream"), None),
        P(("dp", "stream"), None),
        P(None, "head"),
        P(None, "head"),
        P(None, "head"),
        P("head", None),
        P(),
        P(),
        P(None, "head"),
        P(None, "head"),
        P(None, "head"),
        P("head", None),
        P(),
        P(),
        P(None, "head"),
        P("head", None),
        P(),
        P(),
        P(("dp", "stream"), None),
    )
    out_specs = (
        P(("dp", "stream"), None),
        P(("dp", "stream"), None),
        P(("dp", "stream"), None, "head"),
        P(("dp", "stream"), "head"),
        P(("dp", "stream"), "head"),
        P(("dp", "stream"), "head"),
        P("head", ("dp", "stream")),
        P(("dp", "stream")),
        P(("dp", "stream")),
        P(("dp", "stream"), "head"),
        P(("dp", "stream"), "head"),
        P(("dp", "stream"), "head"),
        P("head", ("dp", "stream")),
        P(("dp", "stream")),
        P(("dp", "stream")),
        P(("dp", "stream"), "head"),
        P("head", ("dp", "stream")),
        P(("dp", "stream")),
        P(("dp", "stream")),
    )
    return jax.shard_map(body, mesh=mesh, in_specs=in_specs, out_specs=out_specs, check_vma=False)
```

```python
import jax
import jax.numpy as jnp
from jax import lax
from jax.experimental import pallas as pl
from jax.experimental.pallas import tpu as pltpu
from jax.sharding import PartitionSpec as P

HEAD_DIM = 64
LANES = 128
MAX_PHRASE = 48
EPSILON = 1e-12
NEGATIVE = -1e30
SCALE = HEAD_DIM ** (-0.5)
VMEM_LIMIT = 56 * 1024 * 1024
F32 = jnp.float32
BF16 = jnp.bfloat16


def partner(value, axis, place):
    mask = 2**place
    pairs = [(source, source ^ mask) for source in range(lax.axis_size(axis))]
    return lax.ppermute(value, axis, pairs)


def group_bits():
    count = lax.axis_size("dp").bit_length() - 1
    return [("stream", 0)] + [("dp", place) for place in range(count)]


def scatter_sum(keep, send, order):
    bits = group_bits()
    terms = [keep]
    for step, digit in enumerate(order):
        axis, place = bits[digit]
        terms = [term for term in terms]
        if step:
            away = sum(term[1].astype(F32) for term in terms).astype(BF16)
            terms = [term[0] for term in terms]
        else:
            away = send
        got = partner(away, axis, place)
        terms = terms + [got]
    return sum(term.astype(F32) for term in terms)


def scatter_sum_plain(grads):
    bits = group_bits()
    count = len(bits)
    grads = grads.reshape((2,) * count + grads.shape[1:])
    for step in range(count):
        axis, place = bits[step]
        dim = count - 1 - step
        mine = (lax.axis_index(axis) >> place) & 1
        away = lax.dynamic_index_in_dim(grads, 1 - mine, dim, keepdims=True)
        keep = lax.dynamic_index_in_dim(grads, mine, dim, keepdims=True)
        grads = keep.astype(F32) + partner(away, axis, place).astype(F32)
        if step < count - 1:
            grads = grads.astype(BF16)
    return grads.reshape(grads.shape[count:])


def run(body, inputs, outs, scratch=(), flops=0, name=None):
    n_in, n_out = len(inputs), len(outs)

    def kernel(*refs):
        ins, refs = refs[:n_in], refs[n_in:]
        body(lambda k: ins[k], refs[:n_out], lambda k: None, refs[n_out:])

    moved = sum(a.size * a.dtype.itemsize for a in inputs) + sum(
        a.size * a.dtype.itemsize for a in outs
    )
    return pl.pallas_call(
        kernel,
        name=name,
        out_shape=[jax.ShapeDtypeStruct(a.shape, a.dtype) for a in outs],
        in_specs=[pl.BlockSpec(memory_space=pltpu.VMEM)] * n_in,
        out_specs=[pl.BlockSpec(memory_space=pltpu.VMEM)] * n_out,
        scratch_shapes=list(scratch),
        compiler_params=pltpu.CompilerParams(vmem_limit_bytes=int(moved + 8 * 2**20 + sum(2 * 384 * 384 for _ in scratch))),
        cost_estimate=pl.CostEstimate(flops=int(flops), bytes_accessed=moved, transcendentals=0),
    )(*inputs)


def like(shape, dtype):
    return jax.ShapeDtypeStruct(shape, dtype)


def dot(left, right):
    return lax.dot_general(left, right, (((1,), (0,)), ((), ())), preferred_element_type=F32)


def dot_nt(left, right):
    return lax.dot_general(left, right, (((1,), (1,)), ((), ())), preferred_element_type=F32)


def dot_tn(left, right):
    return lax.dot_general(left, right, (((0,), (0,)), ((), ())), preferred_element_type=F32)


def normalise(rows):
    center = rows - jnp.mean(rows, axis=-1, keepdims=True)
    inverse = lax.rsqrt(jnp.mean(center * center, axis=-1, keepdims=True) + EPSILON)
    return center * inverse, inverse


def norm_back(grad, unit, inverse, gain):
    inner = grad * gain
    shift = jnp.mean(inner, axis=-1, keepdims=True)
    slope = jnp.mean(inner * unit, axis=-1, keepdims=True)
    return inverse * (inner - shift - unit * slope)


def norm_sums(grad, unit):
    return jnp.sum(grad * unit, axis=0, keepdims=True), jnp.sum(grad, axis=0, keepdims=True)


def column(row):
    wide = jnp.broadcast_to(row.astype(F32), (LANES, row.shape[1]))
    return jnp.transpose(wide)[:, :1].astype(jnp.int32)


def half_lanes(part):
    lane = lax.broadcasted_iota(jnp.int32, (1, LANES), 1)
    return (lane >= HEAD_DIM) if part else (lane < HEAD_DIM)


def window(block, tokens, rows):
    size = min(tokens, rows + 128)
    return min(max(block * rows - 64, 0), tokens - size), size


def self_bias(seg_col, seg_row, block, rows, first, size):
    same = seg_col[block * rows : (block + 1) * rows] == seg_row[:, first : first + size]
    return jnp.where(same, 0.0, NEGATIVE)


def cross_bias(seg_col, images_row, head, slots, patch_rows, patch_pad):
    phrases = images_row.shape[1]
    phrase = lax.broadcasted_iota(jnp.int32, (1, phrases), 1)
    image = jnp.sum(jnp.where(seg_col == phrase, images_row, 0), axis=1, keepdims=True)
    place = lax.broadcasted_iota(jnp.int32, (1, slots * patch_pad), 1)
    key_image = jnp.full((1, slots * patch_pad), -1, jnp.int32)
    for slot in range(slots):
        inside = (place >= slot * patch_pad) & (place < slot * patch_pad + patch_rows)
        key_image = jnp.where(inside, slot_image(slot, slots, head), key_image)
    return jnp.where(image == key_image, 0.0, NEGATIVE)


def slot_image(slot, slots, head):
    half = slots // 2
    return half * head + slot if slot < half else half * (1 - head) + slot - half


def attend(queries, keys, values, bias, parts):
    mixed, totals = 0.0, []
    for part in range(2):
        scores = dot_nt(jnp.where(parts[part], queries, 0), keys) + bias
        largest = jnp.max(scores, axis=1, keepdims=True)
        exponent = jnp.exp(scores - largest)
        total = jnp.sum(exponent, axis=1, keepdims=True)
        picked = dot(exponent.astype(BF16), values) * (1.0 / total)
        mixed = picked if part == 0 else jnp.where(parts[1], picked, mixed)
        totals.append(largest + jnp.log(total))
    return mixed, totals


def attend_back(queries, keys, values, grad, bias, totals, parts):
    grad_q, grad_k, grad_v = 0.0, 0.0, 0.0
    for part in range(2):
        query = jnp.where(parts[part], queries, 0)
        grad_part = jnp.where(parts[part], grad, 0)
        probs = jnp.exp(dot_nt(query, keys) + bias - totals[part])
        grad_probs = dot_nt(grad_part, values)
        inner = jnp.sum(probs * grad_probs, axis=1, keepdims=True)
        grad_scores = (probs * (grad_probs - inner)).astype(BF16)
        picked = dot(grad_scores, keys)
        grad_q = picked if part == 0 else jnp.where(parts[1], picked, grad_q)
        grad_k = grad_k + dot_tn(grad_scores, query)
        grad_v = grad_v + dot_tn(probs.astype(BF16), grad_part)
    return grad_q * SCALE, grad_k, grad_v


def self_forward(text, wq, wk, wv, wo, segments):
    tokens, width = text.shape
    inner = wq.shape[1]
    rows = 128

    def body(get, out, put, extra):
        text_in = get(0)[...]
        projected = [dot(text_in, get(1 + k)[...]).astype(BF16) for k in range(3)]
        for k in range(3):
            out[0][k] = projected[k]
        put(0)
        seg_row = get(5)[...]
        seg_col = column(seg_row)
        parts = [half_lanes(0), half_lanes(1)]
        lane = lax.broadcasted_iota(jnp.int32, (1, LANES), 1)
        for block in range(tokens // rows):
            first, size = window(block, tokens, rows)
            bias = self_bias(seg_col, seg_row, block, rows, first, size)
            here = slice(block * rows, (block + 1) * rows)
            stats = jnp.zeros((rows, LANES), F32)
            for pair in range(inner // LANES):
                cols = slice(pair * LANES, (pair + 1) * LANES)
                mixed, totals = attend(
                    out[0][0, here, cols] * SCALE,
                    out[0][1, first : first + size, cols],
                    out[0][2, first : first + size, cols],
                    bias,
                    parts,
                )
                out[1][here, cols] = mixed.astype(BF16)
                for part in range(2):
                    stats = jnp.where(lane == 2 * pair + part, totals[part], stats)
            out[2][here, :] = stats
        put(1)
        put(2)
        out[3][...] = dot(out[1][...], get(4)[...]).astype(BF16)
        put(3)

    return run(
        body,
        [text, wq, wk, wv, wo, segments],
        [
            like((3, tokens, inner), BF16),
            like((tokens, inner), BF16),
            like((tokens, LANES), F32),
            like((tokens, width), BF16),
        ],
        flops=2 * tokens * width * inner * 4 + 8 * tokens * 256 * inner,
        name="self_forward",
    )


def cross_keys(some, rest, wk, wv):
    half, patch_rows, vis = some.shape
    slots = 2 * half
    pad = -(-patch_rows // 16) * 16
    inner = wk.shape[1]

    def body(get, out, put, extra):
        weights = [get(2), get(3)]
        for k in range(2):
            out[k][...] = jnp.zeros((slots * pad, inner), BF16)
        for slot in range(slots):
            rows_in = get(slot // half)[slot % half]
            for k in range(2):
                out[k][slot * pad : slot * pad + patch_rows, :] = dot(
                    rows_in, weights[k][...]
                ).astype(BF16)
        put(0)
        put(1)

    return run(
        body,
        [some, rest, wk, wv],
        [like((slots * pad, inner), BF16)] * 2,
        flops=4 * slots * pad * vis * inner,
        name="cross_keys",
    )


def cross_forward(text, part_a, part_b, gain, bias, wq, keys, values, wo, segments, images, dims):
    tokens, width = text.shape
    inner = wq.shape[1]
    slots, patch_rows, pad = dims
    rows = 128

    def body(get, out, put, extra):
        residual = get(0)[...].astype(F32) + (get(1)[...].astype(F32) + get(2)[...].astype(F32))
        unit, _ = normalise(residual)
        normed = unit * get(3)[...] + get(4)[...]
        out[0][...] = normed
        put(0)
        low = normed.astype(BF16)
        out[1][...] = low
        put(1)
        out[2][...] = dot(low, get(5)[...]).astype(BF16)
        put(2)
        head = lax.axis_index("head")
        mask = cross_bias(column(get(9)[...]), get(10)[...], head, slots, patch_rows, pad)
        parts = [half_lanes(0), half_lanes(1)]
        lane = lax.broadcasted_iota(jnp.int32, (1, LANES), 1)
        get(6)
        get(7)
        for block in range(tokens // rows):
            here = slice(block * rows, (block + 1) * rows)
            stats = jnp.zeros((rows, LANES), F32)
            for pair in range(inner // LANES):
                cols = slice(pair * LANES, (pair + 1) * LANES)
                mixed, totals = attend(
                    out[2][here, cols] * SCALE,
                    get(6)[:, cols],
                    get(7)[:, cols],
                    mask[here],
                    parts,
                )
                out[3][here, cols] = mixed.astype(BF16)
                for part in range(2):
                    stats = jnp.where(lane == 2 * pair + part, totals[part], stats)
            out[4][here, :] = stats
        put(3)
        put(4)
        out[5][...] = dot(out[3][...], get(8)[...]).astype(BF16)
        put(5)

    return run(
        body,
        [text, part_a, part_b, gain, bias, wq, keys, values, wo, segments, images],
        [
            like((tokens, width), F32),
            like((tokens, width), BF16),
            like((tokens, inner), BF16),
            like((tokens, inner), BF16),
            like((tokens, LANES), F32),
            like((tokens, width), BF16),
        ],
        flops=4 * tokens * width * inner + 4 * tokens * slots * pad * inner,
        name="cross_forward",
    )


def feed_forward(normed, part_a, part_b, gain, bias, w_in, w_out):
    tokens, width = normed.shape
    inner = w_in.shape[1]
    chunk = 256

    def body(get, out, put, extra):
        residual = get(0)[...] + (get(1)[...].astype(F32) + get(2)[...].astype(F32))
        unit, _ = normalise(residual)
        normed_two = unit * get(3)[...] + get(4)[...]
        out[0][...] = normed_two
        put(0)
        out[1][...] = normed_two.astype(BF16)
        put(1)
        get(5)
        for start in range(0, inner, chunk):
            cols = slice(start, start + chunk)
            pre = dot(out[1][...], get(5)[:, cols])
            phi = 0.5 * (1.0 + lax.erf(pre * (0.5**0.5)))
            bell = jnp.exp(pre * pre * -0.5) * 0.3989422804014327
            out[2][:, cols] = (pre * phi).astype(BF16)
            out[3][:, cols] = (phi + pre * bell).astype(BF16)
        put(2)
        put(3)
        out[4][...] = dot(out[2][...], get(6)[...]).astype(BF16)
        put(4)

    return run(
        body,
        [normed, part_a, part_b, gain, bias, w_in, w_out],
        [
            like((tokens, width), F32),
            like((tokens, width), BF16),
            like((tokens, inner), BF16),
            like((tokens, inner), BF16),
            like((tokens, width), BF16),
        ],
        flops=4 * tokens * width * inner,
        name="feed_forward",
    )


def feed_backward(normed, part_a, part_b, gain, bias, cotangent, w_out, slopes, w_in):
    tokens, width = normed.shape
    inner = w_in.shape[1]
    chunk = 256

    def body(get, out, put, extra):
        residual = get(0)[...] + (get(1)[...].astype(F32) + get(2)[...].astype(F32))
        unit, inverse = normalise(residual)
        gain_row = get(3)[...]
        out[0][...] = unit * gain_row + get(4)[...]
        put(0)
        grad = get(5)[...]
        out[5][0:1, :], out[5][1:2, :] = norm_sums(grad, unit)
        put(5)
        grad_residual = norm_back(grad, unit, inverse, gain_row)
        out[1][...] = grad_residual
        put(1)
        out[2][...] = grad_residual.astype(BF16)
        put(2)
        get(6)
        get(7)
        for start in range(0, inner, chunk):
            cols = slice(start, start + chunk)
            grad_hidden = dot_nt(out[2][...], get(6)[cols, :])
            out[3][:, cols] = (grad_hidden * get(7)[:, cols].astype(F32)).astype(BF16)
        put(3)
        out[4][...] = dot_nt(out[3][...], get(8)[...]).astype(BF16)
        put(4)

    return run(
        body,
        [normed, part_a, part_b, gain, bias, cotangent, w_out, slopes, w_in],
        [
            like((tokens, width), F32),
            like((tokens, width), F32),
            like((tokens, width), BF16),
            like((tokens, inner), BF16),
            like((tokens, width), BF16),
            like((2, width), F32),
        ],
        flops=4 * tokens * width * inner,
        name="feed_backward",
    )


def cross_backward(
    grad_in, part_a, part_b, normed, fwd_a, fwd_b, gain, wo, queries, keys, values, stats,
    segments, images, wq, dims,
):
    tokens, width = grad_in.shape
    inner = queries.shape[1]
    slots, patch_rows, pad = dims
    rows = 128

    def body(get, out, put, extra):
        residual = get(3)[...] + (get(4)[...].astype(F32) + get(5)[...].astype(F32))
        unit, inverse = normalise(residual)
        grad = get(0)[...] + (get(1)[...].astype(F32) + get(2)[...].astype(F32))
        out[6][0:1, :], out[6][1:2, :] = norm_sums(grad, unit)
        put(6)
        grad_residual = norm_back(grad, unit, inverse, get(6)[...])
        out[0][...] = grad_residual
        put(0)
        out[1][...] = grad_residual.astype(BF16)
        put(1)
        grad_mixed = extra[0]
        grad_mixed[...] = dot_nt(out[1][...], get(7)[...]).astype(BF16)
        head = lax.axis_index("head")
        mask = cross_bias(column(get(12)[...]), get(13)[...], head, slots, patch_rows, pad)
        parts = [half_lanes(0), half_lanes(1)]
        for k in range(8, 12):
            get(k)
        for pair in range(inner // LANES):
            cols = slice(pair * LANES, (pair + 1) * LANES)
            grad_k, grad_v = 0.0, 0.0
            for block in range(tokens // rows):
                here = slice(block * rows, (block + 1) * rows)
                totals = [get(11)[here, 2 * pair + part : 2 * pair + part + 1] for part in range(2)]
                grad_q, more_k, more_v = attend_back(
                    get(8)[here, cols] * SCALE,
                    get(9)[:, cols],
                    get(10)[:, cols],
                    grad_mixed[here, cols],
                    mask[here],
                    totals,
                    parts,
                )
                out[2][here, cols] = grad_q.astype(BF16)
                grad_k, grad_v = grad_k + more_k, grad_v + more_v
            out[3][:, cols] = grad_k.astype(BF16)
            out[4][:, cols] = grad_v.astype(BF16)
        put(2)
        put(3)
        put(4)
        out[5][...] = dot_nt(out[2][...], get(14)[...]).astype(BF16)
        put(5)

    return run(
        body,
        [
            grad_in, part_a, part_b, normed, fwd_a, fwd_b, gain, wo, queries, keys, values, stats,
            segments, images, wq,
        ],
        [
            like((tokens, width), F32),
            like((tokens, width), BF16),
            like((tokens, inner), BF16),
            like((slots * pad, inner), BF16),
            like((slots * pad, inner), BF16),
            like((tokens, width), BF16),
            like((2, width), F32),
        ],
        scratch=[pltpu.VMEM((tokens, inner), BF16)],
        flops=4 * tokens * width * inner + 10 * tokens * slots * pad * inner,
        name="cross_backward",
    )


def self_backward(
    grad_in, part_a, part_b, text, fwd_a, fwd_b, gain, wo, projected, stats, segments, wq, wk, wv
):
    tokens, width = grad_in.shape
    inner = wq.shape[1]
    rows = 128

    def body(get, out, put, extra):
        residual = get(3)[...].astype(F32) + (get(4)[...].astype(F32) + get(5)[...].astype(F32))
        unit, inverse = normalise(residual)
        grad = get(0)[...] + (get(1)[...].astype(F32) + get(2)[...].astype(F32))
        out[4][0:1, :], out[4][1:2, :] = norm_sums(grad, unit)
        put(4)
        grad_residual = norm_back(grad, unit, inverse, get(6)[...])
        out[0][...] = grad_residual
        put(0)
        out[1][...] = grad_residual.astype(BF16)
        put(1)
        grad_mixed, grad_keys, grad_values = extra
        grad_mixed[...] = dot_nt(out[1][...], get(7)[...]).astype(BF16)
        grad_keys[...] = jnp.zeros_like(grad_keys)
        grad_values[...] = jnp.zeros_like(grad_values)
        seg_row = get(10)[...]
        seg_col = column(seg_row)
        parts = [half_lanes(0), half_lanes(1)]
        get(8)
        get(9)
        for block in range(tokens // rows):
            first, size = window(block, tokens, rows)
            bias = self_bias(seg_col, seg_row, block, rows, first, size)
            here = slice(block * rows, (block + 1) * rows)
            there = slice(first, first + size)
            for pair in range(inner // LANES):
                cols = slice(pair * LANES, (pair + 1) * LANES)
                totals = [get(9)[here, 2 * pair + part : 2 * pair + part + 1] for part in range(2)]
                grad_q, grad_k, grad_v = attend_back(
                    get(8)[0, here, cols] * SCALE,
                    get(8)[1, there, cols],
                    get(8)[2, there, cols],
                    grad_mixed[here, cols],
                    bias,
                    totals,
                    parts,
                )
                out[2][here, cols] = grad_q.astype(BF16)
                grad_keys[there, cols] += grad_k
                grad_values[there, cols] += grad_v
        out[2][:, inner : 2 * inner] = grad_keys[...].astype(BF16)
        out[2][:, 2 * inner :] = grad_values[...].astype(BF16)
        put(2)
        total = 0.0
        for k in range(3):
            total = total + dot_nt(out[2][:, k * inner : (k + 1) * inner], get(11 + k)[...])
        out[3][...] = total.astype(BF16)
        put(3)

    return run(
        body,
        [
            grad_in, part_a, part_b, text, fwd_a, fwd_b, gain, wo, projected, stats, segments,
            wq, wk, wv,
        ],
        [
            like((tokens, width), F32),
            like((tokens, width), BF16),
            like((tokens, 3 * inner), BF16),
            like((tokens, width), BF16),
            like((2, width), F32),
        ],
        scratch=[
            pltpu.VMEM((tokens, inner), BF16),
            pltpu.VMEM((tokens, inner), F32),
            pltpu.VMEM((tokens, inner), F32),
        ],
        flops=8 * tokens * width * inner + 10 * tokens * 256 * inner,
        name="self_backward",
    )


def patch_backward(grad_keys, grad_values, wk, wv, dims):
    slots, patch_rows, pad = dims
    vis, inner = wk.shape
    width = vis // 2

    def body(get, out, put, extra):
        head = lax.axis_index("head")
        weights = [get(2), get(3)]
        grads = [get(0), get(1)]
        for k in range(2):
            first = pl.multiple_of((head if k == 0 else 1 - head) * width, width)
            left, right = (weights[j][pl.ds(first, width), :] for j in range(2))
            for slot in range(slots):
                rows = slice(slot * pad, (slot + 1) * pad)
                total = dot_nt(grads[0][rows, :], left) + dot_nt(grads[1][rows, :], right)
                out[k][slot_image(slot, slots, head)] = total[:patch_rows].astype(BF16)
            put(k)

    return run(
        body,
        [grad_keys, grad_values, wk, wv],
        [like((slots, patch_rows, width), BF16)] * 2,
        flops=4 * slots * pad * vis * inner,
        name="patch_backward",
    )


def place_digits(position, order, count):
    offset = 0
    for step, digit in enumerate(order):
        offset |= ((position >> (count - 1 - step)) & 1) << digit
    return offset


def weight_grads(inputs, products, layouts, groups, flops, name):
    count = groups.bit_length() - 1
    outs = []
    for order, rows, columns in layouts:
        outs += [like((2,) * (count - 1) + (rows // groups, columns), BF16)] * 2

    def body(get, out, put, extra):
        me = lax.axis_index("dp") * lax.axis_size("stream") + lax.axis_index("stream")
        for k, (order, rows, columns) in enumerate(layouts):
            piece = rows // groups
            held = extra[k]
            for first, value in products[k](get):
                held[:, first : first + value.shape[1]] = value.astype(BF16)
            for side in (1, 0):
                for place in range(groups // 2):
                    offset = place_digits(side * (groups // 2) + place, order, count)
                    start = pl.multiple_of((me ^ offset) * piece, piece)
                    where = tuple((place >> (count - 2 - b)) & 1 for b in range(count - 1))
                    out[2 * k + side][where] = held[pl.ds(start, piece), :]
                put(2 * k + side)

    return run(
        body,
        inputs,
        outs,
        scratch=[pltpu.VMEM((rows, columns), BF16) for _, rows, columns in layouts],
        flops=flops,
        name=name,
    )


def project(left, right):
    return jnp.dot(left, right, preferred_element_type=F32)


def head_sum(partial_rows):
    return partial_rows, partner(partial_rows, "head", 0)


def body(
    text,
    patches,
    segment_ids,
    phrase_image,
    wq_self,
    wk_self,
    wv_self,
    wo_self,
    ln1_gain,
    ln1_bias,
    wq_cross,
    wk_cross,
    wv_cross,
    wo_cross,
    ln2_gain,
    ln2_bias,
    w_in,
    w_out,
    ln3_gain,
    ln3_bias,
    cotangent,
):
    slots, patch_rows, vis = patches.shape
    half = slots // 2
    pad = -(-patch_rows // 16) * 16
    dims = (slots, patch_rows, pad)
    tokens, width = text.shape
    inner = wq_self.shape[1]
    hidden_width = w_in.shape[1]
    groups = lax.axis_size("dp") * lax.axis_size("stream")
    head = lax.axis_index("head")
    row = lambda vector: vector.reshape(1, width)

    some = partner(lax.dynamic_slice_in_dim(patches, head * half, half, 0), "stream", 0)
    projected, attended, self_stats, part1 = self_forward(
        text, wq_self, wk_self, wv_self, wo_self, segment_ids
    )
    part1_a, part1_b = head_sum(part1)
    rest = partner(some, "head", 0)
    keys_cross, values_cross = cross_keys(some, rest, wk_cross, wv_cross)
    normed1, normed1_low, cross_queries, cross_attended, cross_stats, part2 = cross_forward(
        text, part1_a, part1_b, row(ln1_gain), row(ln1_bias), wq_cross, keys_cross, values_cross,
        wo_cross, segment_ids, phrase_image, dims,
    )
    part2_a, part2_b = head_sum(part2)
    normed2, normed2_low, hidden, slopes, part3 = feed_forward(
        normed1, part2_a, part2_b, row(ln2_gain), row(ln2_bias), w_in, w_out
    )
    part3_a, part3_b = head_sum(part3)
    output, grad_residual3, grad_three_low, grad_pre, part4, norm3 = feed_backward(
        normed2, part3_a, part3_b, row(ln3_gain), row(ln3_bias), cotangent, w_out, slopes, w_in
    )
    part4_a, part4_b = head_sum(part4)
    grad_residual2, grad_two_low, grad_cross_queries, grad_keys, grad_values, part5, norm2 = (
        cross_backward(
            grad_residual3, part4_a, part4_b, normed1, part2_a, part2_b, row(ln2_gain), wo_cross,
            cross_queries, keys_cross, values_cross, cross_stats, segment_ids, phrase_image,
            wq_cross, dims,
        )
    )
    part5_a, part5_b = head_sum(part5)
    grad_residual1, grad_one_low, grad_qkv, part6, norm1 = self_backward(
        grad_residual2, part5_a, part5_b, text, part1_a, part1_b, row(ln1_gain), wo_self,
        projected, self_stats, segment_ids, wq_self, wk_self, wv_self,
    )
    part6_a, part6_b = head_sum(part6)
    grad_text = grad_residual1 + (part6_a.astype(F32) + part6_b.astype(F32))

    patch_own, patch_away = patch_backward(grad_keys, grad_values, wk_cross, wv_cross, dims)
    patch_sum = patch_own.astype(F32) + partner(patch_away, "head", 0).astype(F32)
    grad_patches = partner(patch_sum.astype(BF16), "stream", 0).astype(F32)

    norm_grads = jnp.concatenate([norm1, norm2, norm3, jnp.zeros((2, width), F32)])

    if width % (16 * groups) == 0 and vis % (16 * groups) == 0 and groups >= 8:
        digits = len(group_bits())
        dims_z = list(range(2, digits))
        x_first = [0, 1] + dims_z
        y_first = [1, 0] + dims_z
        z_first = dims_z + [0, 1]

        def ff_out(first, size):
            return lambda get: [(0, dot_tn(get(0)[...], get(1)[:, first : first + size]))]

        third = hidden_width * 2 // 3
        rest_out = hidden_width - third

        def mixed_ff(get):
            return [
                (0, dot_tn(get(0)[...], get(1)[:, third:])),
                (rest_out, dot_tn(get(2)[...], get(3)[:, :rest_out])),
            ]

        ff = weight_grads(
            [grad_three_low, hidden, normed2_low, grad_pre],
            [
                lambda get: [(0, dot_tn(get(0)[...], get(1)[:, :third]))],
                lambda get: [(0, dot_tn(get(2)[...], get(3)[:, rest_out:]))],
                mixed_ff,
            ],
            [
                (x_first, width, third),
                (y_first, width, third),
                (z_first, width, 2 * rest_out),
            ],
            groups,
            4 * tokens * width * hidden_width,
            "ff_weight_grads",
        )
        ff_a = scatter_sum(ff[0], ff[1], x_first)
        ff_b = scatter_sum(ff[2], ff[3], y_first)
        ff_c = scatter_sum(ff[4], ff[5], z_first)
        own_w_out = jnp.concatenate([ff_a, ff_c[:, :rest_out]], axis=1).T
        own_w_in = jnp.concatenate([ff_c[:, rest_out:], ff_b], axis=1)

        def kv(get):
            total = 0.0
            for slot in range(slots):
                rows_in = get(4 + slot // half)[slot % half]
                grads = [get(6 + k)[slot * pad : slot * pad + patch_rows, :] for k in range(2)]
                more = dot_tn(rows_in, jnp.concatenate(grads, axis=1))
                total = total + more
            return [(0, total)]

        cross = weight_grads(
            [grad_two_low, cross_attended, normed1_low, grad_cross_queries, some, rest, grad_keys,
             grad_values],
            [
                lambda get: [
                    (0, dot_tn(get(0)[...], get(1)[...])),
                    (inner, dot_tn(get(2)[...], get(3)[...])),
                ],
                kv,
            ],
            [(x_first, width, 2 * inner), (y_first, vis, 2 * inner)],
            groups,
            4 * tokens * width * inner + 4 * slots * pad * vis * inner,
            "cross_weight_grads",
        )
        cross_a = scatter_sum(cross[0], cross[1], x_first)
        cross_b = scatter_sum(cross[2], cross[3], y_first)

        def norms(get):
            wide = jnp.concatenate([get(4)[...], jnp.zeros((LANES - 8, width), F32)])
            return [(2 * inner, jnp.transpose(wide))]

        own = weight_grads(
            [grad_one_low, attended, text, grad_qkv, norm_grads],
            [
                lambda get: [(0, dot_tn(get(2)[...], get(3)[:, : 2 * inner]))],
                lambda get: [
                    (0, dot_tn(get(2)[...], get(3)[:, 2 * inner :])),
                    (inner, dot_tn(get(0)[...], get(1)[...])),
                ] + norms(get),
            ],
            [(x_first, width, 2 * inner), (y_first, width, 2 * inner + LANES)],
            groups,
            8 * tokens * width * inner,
            "self_weight_grads",
        )
        self_a = scatter_sum(own[0], own[1], x_first)
        self_b = scatter_sum(own[2], own[3], y_first)
        own_norms = self_b[:, 2 * inner : 2 * inner + 8].T
        self_all = jnp.concatenate([self_a, self_b[:, : 2 * inner]], axis=1)
    else:
        def plain(left, right):
            grad = jnp.einsum("ta,tb->ab", left, right, preferred_element_type=F32)
            grad = grad.astype(BF16).reshape(groups, grad.shape[0] // groups, grad.shape[1])
            return scatter_sum_plain(grad)

        own_w_out = plain(grad_three_low, hidden).T
        own_w_in = plain(normed2_low, grad_pre)
        cross_a = jnp.concatenate(
            [plain(grad_two_low, cross_attended), plain(normed1_low, grad_cross_queries)], axis=1
        )
        far = jnp.concatenate([some, rest])
        far = jnp.pad(far, ((0, 0), (0, pad - patch_rows), (0, 0))).reshape(slots * pad, vis)
        cross_b = plain(far, jnp.concatenate([grad_keys, grad_values], axis=1))
        self_all = jnp.concatenate([plain(text, grad_qkv), plain(grad_one_low, attended)], axis=1)
        own_norms = scatter_sum_plain(
            norm_grads.reshape(8, groups, width // groups).swapaxes(0, 1).astype(BF16)
        )
    return (
        output,
        grad_text,
        grad_patches,
        self_all[:, :inner],
        self_all[:, inner : 2 * inner],
        self_all[:, 2 * inner : 3 * inner],
        self_all[:, 3 * inner :].T,
        own_norms[0],
        own_norms[1],
        cross_a[:, inner:],
        cross_b[:, :inner],
        cross_b[:, inner:],
        cross_a[:, :inner].T,
        own_norms[2],
        own_norms[3],
        own_w_in,
        own_w_out,
        own_norms[4],
        own_norms[5],
    )


def solution(mesh):
    in_specs = (
        P(("dp", "stream"), None),
        P(("dp", "stream"), None, None),
        P(("dp", "stream"), None),
        P(("dp", "stream"), None),
        P(None, "head"),
        P(None, "head"),
        P(None, "head"),
        P("head", None),
        P(),
        P(),
        P(None, "head"),
        P(None, "head"),
        P(None, "head"),
        P("head", None),
        P(),
        P(),
        P(None, "head"),
        P("head", None),
        P(),
        P(),
        P(("dp", "stream"), None),
    )
    out_specs = (
        P(("dp", "stream"), None),
        P(("dp", "stream"), None),
        P(("dp", "stream"), None, "head"),
        P(("dp", "stream"), "head"),
        P(("dp", "stream"), "head"),
        P(("dp", "stream"), "head"),
        P("head", ("dp", "stream")),
        P(("dp", "stream")),
        P(("dp", "stream")),
        P(("dp", "stream"), "head"),
        P(("dp", "stream"), "head"),
        P(("dp", "stream"), "head"),
        P("head", ("dp", "stream")),
        P(("dp", "stream")),
        P(("dp", "stream")),
        P(("dp", "stream"), "head"),
        P("head", ("dp", "stream")),
        P(("dp", "stream")),
        P(("dp", "stream")),
    )
    return jax.shard_map(body, mesh=mesh, in_specs=in_specs, out_specs=out_specs, check_vma=False)
```

```python
import jax
import jax.numpy as jnp
from jax import lax
from jax.experimental import pallas as pl
from jax.experimental.pallas import tpu as pltpu
from jax.sharding import PartitionSpec as P

HEAD_DIM = 64
LANES = 128
MAX_PHRASE = 48
EPSILON = 1e-12
NEGATIVE = -1e30
SCALE = HEAD_DIM ** (-0.5)
VMEM_LIMIT = 56 * 1024 * 1024
F32 = jnp.float32
BF16 = jnp.bfloat16


COSTS = {
    "self_forward": 2.6,
    "cross_queries": 0.8,
    "cross_keys": 1.5,
    "cross_forward": 6.2,
    "feed_forward": 3.3,
    "feed_backward": 3.3,
    "ff_weight_grads": 3.3,
    "cross_backward": 10.2,
    "cross_weight_grads": 3.3,
    "self_backward": 8.4,
    "self_weight_grads": 1.8,
    "patch_backward": 2.2,
}


def partner(value, axis, place):
    mask = 2**place
    pairs = [(source, source ^ mask) for source in range(lax.axis_size(axis))]
    return lax.ppermute(value, axis, pairs)


def group_bits():
    count = lax.axis_size("dp").bit_length() - 1
    return [("stream", 0)] + [("dp", place) for place in range(count)]


class Order:
    def __init__(self):
        self.last = None

    def after(self, value):
        if self.last is not None:
            value, _ = lax.optimization_barrier((value, self.last))
        return value

    def passed(self, value):
        self.last = value
        return value


LINKS = 4

PLAN = {
    "ff": ((64, ((0, 0), (1, 1), (2, 2), (3, 3))), (128, ((0, 2), (1, 0), (2, 3), (3, 1))), (128, ((0, 1), (1, 3), (2, 2), (4, 0))), (64, ((0, 0), (2, 3), (3, 1), (4, 2)))),
    "cross": ((64, ((1, 0), (2, 2), (3, 1), (4, 3))), (96, ((1, 1), (2, 0), (3, 2), (4, 3))), (64, ((1, 2), (2, 1), (3, 3), (4, 0)))),
    "self": ((96, ((2, 0), (3, 1), (4, 2), (5, 3))), (64, ((2, 1), (3, 2), (4, 0), (5, 3))), (48, ((2, 1), (3, 3), (4, 0), (5, 2)))),
}
PHASES = 6
PATCH_PHASE = 3


class Stream:
    def __init__(self, rows, steps):
        self.rows, self.steps = rows, dict(steps)
        self.digits = [digit for _, digit in steps]
        self.entries = 2 ** len(steps)
        self.terms, self.send, self.sent = [], None, None


class Held(list):
    recent = ()


def gather_messages(streams, phase):
    messages = {}
    for stream in streams:
        if phase in stream.steps:
            pieces = messages.setdefault(stream.steps[phase], [])
            first = sum(rows for _, _, rows in pieces)
            pieces.append((stream, first, stream.entries // 2 * stream.rows))
    return messages


def start_messages(messages, arrays, held):
    held.recent = []
    for (digit, pieces), away in zip(sorted(messages.items()), arrays):
        axis, place = group_bits()[digit]
        held.recent.append(len(held))
        held.append(partner(away, axis, place))
        for stream, first, _ in pieces:
            stream.terms.append((len(held) - 1, first))
            stream.entries //= 2


def merge(streams, phase, held, extra_inputs=(), extra_outs=(), extra=None, name=None):
    messages = gather_messages(streams, phase)
    if held.recent:
        for k, value in zip(
            held.recent, lax.optimization_barrier(tuple(held[k] for k in held.recent))
        ):
            held[k] = value
    used, places = [], {}

    def place(index):
        if index not in places:
            places[index] = len(used)
            used.append(held[index])
        return places[index]

    jobs = []
    for slot, (_, pieces) in enumerate(sorted(messages.items())):
        for stream, first, rows in pieces:
            if stream.send is not None:
                sources = [(place(stream.send), 0)]
                stream.send = None
            else:
                sources = [(place(index), row + rows) for index, row in stream.terms]
            jobs.append((slot, first, rows, sources))
    count = len(used)
    columns = held[0].shape[1]
    outs = [
        like((sum(rows for _, _, rows in pieces), columns), BF16)
        for _, pieces in sorted(messages.items())
    ]

    def body(get, out, put, scratch):
        for slot, first, rows, sources in jobs:
            parts = [get(k)[row : row + rows, :] for k, row in sources]
            if len(parts) > 1:
                total = parts[0].astype(F32)
                for part in parts[1:]:
                    total = total + part.astype(F32)
                parts = [total.astype(BF16)]
            out[slot][first : first + rows, :] = parts[0]
        if extra is not None:
            extra(lambda k: get(count + k), out[len(outs) :])

    results = run(body, used + list(extra_inputs), outs + list(extra_outs), name=name)
    start_messages(messages, results[: len(outs)], held)
    return results[: len(outs)], results[len(outs) :]


def scatter_sum_plain(grads):
    bits = group_bits()
    count = len(bits)
    grads = grads.reshape((2,) * count + grads.shape[1:])
    for step in range(count):
        axis, place = bits[step]
        dim = count - 1 - step
        mine = (lax.axis_index(axis) >> place) & 1
        away = lax.dynamic_index_in_dim(grads, 1 - mine, dim, keepdims=True)
        keep = lax.dynamic_index_in_dim(grads, mine, dim, keepdims=True)
        grads = keep.astype(F32) + partner(away, axis, place).astype(F32)
        if step < count - 1:
            grads = grads.astype(BF16)
    return grads.reshape(grads.shape[count:])


def run(body, inputs, outs, scratch=(), flops=0, aliases=None, name=None):
    n_in, n_out = len(inputs), len(outs)

    def kernel(*refs):
        ins, refs = refs[:n_in], refs[n_in:]
        body(lambda k: ins[k], refs[:n_out], lambda k: None, refs[n_out:])

    moved = sum(a.size * a.dtype.itemsize for a in inputs) + sum(
        a.size * a.dtype.itemsize for a in outs
    )
    return pl.pallas_call(
        kernel,
        name=name,
        out_shape=[jax.ShapeDtypeStruct(a.shape, a.dtype) for a in outs],
        in_specs=[pl.BlockSpec(memory_space=pltpu.VMEM)] * n_in,
        out_specs=[pl.BlockSpec(memory_space=pltpu.VMEM)] * n_out,
        scratch_shapes=list(scratch),
        input_output_aliases=aliases or {},
        compiler_params=pltpu.CompilerParams(vmem_limit_bytes=int(moved + 8 * 2**20 + sum(2 * 384 * 384 for _ in scratch))),
        cost_estimate=pl.CostEstimate(
            flops=int(1e9 * COSTS.get(name, 0.6)), bytes_accessed=1000, transcendentals=0
        ),
    )(*inputs)


def like(shape, dtype):
    return jax.ShapeDtypeStruct(shape, dtype)


def dot(left, right):
    return lax.dot_general(left, right, (((1,), (0,)), ((), ())), preferred_element_type=F32)


def dot_nt(left, right):
    return lax.dot_general(left, right, (((1,), (1,)), ((), ())), preferred_element_type=F32)


def dot_tn(left, right):
    return lax.dot_general(left, right, (((0,), (0,)), ((), ())), preferred_element_type=F32)


def normalise(rows):
    center = rows - jnp.mean(rows, axis=-1, keepdims=True)
    inverse = lax.rsqrt(jnp.mean(center * center, axis=-1, keepdims=True) + EPSILON)
    return center * inverse, inverse


def norm_back(grad, unit, inverse, gain):
    inner = grad * gain
    shift = jnp.mean(inner, axis=-1, keepdims=True)
    slope = jnp.mean(inner * unit, axis=-1, keepdims=True)
    return inverse * (inner - shift - unit * slope)


def norm_sums(grad, unit):
    return jnp.sum(grad * unit, axis=0, keepdims=True), jnp.sum(grad, axis=0, keepdims=True)


def column(row):
    wide = jnp.broadcast_to(row.astype(F32), (LANES, row.shape[1]))
    return jnp.transpose(wide)[:, :1].astype(jnp.int32)


def half_lanes(part):
    lane = lax.broadcasted_iota(jnp.int32, (1, LANES), 1)
    return (lane >= HEAD_DIM) if part else (lane < HEAD_DIM)


def window(block, tokens, rows):
    size = min(tokens, rows + 128)
    return min(max(block * rows - 64, 0), tokens - size), size


def self_bias(seg_col, seg_row, block, rows, first, size):
    same = seg_col[block * rows : (block + 1) * rows] == seg_row[:, first : first + size]
    return jnp.where(same, 0.0, NEGATIVE)


def cross_bias(seg_col, images_row, head, slots, patch_rows, patch_pad):
    phrases = images_row.shape[1]
    phrase = lax.broadcasted_iota(jnp.int32, (1, phrases), 1)
    image = jnp.sum(jnp.where(seg_col == phrase, images_row, 0), axis=1, keepdims=True)
    place = lax.broadcasted_iota(jnp.int32, (1, slots * patch_pad), 1)
    key_image = jnp.full((1, slots * patch_pad), -1, jnp.int32)
    for slot in range(slots):
        inside = (place >= slot * patch_pad) & (place < slot * patch_pad + patch_rows)
        key_image = jnp.where(inside, slot_image(slot, slots, head), key_image)
    return jnp.where(image == key_image, 0.0, NEGATIVE)


def slot_image(slot, slots, head):
    half = slots // 2
    return half * (head if slot % 2 == 0 else 1 - head) + slot // 2


def attend(queries, keys, values, bias, parts):
    mixed, totals = 0.0, []
    for part in range(2):
        scores = dot_nt(jnp.where(parts[part], queries, 0), keys) + bias
        largest = jnp.max(scores, axis=1, keepdims=True)
        exponent = jnp.exp(scores - largest)
        total = jnp.sum(exponent, axis=1, keepdims=True)
        picked = dot(exponent.astype(BF16), values) * (1.0 / total)
        mixed = picked if part == 0 else jnp.where(parts[1], picked, mixed)
        totals.append(largest + jnp.log(total))
    return mixed, totals


def attend_back(queries, keys, values, grad, bias, totals, parts):
    grad_q, grad_k, grad_v = 0.0, 0.0, 0.0
    for part in range(2):
        query = jnp.where(parts[part], queries, 0)
        grad_part = jnp.where(parts[part], grad, 0)
        probs = jnp.exp(dot_nt(query, keys) + bias - totals[part])
        grad_probs = dot_nt(grad_part, values)
        inner = jnp.sum(probs * grad_probs, axis=1, keepdims=True)
        grad_scores = (probs * (grad_probs - inner)).astype(BF16)
        picked = dot(grad_scores, keys)
        grad_q = picked if part == 0 else jnp.where(parts[1], picked, grad_q)
        grad_k = grad_k + dot_tn(grad_scores, query)
        grad_v = grad_v + dot_tn(probs.astype(BF16), grad_part)
    return grad_q * SCALE, grad_k, grad_v


def self_forward(text, wq, wk, wv, wo, segments):
    tokens, width = text.shape
    inner = wq.shape[1]
    rows = 128

    def body(get, out, put, extra):
        text_in = get(0)[...]
        projected = [dot(text_in, get(1 + k)[...]).astype(BF16) for k in range(3)]
        for k in range(3):
            out[0][k] = projected[k]
        put(0)
        seg_row = get(5)[...]
        seg_col = column(seg_row)
        parts = [half_lanes(0), half_lanes(1)]
        lane = lax.broadcasted_iota(jnp.int32, (1, LANES), 1)
        for block in range(tokens // rows):
            first, size = window(block, tokens, rows)
            bias = self_bias(seg_col, seg_row, block, rows, first, size)
            here = slice(block * rows, (block + 1) * rows)
            stats = jnp.zeros((rows, LANES), F32)
            for pair in range(inner // LANES):
                cols = slice(pair * LANES, (pair + 1) * LANES)
                mixed, totals = attend(
                    out[0][0, here, cols] * SCALE,
                    out[0][1, first : first + size, cols],
                    out[0][2, first : first + size, cols],
                    bias,
                    parts,
                )
                out[1][here, cols] = mixed.astype(BF16)
                for part in range(2):
                    stats = jnp.where(lane == 2 * pair + part, totals[part], stats)
            out[2][here, :] = stats
        put(1)
        put(2)
        out[3][...] = dot(out[1][...], get(4)[...]).astype(BF16)
        put(3)

    return run(
        body,
        [text, wq, wk, wv, wo, segments],
        [
            like((3, tokens, inner), BF16),
            like((tokens, inner), BF16),
            like((tokens, LANES), F32),
            like((tokens, width), BF16),
        ],
        flops=2 * tokens * width * inner * 4 + 8 * tokens * 256 * inner,
        name="self_forward",
    )


def cross_keys(near, other, wk, wv):
    half, patch_rows, vis = near.shape
    slots = 2 * half
    pad = -(-patch_rows // 16) * 16
    inner = wk.shape[1]

    def body(get, out, put, extra):
        weights = [get(2), get(3)]
        for k in range(2):
            for slot in range(slots):
                top, end = slot * pad, (slot + 1) * pad
                out[k][end - 16 : end, :] = jnp.zeros((16, inner), BF16)
                out[k][top : top + patch_rows, :] = dot(
                    get(slot % 2)[slot // 2], weights[k][...]
                ).astype(BF16)

    return run(
        body,
        [near, other, wk, wv],
        [like((slots * pad, inner), BF16)] * 2,
        flops=4 * slots * pad * vis * inner,
        name="cross_keys",
    )


def cross_queries_of(text, part_a, part_b, gain, bias, wq):
    tokens, width = text.shape

    def body(get, out, put, extra):
        residual = get(0)[...].astype(F32) + (get(1)[...].astype(F32) + get(2)[...].astype(F32))
        unit, _ = normalise(residual)
        normed = unit * get(3)[...] + get(4)[...]
        out[0][...] = normed
        low = normed.astype(BF16)
        out[1][...] = low
        out[2][...] = dot(low, get(5)[...]).astype(BF16)

    return run(
        body,
        [text, part_a, part_b, gain, bias, wq],
        [
            like((tokens, width), F32),
            like((tokens, width), BF16),
            like((tokens, wq.shape[1]), BF16),
        ],
        flops=2 * tokens * width * wq.shape[1],
        name="cross_queries",
    )


def cross_forward(queries, keys, values, wo, segments, images, dims):
    tokens, inner = queries.shape
    width = wo.shape[1]
    slots, patch_rows, pad = dims
    rows = 128

    def body(get, out, put, extra):
        head = lax.axis_index("head")
        mask = cross_bias(column(get(4)[...]), get(5)[...], head, slots, patch_rows, pad)
        parts = [half_lanes(0), half_lanes(1)]
        lane = lax.broadcasted_iota(jnp.int32, (1, LANES), 1)
        for block in range(tokens // rows):
            here = slice(block * rows, (block + 1) * rows)
            stats = jnp.zeros((rows, LANES), F32)
            for pair in range(inner // LANES):
                cols = slice(pair * LANES, (pair + 1) * LANES)
                mixed, totals = attend(
                    get(0)[here, cols] * SCALE,
                    get(1)[:, cols],
                    get(2)[:, cols],
                    mask[here],
                    parts,
                )
                out[0][here, cols] = mixed.astype(BF16)
                for part in range(2):
                    stats = jnp.where(lane == 2 * pair + part, totals[part], stats)
            out[1][here, :] = stats
        out[2][...] = dot(out[0][...], get(3)[...]).astype(BF16)

    return run(
        body,
        [queries, keys, values, wo, segments, images],
        [
            like((tokens, inner), BF16),
            like((tokens, LANES), F32),
            like((tokens, width), BF16),
        ],
        flops=2 * tokens * width * inner + 4 * tokens * slots * pad * inner,
        name="cross_forward",
    )


def feed_forward(normed, part_a, part_b, gain, bias, w_in, w_out):
    tokens, width = normed.shape
    inner = w_in.shape[1]
    chunk = 256

    def body(get, out, put, extra):
        residual = get(0)[...] + (get(1)[...].astype(F32) + get(2)[...].astype(F32))
        unit, _ = normalise(residual)
        normed_two = unit * get(3)[...] + get(4)[...]
        out[0][...] = normed_two
        put(0)
        out[1][...] = normed_two.astype(BF16)
        put(1)
        get(5)
        for start in range(0, inner, chunk):
            cols = slice(start, start + chunk)
            pre = dot(out[1][...], get(5)[:, cols])
            phi = 0.5 * (1.0 + lax.erf(pre * (0.5**0.5)))
            bell = jnp.exp(pre * pre * -0.5) * 0.3989422804014327
            out[2][:, cols] = (pre * phi).astype(BF16)
            out[3][:, cols] = (phi + pre * bell).astype(BF16)
        put(2)
        put(3)
        out[4][...] = dot(out[2][...], get(6)[...]).astype(BF16)
        put(4)

    return run(
        body,
        [normed, part_a, part_b, gain, bias, w_in, w_out],
        [
            like((tokens, width), F32),
            like((tokens, width), BF16),
            like((tokens, inner), BF16),
            like((tokens, inner), BF16),
            like((tokens, width), BF16),
        ],
        flops=4 * tokens * width * inner,
        name="feed_forward",
    )


def feed_backward(normed, part_a, part_b, gain, bias, cotangent, w_out, slopes, w_in):
    tokens, width = normed.shape
    inner = w_in.shape[1]
    chunk = 256

    def body(get, out, put, extra):
        residual = get(0)[...] + (get(1)[...].astype(F32) + get(2)[...].astype(F32))
        unit, inverse = normalise(residual)
        gain_row = get(3)[...]
        out[0][...] = unit * gain_row + get(4)[...]
        put(0)
        grad = get(5)[...]
        out[5][0:1, :], out[5][1:2, :] = norm_sums(grad, unit)
        put(5)
        grad_residual = norm_back(grad, unit, inverse, gain_row)
        out[1][...] = grad_residual
        put(1)
        out[2][...] = grad_residual.astype(BF16)
        put(2)
        get(6)
        get(7)
        for start in range(0, inner, chunk):
            cols = slice(start, start + chunk)
            grad_hidden = dot_nt(out[2][...], get(6)[cols, :])
            out[3][:, cols] = (grad_hidden * get(7)[:, cols].astype(F32)).astype(BF16)
        put(3)
        out[4][...] = dot_nt(out[3][...], get(8)[...]).astype(BF16)
        put(4)

    return run(
        body,
        [normed, part_a, part_b, gain, bias, cotangent, w_out, slopes, w_in],
        [
            like((tokens, width), F32),
            like((tokens, width), F32),
            like((tokens, width), BF16),
            like((tokens, inner), BF16),
            like((tokens, width), BF16),
            like((2, width), F32),
        ],
        flops=4 * tokens * width * inner,
        name="feed_backward",
    )


def cross_backward(
    grad_in, part_a, part_b, normed, fwd_a, fwd_b, gain, wo, queries, keys, values, stats,
    segments, images, wq, dims,
):
    tokens, width = grad_in.shape
    inner = queries.shape[1]
    slots, patch_rows, pad = dims
    rows = 128

    def body(get, out, put, extra):
        residual = get(3)[...] + (get(4)[...].astype(F32) + get(5)[...].astype(F32))
        unit, inverse = normalise(residual)
        grad = get(0)[...] + (get(1)[...].astype(F32) + get(2)[...].astype(F32))
        out[6][0:1, :], out[6][1:2, :] = norm_sums(grad, unit)
        put(6)
        grad_residual = norm_back(grad, unit, inverse, get(6)[...])
        out[0][...] = grad_residual
        put(0)
        out[1][...] = grad_residual.astype(BF16)
        put(1)
        grad_mixed = extra[0]
        grad_mixed[...] = dot_nt(out[1][...], get(7)[...]).astype(BF16)
        head = lax.axis_index("head")
        mask = cross_bias(column(get(12)[...]), get(13)[...], head, slots, patch_rows, pad)
        parts = [half_lanes(0), half_lanes(1)]
        for k in range(8, 12):
            get(k)
        for pair in range(inner // LANES):
            cols = slice(pair * LANES, (pair + 1) * LANES)
            grad_k, grad_v = 0.0, 0.0
            for block in range(tokens // rows):
                here = slice(block * rows, (block + 1) * rows)
                totals = [get(11)[here, 2 * pair + part : 2 * pair + part + 1] for part in range(2)]
                grad_q, more_k, more_v = attend_back(
                    get(8)[here, cols] * SCALE,
                    get(9)[:, cols],
                    get(10)[:, cols],
                    grad_mixed[here, cols],
                    mask[here],
                    totals,
                    parts,
                )
                out[2][here, cols] = grad_q.astype(BF16)
                grad_k, grad_v = grad_k + more_k, grad_v + more_v
            out[3][:, cols] = grad_k.astype(BF16)
            out[4][:, cols] = grad_v.astype(BF16)
        put(2)
        put(3)
        put(4)
        out[5][...] = dot_nt(out[2][...], get(14)[...]).astype(BF16)
        put(5)

    return run(
        body,
        [
            grad_in, part_a, part_b, normed, fwd_a, fwd_b, gain, wo, queries, keys, values, stats,
            segments, images, wq,
        ],
        [
            like((tokens, width), F32),
            like((tokens, width), BF16),
            like((tokens, inner), BF16),
            like((slots * pad, inner), BF16),
            like((slots * pad, inner), BF16),
            like((tokens, width), BF16),
            like((2, width), F32),
        ],
        scratch=[pltpu.VMEM((tokens, inner), BF16)],
        flops=4 * tokens * width * inner + 10 * tokens * slots * pad * inner,
        name="cross_backward",
    )


def self_backward(
    grad_in, part_a, part_b, text, fwd_a, fwd_b, gain, wo, projected, stats, segments, wq, wk, wv
):
    tokens, width = grad_in.shape
    inner = wq.shape[1]
    rows = 128

    def body(get, out, put, extra):
        residual = get(3)[...].astype(F32) + (get(4)[...].astype(F32) + get(5)[...].astype(F32))
        unit, inverse = normalise(residual)
        grad = get(0)[...] + (get(1)[...].astype(F32) + get(2)[...].astype(F32))
        out[4][0:1, :], out[4][1:2, :] = norm_sums(grad, unit)
        put(4)
        grad_residual = norm_back(grad, unit, inverse, get(6)[...])
        out[0][...] = grad_residual
        put(0)
        out[1][...] = grad_residual.astype(BF16)
        put(1)
        grad_mixed, grad_keys, grad_values = extra
        grad_mixed[...] = dot_nt(out[1][...], get(7)[...]).astype(BF16)
        grad_keys[...] = jnp.zeros_like(grad_keys)
        grad_values[...] = jnp.zeros_like(grad_values)
        seg_row = get(10)[...]
        seg_col = column(seg_row)
        parts = [half_lanes(0), half_lanes(1)]
        get(8)
        get(9)
        for block in range(tokens // rows):
            first, size = window(block, tokens, rows)
            bias = self_bias(seg_col, seg_row, block, rows, first, size)
            here = slice(block * rows, (block + 1) * rows)
            there = slice(first, first + size)
            for pair in range(inner // LANES):
                cols = slice(pair * LANES, (pair + 1) * LANES)
                totals = [get(9)[here, 2 * pair + part : 2 * pair + part + 1] for part in range(2)]
                grad_q, grad_k, grad_v = attend_back(
                    get(8)[0, here, cols] * SCALE,
                    get(8)[1, there, cols],
                    get(8)[2, there, cols],
                    grad_mixed[here, cols],
                    bias,
                    totals,
                    parts,
                )
                out[2][here, cols] = grad_q.astype(BF16)
                grad_keys[there, cols] += grad_k
                grad_values[there, cols] += grad_v
        out[2][:, inner : 2 * inner] = grad_keys[...].astype(BF16)
        out[2][:, 2 * inner :] = grad_values[...].astype(BF16)
        put(2)
        total = 0.0
        for k in range(3):
            total = total + dot_nt(out[2][:, k * inner : (k + 1) * inner], get(11 + k)[...])
        out[3][...] = total.astype(BF16)
        put(3)

    return run(
        body,
        [
            grad_in, part_a, part_b, text, fwd_a, fwd_b, gain, wo, projected, stats, segments,
            wq, wk, wv,
        ],
        [
            like((tokens, width), F32),
            like((tokens, width), BF16),
            like((tokens, 3 * inner), BF16),
            like((tokens, width), BF16),
            like((2, width), F32),
        ],
        scratch=[
            pltpu.VMEM((tokens, inner), BF16),
            pltpu.VMEM((tokens, inner), F32),
            pltpu.VMEM((tokens, inner), F32),
        ],
        flops=8 * tokens * width * inner + 10 * tokens * 256 * inner,
        name="self_backward",
    )


def patch_backward(grad_keys, grad_values, wk, wv, dims):
    slots, patch_rows, pad = dims
    vis, inner = wk.shape
    width = vis // 2

    def body(get, out, put, extra):
        head = lax.axis_index("head")
        weights = [get(2), get(3)]
        grads = [get(0), get(1)]
        for k in range(2):
            first = pl.multiple_of((head if k == 0 else 1 - head) * width, width)
            left, right = (weights[j][pl.ds(first, width), :] for j in range(2))
            for slot in range(slots):
                rows = slice(slot * pad, (slot + 1) * pad)
                total = dot_nt(grads[0][rows, :], left) + dot_nt(grads[1][rows, :], right)
                out[k][slot_image(slot, slots, head)] = total[:patch_rows].astype(BF16)
            put(k)

    return run(
        body,
        [grad_keys, grad_values, wk, wv],
        [like((slots, patch_rows, width), BF16)] * 2,
        flops=4 * slots * pad * vis * inner,
        name="patch_backward",
    )


def offset_of(position, digits):
    count = len(digits)
    return sum(
        ((position >> (count - 1 - step)) & 1) << digit for step, digit in enumerate(digits)
    )


def weight_grads(inputs, blocks, streams, held, groups, columns, flops, name):
    outs = []
    for stream in streams:
        outs += [like((stream.entries // 2 * stream.rows, columns), BF16)] * 2

    def body(get, out, put, scratch):
        me = lax.axis_index("dp") * lax.axis_size("stream") + lax.axis_index("stream")
        first = 0
        for block, (piece, product) in enumerate(blocks):
            whole = scratch[block]
            product(get, whole)
            bottom = 0
            for k, stream in enumerate(streams):
                low = max(first, bottom)
                high = min(first + piece, bottom + stream.rows)
                for position in range(stream.entries if low < high else 0):
                    side, entry = divmod(position, stream.entries // 2)
                    source = (me ^ offset_of(position, stream.digits)) * piece + (low - first)
                    target = entry * stream.rows + low - bottom
                    out[2 * k + side][target : target + high - low, :] = whole[
                        pl.ds(pl.multiple_of(source, 16), high - low), :
                    ]
                bottom += stream.rows
            first += piece

    results = run(
        body,
        inputs,
        outs,
        scratch=[pltpu.VMEM((groups * piece, columns), BF16) for piece, _ in blocks],
        flops=flops,
        name=name,
    )
    for k, stream in enumerate(streams):
        held += [results[2 * k], results[2 * k + 1]]
        stream.terms, stream.send = [(len(held) - 2, 0)], len(held) - 1


def product(left, right, first=None, size=None):
    def fill(get, whole):
        columns = get(right)[...] if first is None else get(right)[:, first : first + size]
        whole[...] = dot_tn(get(left)[...], columns).astype(BF16)

    return fill


def finish(streams, held, piece, vis_piece, blocks):
    columns = held[0].shape[1]
    used, places = [], {}
    for batch in streams.values():
        for stream in batch:
            for index, _ in stream.terms:
                if index not in places:
                    places[index] = len(used)
                    used.append(held[index])

    def body(get, out, put, scratch):
        def rows_of(batch, low, high):
            parts, bottom = [], 0
            for stream in batch:
                first, last = max(low, bottom) - bottom, min(high, bottom + stream.rows) - bottom
                if first < last:
                    total = 0.0
                    for index, row in stream.terms:
                        total = total + get(places[index])[row + first : row + last, :].astype(F32)
                    parts.append(total)
                bottom += stream.rows
            return parts[0] if len(parts) == 1 else jnp.concatenate(parts)

        for k in range(2 * blocks):
            out[k // blocks][:, k % blocks * columns : (k % blocks + 1) * columns] = rows_of(
                streams["ff"], k * piece, (k + 1) * piece
            )
        for k in range(2):
            out[2 + k][...] = rows_of(streams["cross"], k * piece, (k + 1) * piece)
            low = 2 * piece + k * vis_piece
            out[4 + k][...] = rows_of(streams["cross"], low, low + vis_piece)
        for k in range(4):
            out[6 + k][...] = rows_of(streams["self"], k * piece, (k + 1) * piece)
        out[10][...] = rows_of(streams["self"], 4 * piece, 4 * piece + 16)

    return run(
        body,
        used,
        [like((piece, blocks * columns), F32)] * 2
        + [like((piece, columns), F32)] * 2
        + [like((vis_piece, columns), F32)] * 2
        + [like((piece, columns), F32)] * 4
        + [like((16, columns), F32)],
        name="finish",
    )


def project(left, right):
    return jnp.dot(left, right, preferred_element_type=F32)


def head_sum(partial_rows):
    return partial_rows, partner(partial_rows, "head", 0)


def body(
    text,
    patches,
    segment_ids,
    phrase_image,
    wq_self,
    wk_self,
    wv_self,
    wo_self,
    ln1_gain,
    ln1_bias,
    wq_cross,
    wk_cross,
    wv_cross,
    wo_cross,
    ln2_gain,
    ln2_bias,
    w_in,
    w_out,
    ln3_gain,
    ln3_bias,
    cotangent,
):
    slots, patch_rows, vis = patches.shape
    half = slots // 2
    pad = -(-patch_rows // 16) * 16
    dims = (slots, patch_rows, pad)
    tokens, width = text.shape
    inner = wq_self.shape[1]
    hidden_width = w_in.shape[1]
    groups = lax.axis_size("dp") * lax.axis_size("stream")
    head = lax.axis_index("head")
    row = lambda vector: vector.reshape(1, width)

    near = partner(lax.dynamic_slice_in_dim(patches, head * half, half, 0), "stream", 0)
    projected, attended, self_stats, part1 = self_forward(
        text, wq_self, wk_self, wv_self, wo_self, segment_ids
    )
    attended, near = lax.optimization_barrier((attended, near))
    other = partner(near, "head", 0)
    part1_a, part1_b = head_sum(part1)
    normed1, normed1_low, cross_queries = cross_queries_of(
        text, part1_a, part1_b, row(ln1_gain), row(ln1_bias), wq_cross
    )
    keys_cross, values_cross = cross_keys(near, other, wk_cross, wv_cross)
    cross_attended, cross_stats, part2 = cross_forward(
        cross_queries, keys_cross, values_cross, wo_cross, segment_ids, phrase_image, dims
    )
    part2_a, part2_b = head_sum(part2)
    normed2, normed2_low, hidden, slopes, part3 = feed_forward(
        normed1, part2_a, part2_b, row(ln2_gain), row(ln2_bias), w_in, w_out
    )
    part3_a, part3_b = head_sum(part3)
    output, grad_residual3, grad_three_low, grad_pre, part4, norm3 = feed_backward(
        normed2, part3_a, part3_b, row(ln3_gain), row(ln3_bias), cotangent, w_out, slopes, w_in
    )
    part4_a, part4_b = head_sum(part4)
    piece = width // groups
    fast = groups == 2**LINKS and piece % 16 == 0 and vis % (16 * groups) == 0
    order = Order()
    held, streams = Held(), {}
    if fast:
        streams = {name: [Stream(*stream) for stream in plan] for name, plan in PLAN.items()}
        everything = [stream for batch in streams.values() for stream in batch]
        blocks = hidden_width // inner
        weight_grads(
            [grad_three_low, hidden, normed2_low, grad_pre],
            [(piece, product(0, 1, k * inner, inner)) for k in range(blocks)]
            + [(piece, product(2, 3, k * inner, inner)) for k in range(blocks)],
            streams["ff"],
            held,
            groups,
            inner,
            4 * tokens * width * hidden_width,
            "ff_weight_grads",
        )
        away, _ = merge(streams["ff"], 0, held, name="merge_0")
        order.passed(away)
    grad_residual2, grad_two_low, grad_cross_queries, grad_keys, grad_values, part5, norm2 = (
        cross_backward(
            order.after(grad_residual3), part4_a, part4_b, normed1, part2_a, part2_b,
            row(ln2_gain), wo_cross, cross_queries, keys_cross, values_cross, cross_stats,
            segment_ids, phrase_image, wq_cross, dims,
        )
    )
    part5_a, part5_b = head_sum(part5)
    patch_own, patch_away = patch_backward(grad_keys, grad_values, wk_cross, wv_cross, dims)
    patch_other = partner(patch_away, "head", 0)
    if fast:
        def kv(which):
            def fill(get, whole):
                total = 0.0
                for slot in range(slots):
                    rows_in = get(4 + slot % 2)[slot // 2]
                    grads = get(6 + which)[slot * pad : slot * pad + patch_rows, :]
                    total = total + dot_tn(rows_in, grads)
                whole[...] = total.astype(BF16)

            return fill

        weight_grads(
            [grad_two_low, cross_attended, normed1_low, grad_cross_queries, near,
             other, grad_keys, grad_values],
            [
                (piece, product(0, 1)),
                (piece, product(2, 3)),
                (vis // groups, kv(0)),
                (vis // groups, kv(1)),
            ],
            streams["cross"],
            held,
            groups,
            inner,
            4 * tokens * width * inner + 4 * slots * pad * vis * inner,
            "cross_weight_grads",
        )
        away, _ = merge(streams["ff"] + streams["cross"], 1, held, name="merge_1")
        order.passed(away)
    grad_residual1, grad_one_low, grad_qkv, part6, norm1 = self_backward(
        order.after(grad_residual2), part5_a, part5_b, text, part1_a, part1_b, row(ln1_gain),
        wo_self, projected, self_stats, segment_ids, wq_self, wk_self, wv_self,
    )
    part6_a, part6_b = head_sum(part6)
    add_patches = (
        [patch_own, patch_other],
        [like(patch_own.shape, BF16)],
        lambda get, out: out[0].__setitem__(
            ..., (get(0)[...].astype(F32) + get(1)[...].astype(F32)).astype(BF16)
        ),
    )
    add_text = (
        [grad_residual1, part6_a, part6_b],
        [like((tokens, width), F32)],
        lambda get, out: out[0].__setitem__(
            ..., get(0)[...] + (get(1)[...].astype(F32) + get(2)[...].astype(F32))
        ),
    )
    if fast:
        def norms(get, whole):
            rows = jnp.concatenate([get(k)[...] for k in (4, 5, 6)] + [jnp.zeros((2, width), F32)])
            inside = lax.broadcasted_iota(jnp.int32, (8, inner), 1) < piece
            for group in range(groups):
                turned = pltpu.roll(rows, (width - group * piece) % width, 1)[:, :inner]
                entry = jnp.concatenate([jnp.where(inside, turned, 0.0), jnp.zeros((8, inner), F32)])
                whole[group * 16 : (group + 1) * 16, :] = entry.astype(BF16)

        weight_grads(
            [grad_one_low, attended, text, grad_qkv, norm1, norm2, norm3],
            [(piece, product(2, 3, k * inner, inner)) for k in range(3)]
            + [(piece, product(0, 1)), (16, norms)],
            streams["self"],
            held,
            groups,
            inner,
            8 * tokens * width * inner,
            "self_weight_grads",
        )
        grad_patches = None
        for phase in range(2, PHASES):
            work = {PATCH_PHASE: add_patches, PATCH_PHASE + 1: add_text}.get(phase, ((), (), None))
            if phase == PATCH_PHASE + 1:
                held[-1], grad_patches = lax.optimization_barrier((held[-1], grad_patches))
            away, more = merge(everything, phase, held, *work, name="merge_%d" % phase)
            if phase == PATCH_PHASE:
                grad_patches = partner(more[0], "stream", 0)
            elif phase == PATCH_PHASE + 1:
                grad_text = more[0]
        grad_patches = grad_patches.astype(F32)
        shares = finish(streams, held, piece, vis // groups, blocks)
        own_w_out, own_w_in, cross_wo, cross_wq, cross_wk, cross_wv = shares[:6]
        self_wq, self_wk, self_wv, self_wo = shares[6:10]
        own_w_out, cross_wo, self_wo = own_w_out.T, cross_wo.T, self_wo.T
        own_norms = [shares[10][k, :piece] for k in range(6)]
    else:
        patch_sum = (patch_own.astype(F32) + patch_other.astype(F32)).astype(BF16)
        grad_patches = partner(patch_sum, "stream", 0).astype(F32)
        grad_text = grad_residual1 + (part6_a.astype(F32) + part6_b.astype(F32))
        norm_grads = jnp.concatenate([norm1, norm2, norm3, jnp.zeros((2, width), F32)])

        def plain(left, right):
            grad = jnp.einsum("ta,tb->ab", left, right, preferred_element_type=F32)
            grad = grad.astype(BF16).reshape(groups, grad.shape[0] // groups, grad.shape[1])
            return scatter_sum_plain(grad)

        own_w_out = plain(grad_three_low, hidden).T
        own_w_in = plain(normed2_low, grad_pre)
        cross_wo = plain(grad_two_low, cross_attended).T
        cross_wq = plain(normed1_low, grad_cross_queries)
        far = jnp.stack([near, other], axis=1).reshape(slots, patch_rows, vis)
        far = jnp.pad(far, ((0, 0), (0, pad - patch_rows), (0, 0))).reshape(slots * pad, vis)
        cross_wk, cross_wv = plain(far, grad_keys), plain(far, grad_values)
        self_wq, self_wk, self_wv = jnp.split(plain(text, grad_qkv), 3, axis=1)
        self_wo = plain(grad_one_low, attended).T
        own_norms = scatter_sum_plain(
            norm_grads.reshape(8, groups, width // groups).swapaxes(0, 1).astype(BF16)
        )
    return (
        output,
        grad_text,
        grad_patches,
        self_wq,
        self_wk,
        self_wv,
        self_wo,
        own_norms[0],
        own_norms[1],
        cross_wq,
        cross_wk,
        cross_wv,
        cross_wo,
        own_norms[2],
        own_norms[3],
        own_w_in,
        own_w_out,
        own_norms[4],
        own_norms[5],
    )


def solution(mesh):
    in_specs = (
        P(("dp", "stream"), None),
        P(("dp", "stream"), None, None),
        P(("dp", "stream"), None),
        P(("dp", "stream"), None),
        P(None, "head"),
        P(None, "head"),
        P(None, "head"),
        P("head", None),
        P(),
        P(),
        P(None, "head"),
        P(None, "head"),
        P(None, "head"),
        P("head", None),
        P(),
        P(),
        P(None, "head"),
        P("head", None),
        P(),
        P(),
        P(("dp", "stream"), None),
    )
    out_specs = (
        P(("dp", "stream"), None),
        P(("dp", "stream"), None),
        P(("dp", "stream"), None, "head"),
        P(("dp", "stream"), "head"),
        P(("dp", "stream"), "head"),
        P(("dp", "stream"), "head"),
        P("head", ("dp", "stream")),
        P(("dp", "stream")),
        P(("dp", "stream")),
        P(("dp", "stream"), "head"),
        P(("dp", "stream"), "head"),
        P(("dp", "stream"), "head"),
        P("head", ("dp", "stream")),
        P(("dp", "stream")),
        P(("dp", "stream")),
        P(("dp", "stream"), "head"),
        P("head", ("dp", "stream")),
        P(("dp", "stream")),
        P(("dp", "stream")),
    )
    return jax.shard_map(body, mesh=mesh, in_specs=in_specs, out_specs=out_specs, check_vma=False)
```

```python
import jax
import jax.numpy as jnp
from jax import lax
from jax.experimental import pallas as pl
from jax.experimental.pallas import tpu as pltpu
from jax.sharding import PartitionSpec as P

HEAD_DIM = 64
LANES = 128
MAX_PHRASE = 48
EPSILON = 1e-12
NEGATIVE = -1e30
SCALE = HEAD_DIM ** (-0.5)
VMEM_LIMIT = 56 * 1024 * 1024
F32 = jnp.float32
BF16 = jnp.bfloat16


COSTS = {
    "self_forward": 2.6,
    "cross_queries": 0.8,
    "cross_keys": 1.5,
    "cross_forward": 6.2,
    "feed_forward": 3.3,
    "feed_backward": 3.3,
    "ff_weight_grads": 3.3,
    "cross_backward": 0.1,
    "cross_weight_grads": 3.3,
    "self_backward": 0.1,
    "self_weight_grads": 0.1,
    "patch_backward": 0.1,
}


def partner(value, axis, place):
    mask = 2**place
    pairs = [(source, source ^ mask) for source in range(lax.axis_size(axis))]
    return lax.ppermute(value, axis, pairs)


def group_bits():
    count = lax.axis_size("dp").bit_length() - 1
    return [("stream", 0)] + [("dp", place) for place in range(count)]


class Order:
    def __init__(self):
        self.last = None

    def after(self, value):
        if self.last is not None:
            value, _ = lax.optimization_barrier((value, self.last))
        return value

    def passed(self, value):
        self.last = value
        return value


LINKS = 4

PLAN = {
    "ff": ((48, ((0, 0), (1, 2), (2, 1), (3, 3))), (96, ((0, 0), (1, 2), (2, 3), (4, 1))), (128, ((0, 1), (1, 0), (2, 3), (4, 2))), (112, ((0, 2), (1, 3), (3, 1), (5, 0)))),
    "cross": ((48, ((1, 0), (2, 1), (3, 2), (4, 3))), (32, ((1, 0), (2, 2), (3, 3), (4, 1))), (96, ((1, 1), (2, 2), (3, 0), (4, 3))), (48, ((1, 1), (2, 0), (3, 3), (5, 2)))),
    "self": ((80, ((2, 0), (3, 1), (4, 3), (5, 2))), (32, ((2, 0), (3, 2), (4, 1), (5, 3))), (96, ((2, 1), (3, 0), (4, 2), (5, 3)))),
}
PHASES = 6
PATCH_PHASE = 4


class Stream:
    def __init__(self, rows, steps):
        self.rows, self.steps = rows, dict(steps)
        self.digits = [digit for _, digit in steps]
        self.entries = 2 ** len(steps)
        self.terms, self.send, self.sent = [], None, None


class Held(list):
    recent = ()


def gather_messages(streams, phase):
    messages = {}
    for stream in streams:
        if phase in stream.steps:
            pieces = messages.setdefault(stream.steps[phase], [])
            first = sum(rows for _, _, rows in pieces)
            pieces.append((stream, first, stream.entries // 2 * stream.rows))
    return messages


def start_messages(messages, arrays, held):
    held.recent = []
    for (digit, pieces), away in zip(sorted(messages.items()), arrays):
        axis, place = group_bits()[digit]
        held.recent.append(len(held))
        held.append(partner(away, axis, place))
        for stream, first, _ in pieces:
            stream.terms.append((len(held) - 1, first))
            stream.entries //= 2


def merge(streams, phase, held, extra_inputs=(), extra_outs=(), extra=None, name=None):
    messages = gather_messages(streams, phase)
    before = None
    for k in held.recent:
        if before is not None:
            held[k], _ = lax.optimization_barrier((held[k], held[before]))
        before = k
    if before is not None:
        for k, value in zip(
            held.recent, lax.optimization_barrier(tuple(held[k] for k in held.recent))
        ):
            held[k] = value
    used, places = [], {}

    def place(index):
        if index not in places:
            places[index] = len(used)
            used.append(held[index])
        return places[index]

    columns = held[0].shape[1]
    jobs, outs, aways = [], [], []
    for _, pieces in sorted(messages.items()):
        if len(pieces) == 1 and pieces[0][0].send is not None:
            aways.append(held[pieces[0][0].send])
            pieces[0][0].send = None
            continue
        aways.append(len(outs))
        for stream, first, rows in pieces:
            if stream.send is not None:
                sources = [(place(stream.send), 0)]
                stream.send = None
            else:
                sources = [(place(index), row + rows) for index, row in stream.terms]
            jobs.append((len(outs), first, rows, sources))
        outs.append(like((sum(rows for _, _, rows in pieces), columns), BF16))
    count = len(used)

    def body(get, out, put, scratch):
        for slot, first, rows, sources in jobs:
            parts = [get(k)[row : row + rows, :] for k, row in sources]
            if len(parts) > 1:
                total = parts[0].astype(F32)
                for part in parts[1:]:
                    total = total + part.astype(F32)
                parts = [total.astype(BF16)]
            out[slot][first : first + rows, :] = parts[0]
        if extra is not None:
            extra(lambda k: get(count + k), out[len(outs) :])

    results = []
    if outs or extra_outs:
        results = run(body, used + list(extra_inputs), outs + list(extra_outs), name=name)
    aways = [results[away] if isinstance(away, int) else away for away in aways]
    start_messages(messages, aways, held)
    return aways, results[len(outs) :]


def scatter_sum_plain(grads):
    bits = group_bits()
    count = len(bits)
    grads = grads.reshape((2,) * count + grads.shape[1:])
    for step in range(count):
        axis, place = bits[step]
        dim = count - 1 - step
        mine = (lax.axis_index(axis) >> place) & 1
        away = lax.dynamic_index_in_dim(grads, 1 - mine, dim, keepdims=True)
        keep = lax.dynamic_index_in_dim(grads, mine, dim, keepdims=True)
        grads = keep.astype(F32) + partner(away, axis, place).astype(F32)
        if step < count - 1:
            grads = grads.astype(BF16)
    return grads.reshape(grads.shape[count:])


def run(body, inputs, outs, scratch=(), flops=0, aliases=None, name=None):
    n_in, n_out = len(inputs), len(outs)

    def kernel(*refs):
        ins, refs = refs[:n_in], refs[n_in:]
        body(lambda k: ins[k], refs[:n_out], lambda k: None, refs[n_out:])

    moved = sum(a.size * a.dtype.itemsize for a in inputs) + sum(
        a.size * a.dtype.itemsize for a in outs
    )
    return pl.pallas_call(
        kernel,
        name=name,
        out_shape=[jax.ShapeDtypeStruct(a.shape, a.dtype) for a in outs],
        in_specs=[pl.BlockSpec(memory_space=pltpu.VMEM)] * n_in,
        out_specs=[pl.BlockSpec(memory_space=pltpu.VMEM)] * n_out,
        scratch_shapes=list(scratch),
        input_output_aliases=aliases or {},
        compiler_params=pltpu.CompilerParams(vmem_limit_bytes=int(moved + 8 * 2**20 + sum(2 * 384 * 384 for _ in scratch))),
        cost_estimate=pl.CostEstimate(
            flops=int(1e9 * COSTS.get(name, 0.6)), bytes_accessed=1000, transcendentals=0
        ),
    )(*inputs)


def like(shape, dtype):
    return jax.ShapeDtypeStruct(shape, dtype)


def dot(left, right):
    return lax.dot_general(left, right, (((1,), (0,)), ((), ())), preferred_element_type=F32)


def dot_nt(left, right):
    return lax.dot_general(left, right, (((1,), (1,)), ((), ())), preferred_element_type=F32)


def dot_tn(left, right):
    return lax.dot_general(left, right, (((0,), (0,)), ((), ())), preferred_element_type=F32)


def normalise(rows):
    center = rows - jnp.mean(rows, axis=-1, keepdims=True)
    inverse = lax.rsqrt(jnp.mean(center * center, axis=-1, keepdims=True) + EPSILON)
    return center * inverse, inverse


def norm_back(grad, unit, inverse, gain):
    inner = grad * gain
    shift = jnp.mean(inner, axis=-1, keepdims=True)
    slope = jnp.mean(inner * unit, axis=-1, keepdims=True)
    return inverse * (inner - shift - unit * slope)


def norm_sums(grad, unit):
    return jnp.sum(grad * unit, axis=0, keepdims=True), jnp.sum(grad, axis=0, keepdims=True)


def column(row):
    wide = jnp.broadcast_to(row.astype(F32), (LANES, row.shape[1]))
    return jnp.transpose(wide)[:, :1].astype(jnp.int32)


def half_lanes(part):
    lane = lax.broadcasted_iota(jnp.int32, (1, LANES), 1)
    return (lane >= HEAD_DIM) if part else (lane < HEAD_DIM)


def window(block, tokens, rows):
    size = min(tokens, rows + 128)
    return min(max(block * rows - 64, 0), tokens - size), size


def self_bias(seg_col, seg_row, block, rows, first, size):
    same = seg_col[block * rows : (block + 1) * rows] == seg_row[:, first : first + size]
    return jnp.where(same, 0.0, NEGATIVE)


def cross_bias(seg_col, images_row, head, slots, patch_rows, patch_pad):
    phrases = images_row.shape[1]
    phrase = lax.broadcasted_iota(jnp.int32, (1, phrases), 1)
    image = jnp.sum(jnp.where(seg_col == phrase, images_row, 0), axis=1, keepdims=True)
    place = lax.broadcasted_iota(jnp.int32, (1, slots * patch_pad), 1)
    key_image = jnp.full((1, slots * patch_pad), -1, jnp.int32)
    for slot in range(slots):
        inside = (place >= slot * patch_pad) & (place < slot * patch_pad + patch_rows)
        key_image = jnp.where(inside, slot_image(slot, slots, head), key_image)
    return jnp.where(image == key_image, 0.0, NEGATIVE)


def slot_image(slot, slots, head):
    half = slots // 2
    return half * (head if slot % 2 == 0 else 1 - head) + slot // 2


def attend(queries, keys, values, bias, parts):
    mixed, totals = 0.0, []
    for part in range(2):
        scores = dot_nt(jnp.where(parts[part], queries, 0), keys) + bias
        largest = jnp.max(scores, axis=1, keepdims=True)
        exponent = jnp.exp(scores - largest)
        total = jnp.sum(exponent, axis=1, keepdims=True)
        picked = dot(exponent.astype(BF16), values) * (1.0 / total)
        mixed = picked if part == 0 else jnp.where(parts[1], picked, mixed)
        totals.append(largest + jnp.log(total))
    return mixed, totals


def attend_back(queries, keys, values, grad, bias, totals, parts):
    both = []
    for part in range(2):
        query = jnp.where(parts[part], queries, 0)
        grad_part = jnp.where(parts[part], grad, 0)
        probs = jnp.exp(dot_nt(query, keys) + bias - totals[part])
        grad_probs = dot_nt(grad_part, values)
        inner = jnp.sum(probs * grad_probs, axis=1, keepdims=True)
        grad_scores = (probs * (grad_probs - inner)).astype(BF16)
        both.append((query, grad_part, probs.astype(BF16), grad_scores))
    query, grad_part, probs, grad_scores = [
        jnp.concatenate([both[0][k], both[1][k]], axis=0) for k in range(4)
    ]
    keys = jnp.concatenate([jnp.where(parts[part], keys, 0) for part in range(2)], axis=0)
    grad_q = dot(jnp.concatenate([both[0][3], both[1][3]], axis=1), keys)
    return grad_q * SCALE, dot_tn(grad_scores, query), dot_tn(probs, grad_part)


def self_forward(text, wq, wk, wv, wo, segments):
    tokens, width = text.shape
    inner = wq.shape[1]
    rows = 128

    def body(get, out, put, extra):
        text_in = get(0)[...]
        projected = [dot(text_in, get(1 + k)[...]).astype(BF16) for k in range(3)]
        for k in range(3):
            out[0][k] = projected[k]
        put(0)
        seg_row = get(5)[...]
        seg_col = column(seg_row)
        parts = [half_lanes(0), half_lanes(1)]
        lane = lax.broadcasted_iota(jnp.int32, (1, LANES), 1)
        for block in range(tokens // rows):
            first, size = window(block, tokens, rows)
            bias = self_bias(seg_col, seg_row, block, rows, first, size)
            here = slice(block * rows, (block + 1) * rows)
            stats = jnp.zeros((rows, LANES), F32)
            for pair in range(inner // LANES):
                cols = slice(pair * LANES, (pair + 1) * LANES)
                mixed, totals = attend(
                    out[0][0, here, cols] * SCALE,
                    out[0][1, first : first + size, cols],
                    out[0][2, first : first + size, cols],
                    bias,
                    parts,
                )
                out[1][here, cols] = mixed.astype(BF16)
                for part in range(2):
                    stats = jnp.where(lane == 2 * pair + part, totals[part], stats)
            out[2][here, :] = stats
        put(1)
        put(2)
        out[3][...] = dot(out[1][...], get(4)[...]).astype(BF16)
        put(3)

    return run(
        body,
        [text, wq, wk, wv, wo, segments],
        [
            like((3, tokens, inner), BF16),
            like((tokens, inner), BF16),
            like((tokens, LANES), F32),
            like((tokens, width), BF16),
        ],
        flops=2 * tokens * width * inner * 4 + 8 * tokens * 256 * inner,
        name="self_forward",
    )


def cross_keys(near, other, wk, wv):
    half, patch_rows, vis = near.shape
    slots = 2 * half
    pad = -(-patch_rows // 16) * 16
    inner = wk.shape[1]

    def body(get, out, put, extra):
        weights = [get(2), get(3)]
        for k in range(2):
            for slot in range(slots):
                top, end = slot * pad, (slot + 1) * pad
                out[k][end - 16 : end, :] = jnp.zeros((16, inner), BF16)
                out[k][top : top + patch_rows, :] = dot(
                    get(slot % 2)[slot // 2], weights[k][...]
                ).astype(BF16)

    return run(
        body,
        [near, other, wk, wv],
        [like((slots * pad, inner), BF16)] * 2,
        flops=4 * slots * pad * vis * inner,
        name="cross_keys",
    )


def cross_queries_of(text, part_a, part_b, gain, bias, wq):
    tokens, width = text.shape

    def body(get, out, put, extra):
        residual = get(0)[...].astype(F32) + (get(1)[...].astype(F32) + get(2)[...].astype(F32))
        unit, _ = normalise(residual)
        normed = unit * get(3)[...] + get(4)[...]
        out[0][...] = normed
        low = normed.astype(BF16)
        out[1][...] = low
        out[2][...] = dot(low, get(5)[...]).astype(BF16)

    return run(
        body,
        [text, part_a, part_b, gain, bias, wq],
        [
            like((tokens, width), F32),
            like((tokens, width), BF16),
            like((tokens, wq.shape[1]), BF16),
        ],
        flops=2 * tokens * width * wq.shape[1],
        name="cross_queries",
    )


def cross_forward(queries, keys, values, wo, segments, images, dims):
    tokens, inner = queries.shape
    width = wo.shape[1]
    slots, patch_rows, pad = dims
    rows = tokens

    def body(get, out, put, extra):
        head = lax.axis_index("head")
        mask = cross_bias(column(get(4)[...]), get(5)[...], head, slots, patch_rows, pad)
        parts = [half_lanes(0), half_lanes(1)]
        lane = lax.broadcasted_iota(jnp.int32, (1, LANES), 1)
        for block in range(tokens // rows):
            here = slice(block * rows, (block + 1) * rows)
            stats = jnp.zeros((rows, LANES), F32)
            for pair in range(inner // LANES):
                cols = slice(pair * LANES, (pair + 1) * LANES)
                mixed, totals = attend(
                    get(0)[here, cols] * SCALE,
                    get(1)[:, cols],
                    get(2)[:, cols],
                    mask[here],
                    parts,
                )
                out[0][here, cols] = mixed.astype(BF16)
                for part in range(2):
                    stats = jnp.where(lane == 2 * pair + part, totals[part], stats)
            out[1][here, :] = stats
        out[2][...] = dot(out[0][...], get(3)[...]).astype(BF16)

    return run(
        body,
        [queries, keys, values, wo, segments, images],
        [
            like((tokens, inner), BF16),
            like((tokens, LANES), F32),
            like((tokens, width), BF16),
        ],
        flops=2 * tokens * width * inner + 4 * tokens * slots * pad * inner,
        name="cross_forward",
    )


def feed_forward(normed, part_a, part_b, gain, bias, w_in, w_out):
    tokens, width = normed.shape
    inner = w_in.shape[1]
    chunk = 256

    def body(get, out, put, extra):
        residual = get(0)[...] + (get(1)[...].astype(F32) + get(2)[...].astype(F32))
        unit, _ = normalise(residual)
        normed_two = unit * get(3)[...] + get(4)[...]
        out[0][...] = normed_two
        put(0)
        out[1][...] = normed_two.astype(BF16)
        put(1)
        get(5)
        for start in range(0, inner, chunk):
            cols = slice(start, start + chunk)
            pre = dot(out[1][...], get(5)[:, cols])
            phi = 0.5 * (1.0 + lax.erf(pre * (0.5**0.5)))
            bell = jnp.exp(pre * pre * -0.5) * 0.3989422804014327
            out[2][:, cols] = (pre * phi).astype(BF16)
            out[3][:, cols] = (phi + pre * bell).astype(BF16)
        put(2)
        put(3)
        out[4][...] = dot(out[2][...], get(6)[...]).astype(BF16)
        put(4)

    return run(
        body,
        [normed, part_a, part_b, gain, bias, w_in, w_out],
        [
            like((tokens, width), F32),
            like((tokens, width), BF16),
            like((tokens, inner), BF16),
            like((tokens, inner), BF16),
            like((tokens, width), BF16),
        ],
        flops=4 * tokens * width * inner,
        name="feed_forward",
    )


def feed_backward(normed, part_a, part_b, gain, bias, cotangent, w_out, slopes, w_in):
    tokens, width = normed.shape
    inner = w_in.shape[1]
    chunk = 256

    def body(get, out, put, extra):
        residual = get(0)[...] + (get(1)[...].astype(F32) + get(2)[...].astype(F32))
        unit, inverse = normalise(residual)
        gain_row = get(3)[...]
        out[0][...] = unit * gain_row + get(4)[...]
        put(0)
        grad = get(5)[...]
        out[5][0:1, :], out[5][1:2, :] = norm_sums(grad, unit)
        put(5)
        grad_residual = norm_back(grad, unit, inverse, gain_row)
        out[1][...] = grad_residual
        put(1)
        out[2][...] = grad_residual.astype(BF16)
        put(2)
        get(6)
        get(7)
        for start in range(0, inner, chunk):
            cols = slice(start, start + chunk)
            grad_hidden = dot_nt(out[2][...], get(6)[cols, :])
            out[3][:, cols] = (grad_hidden * get(7)[:, cols].astype(F32)).astype(BF16)
        put(3)
        out[4][...] = dot_nt(out[3][...], get(8)[...]).astype(BF16)
        put(4)

    return run(
        body,
        [normed, part_a, part_b, gain, bias, cotangent, w_out, slopes, w_in],
        [
            like((tokens, width), F32),
            like((tokens, width), F32),
            like((tokens, width), BF16),
            like((tokens, inner), BF16),
            like((tokens, width), BF16),
            like((2, width), F32),
        ],
        flops=4 * tokens * width * inner,
        name="feed_backward",
    )


def cross_backward(
    grad_in, part_a, part_b, normed, fwd_a, fwd_b, gain, wo, queries, keys, values, stats,
    segments, images, wq, dims,
):
    tokens, width = grad_in.shape
    inner = queries.shape[1]
    slots, patch_rows, pad = dims
    rows = tokens

    def body(get, out, put, extra):
        residual = get(3)[...] + (get(4)[...].astype(F32) + get(5)[...].astype(F32))
        unit, inverse = normalise(residual)
        grad = get(0)[...] + (get(1)[...].astype(F32) + get(2)[...].astype(F32))
        out[6][0:1, :], out[6][1:2, :] = norm_sums(grad, unit)
        put(6)
        grad_residual = norm_back(grad, unit, inverse, get(6)[...])
        out[0][...] = grad_residual
        put(0)
        out[1][...] = grad_residual.astype(BF16)
        put(1)
        grad_mixed = extra[0]
        grad_mixed[...] = dot_nt(out[1][...], get(7)[...]).astype(BF16)
        head = lax.axis_index("head")
        mask = cross_bias(column(get(12)[...]), get(13)[...], head, slots, patch_rows, pad)
        parts = [half_lanes(0), half_lanes(1)]
        for k in range(8, 12):
            get(k)
        for pair in range(inner // LANES):
            cols = slice(pair * LANES, (pair + 1) * LANES)
            grad_k, grad_v = 0.0, 0.0
            for block in range(tokens // rows):
                here = slice(block * rows, (block + 1) * rows)
                totals = [get(11)[here, 2 * pair + part : 2 * pair + part + 1] for part in range(2)]
                grad_q, more_k, more_v = attend_back(
                    get(8)[here, cols] * SCALE,
                    get(9)[:, cols],
                    get(10)[:, cols],
                    grad_mixed[here, cols],
                    mask[here],
                    totals,
                    parts,
                )
                out[2][here, cols] = grad_q.astype(BF16)
                grad_k, grad_v = grad_k + more_k, grad_v + more_v
            out[3][:, cols] = grad_k.astype(BF16)
            out[4][:, cols] = grad_v.astype(BF16)
        put(2)
        put(3)
        put(4)
        out[5][...] = dot_nt(out[2][...], get(14)[...]).astype(BF16)
        put(5)

    return run(
        body,
        [
            grad_in, part_a, part_b, normed, fwd_a, fwd_b, gain, wo, queries, keys, values, stats,
            segments, images, wq,
        ],
        [
            like((tokens, width), F32),
            like((tokens, width), BF16),
            like((tokens, inner), BF16),
            like((slots * pad, inner), BF16),
            like((slots * pad, inner), BF16),
            like((tokens, width), BF16),
            like((2, width), F32),
        ],
        scratch=[pltpu.VMEM((tokens, inner), BF16)],
        flops=4 * tokens * width * inner + 10 * tokens * slots * pad * inner,
        name="cross_backward",
    )


def self_backward(
    grad_in, part_a, part_b, text, fwd_a, fwd_b, gain, wo, projected, stats, segments, wq, wk, wv
):
    tokens, width = grad_in.shape
    inner = wq.shape[1]
    rows = tokens

    def body(get, out, put, extra):
        residual = get(3)[...].astype(F32) + (get(4)[...].astype(F32) + get(5)[...].astype(F32))
        unit, inverse = normalise(residual)
        grad = get(0)[...] + (get(1)[...].astype(F32) + get(2)[...].astype(F32))
        out[4][0:1, :], out[4][1:2, :] = norm_sums(grad, unit)
        put(4)
        grad_residual = norm_back(grad, unit, inverse, get(6)[...])
        out[0][...] = grad_residual
        put(0)
        out[1][...] = grad_residual.astype(BF16)
        put(1)
        grad_mixed, grad_keys, grad_values = extra
        grad_mixed[...] = dot_nt(out[1][...], get(7)[...]).astype(BF16)
        grad_keys[...] = jnp.zeros_like(grad_keys)
        grad_values[...] = jnp.zeros_like(grad_values)
        seg_row = get(10)[...]
        seg_col = column(seg_row)
        parts = [half_lanes(0), half_lanes(1)]
        get(8)
        get(9)
        for block in range(tokens // rows):
            first, size = window(block, tokens, rows)
            bias = self_bias(seg_col, seg_row, block, rows, first, size)
            here = slice(block * rows, (block + 1) * rows)
            there = slice(first, first + size)
            for pair in range(inner // LANES):
                cols = slice(pair * LANES, (pair + 1) * LANES)
                totals = [get(9)[here, 2 * pair + part : 2 * pair + part + 1] for part in range(2)]
                grad_q, grad_k, grad_v = attend_back(
                    get(8)[0, here, cols] * SCALE,
                    get(8)[1, there, cols],
                    get(8)[2, there, cols],
                    grad_mixed[here, cols],
                    bias,
                    totals,
                    parts,
                )
                out[2][here, cols] = grad_q.astype(BF16)
                grad_keys[there, cols] += grad_k
                grad_values[there, cols] += grad_v
        out[2][:, inner : 2 * inner] = grad_keys[...].astype(BF16)
        out[2][:, 2 * inner :] = grad_values[...].astype(BF16)
        put(2)
        total = 0.0
        for k in range(3):
            total = total + dot_nt(out[2][:, k * inner : (k + 1) * inner], get(11 + k)[...])
        out[3][...] = total.astype(BF16)
        put(3)

    return run(
        body,
        [
            grad_in, part_a, part_b, text, fwd_a, fwd_b, gain, wo, projected, stats, segments,
            wq, wk, wv,
        ],
        [
            like((tokens, width), F32),
            like((tokens, width), BF16),
            like((tokens, 3 * inner), BF16),
            like((tokens, width), BF16),
            like((2, width), F32),
        ],
        scratch=[
            pltpu.VMEM((tokens, inner), BF16),
            pltpu.VMEM((tokens, inner), F32),
            pltpu.VMEM((tokens, inner), F32),
        ],
        flops=8 * tokens * width * inner + 10 * tokens * 256 * inner,
        name="self_backward",
    )


def patch_backward(grad_keys, grad_values, wk, wv, dims):
    slots, patch_rows, pad = dims
    vis, inner = wk.shape
    width = vis // 2

    def body(get, out, put, extra):
        head = lax.axis_index("head")
        weights = [get(2), get(3)]
        grads = [get(0), get(1)]
        for k in range(2):
            first = pl.multiple_of((head if k == 0 else 1 - head) * width, width)
            left, right = (weights[j][pl.ds(first, width), :] for j in range(2))
            for slot in range(slots):
                rows = slice(slot * pad, (slot + 1) * pad)
                total = dot_nt(grads[0][rows, :], left) + dot_nt(grads[1][rows, :], right)
                out[k][slot_image(slot, slots, head)] = total[:patch_rows].astype(BF16)
            put(k)

    return run(
        body,
        [grad_keys, grad_values, wk, wv],
        [like((slots, patch_rows, width), BF16)] * 2,
        flops=4 * slots * pad * vis * inner,
        name="patch_backward",
    )


def offset_of(position, digits):
    count = len(digits)
    return sum(
        ((position >> (count - 1 - step)) & 1) << digit for step, digit in enumerate(digits)
    )


def weight_grads(inputs, blocks, streams, held, groups, columns, flops, name):
    outs = []
    for stream in streams:
        outs += [like((stream.entries // 2 * stream.rows, columns), BF16)] * 2

    def body(get, out, put, scratch):
        me = lax.axis_index("dp") * lax.axis_size("stream") + lax.axis_index("stream")
        first = 0
        for block, (piece, product) in enumerate(blocks):
            whole = scratch[block]
            product(get, whole)
            bottom = 0
            for k, stream in enumerate(streams):
                low = max(first, bottom)
                high = min(first + piece, bottom + stream.rows)
                for position in range(stream.entries if low < high else 0):
                    side, entry = divmod(position, stream.entries // 2)
                    source = (me ^ offset_of(position, stream.digits)) * piece + (low - first)
                    target = entry * stream.rows + low - bottom
                    out[2 * k + side][target : target + high - low, :] = whole[
                        pl.ds(pl.multiple_of(source, 16), high - low), :
                    ]
                bottom += stream.rows
            first += piece

    results = run(
        body,
        inputs,
        outs,
        scratch=[pltpu.VMEM((groups * piece, columns), BF16) for piece, _ in blocks],
        flops=flops,
        name=name,
    )
    for k, stream in enumerate(streams):
        held += [results[2 * k], results[2 * k + 1]]
        stream.terms, stream.send = [(len(held) - 2, 0)], len(held) - 1


def product(left, right, first=None, size=None):
    def fill(get, whole):
        columns = get(right)[...] if first is None else get(right)[:, first : first + size]
        whole[...] = dot_tn(get(left)[...], columns).astype(BF16)

    return fill


def finish(streams, held, piece, vis_piece, blocks):
    columns = held[0].shape[1]
    used, places = [], {}
    for batch in streams.values():
        for stream in batch:
            for index, _ in stream.terms:
                if index not in places:
                    places[index] = len(used)
                    used.append(held[index])

    def body(get, out, put, scratch):
        def rows_of(batch, low, high):
            parts, bottom = [], 0
            for stream in batch:
                first, last = max(low, bottom) - bottom, min(high, bottom + stream.rows) - bottom
                if first < last:
                    total = 0.0
                    for index, row in stream.terms:
                        total = total + get(places[index])[row + first : row + last, :].astype(F32)
                    parts.append(total)
                bottom += stream.rows
            return parts[0] if len(parts) == 1 else jnp.concatenate(parts)

        for k in range(2 * blocks):
            out[k // blocks][:, k % blocks * columns : (k % blocks + 1) * columns] = rows_of(
                streams["ff"], k * piece, (k + 1) * piece
            )
        for k in range(2):
            out[2 + k][...] = rows_of(streams["cross"], k * piece, (k + 1) * piece)
            low = 2 * piece + k * vis_piece
            out[4 + k][...] = rows_of(streams["cross"], low, low + vis_piece)
        for k in range(4):
            out[6 + k][...] = rows_of(streams["self"], k * piece, (k + 1) * piece)
        out[10][...] = rows_of(streams["self"], 4 * piece, 4 * piece + 16)

    return run(
        body,
        used,
        [like((piece, blocks * columns), F32)] * 2
        + [like((piece, columns), F32)] * 2
        + [like((vis_piece, columns), F32)] * 2
        + [like((piece, columns), F32)] * 4
        + [like((16, columns), F32)],
        name="finish",
    )


def project(left, right):
    return jnp.dot(left, right, preferred_element_type=F32)


def head_sum(partial_rows):
    return partial_rows, partner(partial_rows, "head", 0)


def body(
    text,
    patches,
    segment_ids,
    phrase_image,
    wq_self,
    wk_self,
    wv_self,
    wo_self,
    ln1_gain,
    ln1_bias,
    wq_cross,
    wk_cross,
    wv_cross,
    wo_cross,
    ln2_gain,
    ln2_bias,
    w_in,
    w_out,
    ln3_gain,
    ln3_bias,
    cotangent,
):
    slots, patch_rows, vis = patches.shape
    half = slots // 2
    pad = -(-patch_rows // 16) * 16
    dims = (slots, patch_rows, pad)
    tokens, width = text.shape
    inner = wq_self.shape[1]
    hidden_width = w_in.shape[1]
    groups = lax.axis_size("dp") * lax.axis_size("stream")
    head = lax.axis_index("head")
    row = lambda vector: vector.reshape(1, width)

    near = partner(lax.dynamic_slice_in_dim(patches, head * half, half, 0), "stream", 0)
    projected, attended, self_stats, part1 = self_forward(
        text, wq_self, wk_self, wv_self, wo_self, segment_ids
    )
    attended, near = lax.optimization_barrier((attended, near))
    other = partner(near, "head", 0)
    part1_a, part1_b = head_sum(part1)
    normed1, normed1_low, cross_queries = cross_queries_of(
        text, part1_a, part1_b, row(ln1_gain), row(ln1_bias), wq_cross
    )
    keys_cross, values_cross = cross_keys(near, other, wk_cross, wv_cross)
    cross_attended, cross_stats, part2 = cross_forward(
        cross_queries, keys_cross, values_cross, wo_cross, segment_ids, phrase_image, dims
    )
    part2_a, part2_b = head_sum(part2)
    normed2, normed2_low, hidden, slopes, part3 = feed_forward(
        normed1, part2_a, part2_b, row(ln2_gain), row(ln2_bias), w_in, w_out
    )
    part3_a, part3_b = head_sum(part3)
    output, grad_residual3, grad_three_low, grad_pre, part4, norm3 = feed_backward(
        normed2, part3_a, part3_b, row(ln3_gain), row(ln3_bias), cotangent, w_out, slopes, w_in
    )
    part4_a, part4_b = head_sum(part4)
    piece = width // groups
    fast = groups == 2**LINKS and piece % 16 == 0 and vis % (16 * groups) == 0
    order = Order()
    held, streams = Held(), {}
    if fast:
        streams = {name: [Stream(*stream) for stream in plan] for name, plan in PLAN.items()}
        everything = [stream for batch in streams.values() for stream in batch]
        blocks = hidden_width // inner
        weight_grads(
            [grad_three_low, hidden, normed2_low, grad_pre],
            [(piece, product(0, 1, k * inner, inner)) for k in range(blocks)]
            + [(piece, product(2, 3, k * inner, inner)) for k in range(blocks)],
            streams["ff"],
            held,
            groups,
            inner,
            4 * tokens * width * hidden_width,
            "ff_weight_grads",
        )
        away, _ = merge(streams["ff"], 0, held, name="merge_0")
        order.passed(away)
    grad_residual2, grad_two_low, grad_cross_queries, grad_keys, grad_values, part5, norm2 = (
        cross_backward(
            order.after(grad_residual3), part4_a, part4_b, normed1, part2_a, part2_b,
            row(ln2_gain), wo_cross, cross_queries, keys_cross, values_cross, cross_stats,
            segment_ids, phrase_image, wq_cross, dims,
        )
    )
    part5_a, part5_b = head_sum(part5)
    if fast:
        def kv(which):
            def fill(get, whole):
                total = 0.0
                for slot in range(slots):
                    rows_in = get(4 + slot % 2)[slot // 2]
                    grads = get(6 + which)[slot * pad : slot * pad + patch_rows, :]
                    total = total + dot_tn(rows_in, grads)
                whole[...] = total.astype(BF16)

            return fill

        weight_grads(
            [grad_two_low, cross_attended, normed1_low, grad_cross_queries, near,
             other, grad_keys, grad_values],
            [
                (piece, product(0, 1)),
                (piece, product(2, 3)),
                (vis // groups, kv(0)),
                (vis // groups, kv(1)),
            ],
            streams["cross"],
            held,
            groups,
            inner,
            4 * tokens * width * inner + 4 * slots * pad * vis * inner,
            "cross_weight_grads",
        )
        away, _ = merge(streams["ff"] + streams["cross"], 1, held, name="merge_1")
        order.passed(away)
    grad_residual1, grad_one_low, grad_qkv, part6, norm1 = self_backward(
        order.after(grad_residual2), part5_a, part5_b, text, part1_a, part1_b, row(ln1_gain),
        wo_self, projected, self_stats, segment_ids, wq_self, wk_self, wv_self,
    )
    part6_a, part6_b = head_sum(part6)
    grad_keys, _ = lax.optimization_barrier((grad_keys, grad_qkv))
    patch_own, patch_away = patch_backward(grad_keys, grad_values, wk_cross, wv_cross, dims)
    patch_other = partner(patch_away, "head", 0)
    add_patches = (
        [patch_own, patch_other],
        [like(patch_own.shape, BF16)],
        lambda get, out: out[0].__setitem__(
            ..., (get(0)[...].astype(F32) + get(1)[...].astype(F32)).astype(BF16)
        ),
    )
    grad_text = grad_residual1 + (part6_a.astype(F32) + part6_b.astype(F32))
    if fast:
        def norms(get, whole):
            rows = jnp.concatenate([get(k)[...] for k in (4, 5, 6)] + [jnp.zeros((2, width), F32)])
            inside = lax.broadcasted_iota(jnp.int32, (8, inner), 1) < piece
            for group in range(groups):
                turned = pltpu.roll(rows, (width - group * piece) % width, 1)[:, :inner]
                entry = jnp.concatenate([jnp.where(inside, turned, 0.0), jnp.zeros((8, inner), F32)])
                whole[group * 16 : (group + 1) * 16, :] = entry.astype(BF16)

        weight_grads(
            [grad_one_low, attended, text, grad_qkv, norm1, norm2, norm3],
            [(piece, product(2, 3, k * inner, inner)) for k in range(3)]
            + [(piece, product(0, 1)), (16, norms)],
            streams["self"],
            held,
            groups,
            inner,
            8 * tokens * width * inner,
            "self_weight_grads",
        )
        grad_patches = None
        early = held.recent[0]
        held[early], patch_own, _ = lax.optimization_barrier((held[early], patch_own, held[-1]))
        for phase in range(2, PHASES):
            work = add_patches if phase == PATCH_PHASE else ((), (), None)
            if phase == PATCH_PHASE + 1:
                held[-1], grad_patches = lax.optimization_barrier((held[-1], grad_patches))
            away, more = merge(everything, phase, held, *work, name="merge_%d" % phase)
            if phase == PATCH_PHASE:
                grad_patches = partner(more[0], "stream", 0)
        grad_patches = grad_patches.astype(F32)
        shares = finish(streams, held, piece, vis // groups, blocks)
        own_w_out, own_w_in, cross_wo, cross_wq, cross_wk, cross_wv = shares[:6]
        self_wq, self_wk, self_wv, self_wo = shares[6:10]
        own_w_out, cross_wo, self_wo = own_w_out.T, cross_wo.T, self_wo.T
        own_norms = [shares[10][k, :piece] for k in range(6)]
    else:
        patch_sum = (patch_own.astype(F32) + patch_other.astype(F32)).astype(BF16)
        grad_patches = partner(patch_sum, "stream", 0).astype(F32)
        norm_grads = jnp.concatenate([norm1, norm2, norm3, jnp.zeros((2, width), F32)])

        def plain(left, right):
            grad = jnp.einsum("ta,tb->ab", left, right, preferred_element_type=F32)
            grad = grad.astype(BF16).reshape(groups, grad.shape[0] // groups, grad.shape[1])
            return scatter_sum_plain(grad)

        own_w_out = plain(grad_three_low, hidden).T
        own_w_in = plain(normed2_low, grad_pre)
        cross_wo = plain(grad_two_low, cross_attended).T
        cross_wq = plain(normed1_low, grad_cross_queries)
        far = jnp.stack([near, other], axis=1).reshape(slots, patch_rows, vis)
        far = jnp.pad(far, ((0, 0), (0, pad - patch_rows), (0, 0))).reshape(slots * pad, vis)
        cross_wk, cross_wv = plain(far, grad_keys), plain(far, grad_values)
        self_wq, self_wk, self_wv = jnp.split(plain(text, grad_qkv), 3, axis=1)
        self_wo = plain(grad_one_low, attended).T
        own_norms = scatter_sum_plain(
            norm_grads.reshape(8, groups, width // groups).swapaxes(0, 1).astype(BF16)
        )
    return (
        output,
        grad_text,
        grad_patches,
        self_wq,
        self_wk,
        self_wv,
        self_wo,
        own_norms[0],
        own_norms[1],
        cross_wq,
        cross_wk,
        cross_wv,
        cross_wo,
        own_norms[2],
        own_norms[3],
        own_w_in,
        own_w_out,
        own_norms[4],
        own_norms[5],
    )


def solution(mesh):
    in_specs = (
        P(("dp", "stream"), None),
        P(("dp", "stream"), None, None),
        P(("dp", "stream"), None),
        P(("dp", "stream"), None),
        P(None, "head"),
        P(None, "head"),
        P(None, "head"),
        P("head", None),
        P(),
        P(),
        P(None, "head"),
        P(None, "head"),
        P(None, "head"),
        P("head", None),
        P(),
        P(),
        P(None, "head"),
        P("head", None),
        P(),
        P(),
        P(("dp", "stream"), None),
    )
    out_specs = (
        P(("dp", "stream"), None),
        P(("dp", "stream"), None),
        P(("dp", "stream"), None, "head"),
        P(("dp", "stream"), "head"),
        P(("dp", "stream"), "head"),
        P(("dp", "stream"), "head"),
        P("head", ("dp", "stream")),
        P(("dp", "stream")),
        P(("dp", "stream")),
        P(("dp", "stream"), "head"),
        P(("dp", "stream"), "head"),
        P(("dp", "stream"), "head"),
        P("head", ("dp", "stream")),
        P(("dp", "stream")),
        P(("dp", "stream")),
        P(("dp", "stream"), "head"),
        P("head", ("dp", "stream")),
        P(("dp", "stream")),
        P(("dp", "stream")),
    )
    return jax.shard_map(body, mesh=mesh, in_specs=in_specs, out_specs=out_specs, check_vma=False)
```

```python
import jax
import jax.numpy as jnp
from jax import lax
from jax.experimental import pallas as pl
from jax.experimental.pallas import tpu as pltpu
from jax.sharding import PartitionSpec as P

HEAD_DIM = 64
LANES = 128
MAX_PHRASE = 48
EPSILON = 1e-12
NEGATIVE = -1e30
SCALE = HEAD_DIM ** (-0.5)
VMEM_LIMIT = 56 * 1024 * 1024
F32 = jnp.float32
BF16 = jnp.bfloat16


COSTS = {
    "self_forward": 0.8,
    "cross_queries": 0.1,
    "cross_keys": 0.3,
    "cross_forward": 6.2,
    "feed_forward": 3.3,
    "feed_backward": 3.3,
    "ff_weight_grads": 1.1,
    "cross_backward": 0.1,
    "cross_weight_grads": 3.3,
    "self_backward": 0.1,
    "self_weight_grads": 0.1,
    "patch_backward": 0.1,
}


def partner(value, axis, place):
    mask = 2**place
    pairs = [(source, source ^ mask) for source in range(lax.axis_size(axis))]
    return lax.ppermute(value, axis, pairs)


def group_bits():
    count = lax.axis_size("dp").bit_length() - 1
    return [("stream", 0)] + [("dp", place) for place in range(count)]


class Order:
    def __init__(self):
        self.last = None

    def after(self, value):
        if self.last is not None:
            value, _ = lax.optimization_barrier((value, self.last))
        return value

    def passed(self, value):
        self.last = value
        return value


LINKS = 4

PLAN = {
    "ff": ((48, ((0, 0), (1, 2), (2, 1), (3, 3))), (96, ((0, 0), (1, 2), (2, 3), (4, 1))), (128, ((0, 1), (1, 0), (2, 3), (4, 2))), (112, ((0, 2), (1, 3), (3, 1), (5, 0)))),
    "cross": ((48, ((1, 0), (2, 1), (3, 2), (4, 3))), (32, ((1, 0), (2, 2), (3, 3), (4, 1))), (96, ((1, 1), (2, 2), (3, 0), (4, 3))), (48, ((1, 1), (2, 0), (3, 3), (5, 2)))),
    "self": ((80, ((2, 0), (3, 1), (4, 3), (5, 2))), (32, ((2, 0), (3, 2), (4, 1), (5, 3))), (96, ((2, 1), (3, 0), (4, 2), (5, 3)))),
}
PHASES = 6
PATCH_PHASE = 4


class Stream:
    def __init__(self, rows, steps):
        self.rows, self.steps = rows, dict(steps)
        self.digits = [digit for _, digit in steps]
        self.entries = 2 ** len(steps)
        self.terms, self.send, self.sent = [], None, None


class Held(list):
    recent = ()
    phase = None


def gather_messages(streams, phase):
    messages = {}
    for stream in streams:
        if phase in stream.steps:
            pieces = messages.setdefault(stream.steps[phase], [])
            first = sum(rows for _, _, rows in pieces)
            pieces.append((stream, first, stream.entries // 2 * stream.rows))
    return messages


def start_messages(messages, arrays, held, phase):
    if held.phase != phase:
        held.phase, held.recent = phase, []
    for (digit, pieces), away in zip(sorted(messages.items()), arrays):
        axis, place = group_bits()[digit]
        held.recent.append(len(held))
        held.append(partner(away, axis, place))
        for stream, first, _ in pieces:
            stream.terms.append((len(held) - 1, first))
            stream.entries //= 2


def merge(streams, phase, held, extra_inputs=(), extra_outs=(), extra=None, name=None):
    messages = gather_messages(streams, phase)
    before = None
    for k in held.recent if held.phase != phase else ():
        if before is not None:
            held[k], _ = lax.optimization_barrier((held[k], held[before]))
        before = k
    if before is not None:
        for k, value in zip(
            held.recent, lax.optimization_barrier(tuple(held[k] for k in held.recent))
        ):
            held[k] = value
    used, places = [], {}

    def place(index):
        if index not in places:
            places[index] = len(used)
            used.append(held[index])
        return places[index]

    columns = held[0].shape[1]
    jobs, outs, aways = [], [], []
    for _, pieces in sorted(messages.items()):
        if len(pieces) == 1 and pieces[0][0].send is not None:
            aways.append(held[pieces[0][0].send])
            pieces[0][0].send = None
            continue
        aways.append(len(outs))
        for stream, first, rows in pieces:
            if stream.send is not None:
                sources = [(place(stream.send), 0)]
                stream.send = None
            else:
                sources = [(place(index), row + rows) for index, row in stream.terms]
            jobs.append((len(outs), first, rows, sources))
        outs.append(like((sum(rows for _, _, rows in pieces), columns), BF16))
    count = len(used)

    def body(get, out, put, scratch):
        for slot, first, rows, sources in jobs:
            parts = [get(k)[row : row + rows, :] for k, row in sources]
            if len(parts) > 1:
                total = parts[0].astype(F32)
                for part in parts[1:]:
                    total = total + part.astype(F32)
                parts = [total.astype(BF16)]
            out[slot][first : first + rows, :] = parts[0]
        if extra is not None:
            extra(lambda k: get(count + k), out[len(outs) :])

    results = []
    if outs or extra_outs:
        results = run(body, used + list(extra_inputs), outs + list(extra_outs), name=name)
    aways = [results[away] if isinstance(away, int) else away for away in aways]
    start_messages(messages, aways, held, phase)
    return aways, results[len(outs) :]


def scatter_sum_plain(grads):
    bits = group_bits()
    count = len(bits)
    grads = grads.reshape((2,) * count + grads.shape[1:])
    for step in range(count):
        axis, place = bits[step]
        dim = count - 1 - step
        mine = (lax.axis_index(axis) >> place) & 1
        away = lax.dynamic_index_in_dim(grads, 1 - mine, dim, keepdims=True)
        keep = lax.dynamic_index_in_dim(grads, mine, dim, keepdims=True)
        grads = keep.astype(F32) + partner(away, axis, place).astype(F32)
        if step < count - 1:
            grads = grads.astype(BF16)
    return grads.reshape(grads.shape[count:])


def run(body, inputs, outs, scratch=(), flops=0, aliases=None, name=None):
    n_in, n_out = len(inputs), len(outs)

    def kernel(*refs):
        ins, refs = refs[:n_in], refs[n_in:]
        body(lambda k: ins[k], refs[:n_out], lambda k: None, refs[n_out:])

    moved = sum(a.size * a.dtype.itemsize for a in inputs) + sum(
        a.size * a.dtype.itemsize for a in outs
    )
    return pl.pallas_call(
        kernel,
        name=name,
        out_shape=[jax.ShapeDtypeStruct(a.shape, a.dtype) for a in outs],
        in_specs=[pl.BlockSpec(memory_space=pltpu.VMEM)] * n_in,
        out_specs=[pl.BlockSpec(memory_space=pltpu.VMEM)] * n_out,
        scratch_shapes=list(scratch),
        input_output_aliases=aliases or {},
        compiler_params=pltpu.CompilerParams(vmem_limit_bytes=int(moved + 8 * 2**20 + sum(2 * 384 * 384 for _ in scratch))),
        cost_estimate=pl.CostEstimate(
            flops=int(1e9 * COSTS.get(name, 0.6)), bytes_accessed=1000, transcendentals=0
        ),
    )(*inputs)


def like(shape, dtype):
    return jax.ShapeDtypeStruct(shape, dtype)


def dot(left, right):
    return lax.dot_general(left, right, (((1,), (0,)), ((), ())), preferred_element_type=F32)


def dot_nt(left, right):
    return lax.dot_general(left, right, (((1,), (1,)), ((), ())), preferred_element_type=F32)


def dot_tn(left, right):
    return lax.dot_general(left, right, (((0,), (0,)), ((), ())), preferred_element_type=F32)


def normalise(rows):
    center = rows - jnp.mean(rows, axis=-1, keepdims=True)
    inverse = lax.rsqrt(jnp.mean(center * center, axis=-1, keepdims=True) + EPSILON)
    return center * inverse, inverse


def norm_back(grad, unit, inverse, gain):
    inner = grad * gain
    shift = jnp.mean(inner, axis=-1, keepdims=True)
    slope = jnp.mean(inner * unit, axis=-1, keepdims=True)
    return inverse * (inner - shift - unit * slope)


def norm_sums(grad, unit):
    return jnp.sum(grad * unit, axis=0, keepdims=True), jnp.sum(grad, axis=0, keepdims=True)


def column(row):
    wide = jnp.broadcast_to(row.astype(F32), (LANES, row.shape[1]))
    return jnp.transpose(wide)[:, :1].astype(jnp.int32)


def half_lanes(part):
    lane = lax.broadcasted_iota(jnp.int32, (1, LANES), 1)
    return (lane >= HEAD_DIM) if part else (lane < HEAD_DIM)


def window(block, tokens, rows):
    size = min(tokens, rows + 128)
    return min(max(block * rows - 64, 0), tokens - size), size


def self_bias(seg_col, seg_row, block, rows, first, size):
    same = seg_col[block * rows : (block + 1) * rows] == seg_row[:, first : first + size]
    return jnp.where(same, 0.0, NEGATIVE)


def cross_bias(seg_col, images_row, head, slots, patch_rows, patch_pad):
    phrases = images_row.shape[1]
    phrase = lax.broadcasted_iota(jnp.int32, (1, phrases), 1)
    image = jnp.sum(jnp.where(seg_col == phrase, images_row, 0), axis=1, keepdims=True)
    place = lax.broadcasted_iota(jnp.int32, (1, slots * patch_pad), 1)
    key_image = jnp.full((1, slots * patch_pad), -1, jnp.int32)
    for slot in range(slots):
        inside = (place >= slot * patch_pad) & (place < slot * patch_pad + patch_rows)
        key_image = jnp.where(inside, slot_image(slot, slots, head), key_image)
    return jnp.where(image == key_image, 0.0, NEGATIVE)


def slot_image(slot, slots, head):
    half = slots // 2
    return half * (head if slot % 2 == 0 else 1 - head) + slot // 2


def attend(queries, keys, values, bias, parts):
    mixed, totals = 0.0, []
    for part in range(2):
        scores = dot_nt(jnp.where(parts[part], queries, 0), keys) + bias
        largest = jnp.max(scores, axis=1, keepdims=True)
        exponent = jnp.exp(scores - largest)
        total = jnp.sum(exponent, axis=1, keepdims=True)
        picked = dot(exponent.astype(BF16), values) * (1.0 / total)
        mixed = picked if part == 0 else jnp.where(parts[1], picked, mixed)
        totals.append(largest + jnp.log(total))
    return mixed, totals


def attend_back(queries, keys, values, grad, bias, totals, parts):
    both = []
    for part in range(2):
        query = jnp.where(parts[part], queries, 0)
        grad_part = jnp.where(parts[part], grad, 0)
        probs = jnp.exp(dot_nt(query, keys) + bias - totals[part])
        grad_probs = dot_nt(grad_part, values)
        inner = jnp.sum(probs * grad_probs, axis=1, keepdims=True)
        grad_scores = (probs * (grad_probs - inner)).astype(BF16)
        both.append((query, grad_part, probs.astype(BF16), grad_scores))
    query, grad_part, probs, grad_scores = [
        jnp.concatenate([both[0][k], both[1][k]], axis=0) for k in range(4)
    ]
    keys = jnp.concatenate([jnp.where(parts[part], keys, 0) for part in range(2)], axis=0)
    grad_q = dot(jnp.concatenate([both[0][3], both[1][3]], axis=1), keys)
    return grad_q * SCALE, dot_tn(grad_scores, query), dot_tn(probs, grad_part)


def self_forward(text, wq, wk, wv, wo, segments, early):
    tokens, width = text.shape
    inner = wq.shape[1]
    rows = 128

    def body(get, out, put, extra):
        text_in = get(0)[...]
        projected = [dot(text_in, get(1 + k)[...]).astype(BF16) for k in range(3)]
        for k in range(3):
            out[0][k] = projected[k]
        put(0)
        seg_row = get(5)[...]
        seg_col = column(seg_row)
        parts = [half_lanes(0), half_lanes(1)]
        lane = lax.broadcasted_iota(jnp.int32, (1, LANES), 1)
        for block in range(tokens // rows):
            first, size = window(block, tokens, rows)
            bias = self_bias(seg_col, seg_row, block, rows, first, size)
            here = slice(block * rows, (block + 1) * rows)
            stats = jnp.zeros((rows, LANES), F32)
            for pair in range(inner // LANES):
                cols = slice(pair * LANES, (pair + 1) * LANES)
                mixed, totals = attend(
                    out[0][0, here, cols] * SCALE,
                    out[0][1, first : first + size, cols],
                    out[0][2, first : first + size, cols],
                    bias,
                    parts,
                )
                out[1][here, cols] = mixed.astype(BF16)
                for part in range(2):
                    stats = jnp.where(lane == 2 * pair + part, totals[part], stats)
            out[2][here, :] = stats
        put(1)
        put(2)
        out[3][...] = dot(out[1][...], get(4)[...]).astype(BF16)
        put(3)

    return run(
        body,
        [text, wq, wk, wv, wo, segments] + early,
        [
            like((3, tokens, inner), BF16),
            like((tokens, inner), BF16),
            like((tokens, LANES), F32),
            like((tokens, width), BF16),
        ],
        flops=2 * tokens * width * inner * 4 + 8 * tokens * 256 * inner,
        name="self_forward",
    )


def cross_keys(some, first, wk, wv, before):
    half, patch_rows, vis = some.shape
    slots = 2 * half
    pad = -(-patch_rows // 16) * 16
    inner = wk.shape[1]

    def body(get, out, put, extra):
        weights = [get(1), get(2)]
        for k in range(2):
            for slot in range(first, slots, 2):
                top, end = slot * pad, (slot + 1) * pad
                out[k][end - 16 : end, :] = jnp.zeros((16, inner), BF16)
                out[k][top : top + patch_rows, :] = dot(
                    get(0)[slot // 2], weights[k][...]
                ).astype(BF16)

    return run(
        body,
        [some, wk, wv] + list(before),
        [like((slots * pad, inner), BF16)] * 2,
        aliases={3 + k: k for k in range(len(before))},
        name="cross_keys",
    )


def cross_queries_of(text, part_a, part_b, gain, bias, wq):
    tokens, width = text.shape

    def body(get, out, put, extra):
        residual = get(0)[...].astype(F32) + (get(1)[...].astype(F32) + get(2)[...].astype(F32))
        unit, _ = normalise(residual)
        normed = unit * get(3)[...] + get(4)[...]
        out[0][...] = normed
        low = normed.astype(BF16)
        out[1][...] = low
        out[2][...] = dot(low, get(5)[...]).astype(BF16)

    return run(
        body,
        [text, part_a, part_b, gain, bias, wq],
        [
            like((tokens, width), F32),
            like((tokens, width), BF16),
            like((tokens, wq.shape[1]), BF16),
        ],
        flops=2 * tokens * width * wq.shape[1],
        name="cross_queries",
    )


def cross_forward(queries, keys, values, wo, segments, images, dims):
    tokens, inner = queries.shape
    width = wo.shape[1]
    slots, patch_rows, pad = dims
    rows = tokens

    def body(get, out, put, extra):
        head = lax.axis_index("head")
        mask = cross_bias(column(get(4)[...]), get(5)[...], head, slots, patch_rows, pad)
        parts = [half_lanes(0), half_lanes(1)]
        lane = lax.broadcasted_iota(jnp.int32, (1, LANES), 1)
        for block in range(tokens // rows):
            here = slice(block * rows, (block + 1) * rows)
            stats = jnp.zeros((rows, LANES), F32)
            for pair in range(inner // LANES):
                cols = slice(pair * LANES, (pair + 1) * LANES)
                mixed, totals = attend(
                    get(0)[here, cols] * SCALE,
                    get(1)[:, cols],
                    get(2)[:, cols],
                    mask[here],
                    parts,
                )
                out[0][here, cols] = mixed.astype(BF16)
                for part in range(2):
                    stats = jnp.where(lane == 2 * pair + part, totals[part], stats)
            out[1][here, :] = stats
        out[2][...] = dot(out[0][...], get(3)[...]).astype(BF16)

    return run(
        body,
        [queries, keys, values, wo, segments, images],
        [
            like((tokens, inner), BF16),
            like((tokens, LANES), F32),
            like((tokens, width), BF16),
        ],
        flops=2 * tokens * width * inner + 4 * tokens * slots * pad * inner,
        name="cross_forward",
    )


def feed_forward(normed, part_a, part_b, gain, bias, w_in, w_out):
    tokens, width = normed.shape
    inner = w_in.shape[1]
    chunk = 256

    def body(get, out, put, extra):
        residual = get(0)[...] + (get(1)[...].astype(F32) + get(2)[...].astype(F32))
        unit, _ = normalise(residual)
        normed_two = unit * get(3)[...] + get(4)[...]
        out[0][...] = normed_two
        put(0)
        out[1][...] = normed_two.astype(BF16)
        put(1)
        get(5)
        for start in range(0, inner, chunk):
            cols = slice(start, start + chunk)
            pre = dot(out[1][...], get(5)[:, cols])
            phi = 0.5 * (1.0 + lax.erf(pre * (0.5**0.5)))
            bell = jnp.exp(pre * pre * -0.5) * 0.3989422804014327
            out[2][:, cols] = (pre * phi).astype(BF16)
            out[3][:, cols] = (phi + pre * bell).astype(BF16)
        put(2)
        put(3)
        out[4][...] = dot(out[2][...], get(6)[...]).astype(BF16)
        put(4)

    return run(
        body,
        [normed, part_a, part_b, gain, bias, w_in, w_out],
        [
            like((tokens, width), F32),
            like((tokens, width), BF16),
            like((tokens, inner), BF16),
            like((tokens, inner), BF16),
            like((tokens, width), BF16),
        ],
        flops=4 * tokens * width * inner,
        name="feed_forward",
    )


def feed_backward(normed, part_a, part_b, gain, bias, cotangent, w_out, slopes, w_in):
    tokens, width = normed.shape
    inner = w_in.shape[1]
    chunk = 256

    def body(get, out, put, extra):
        residual = get(0)[...] + (get(1)[...].astype(F32) + get(2)[...].astype(F32))
        unit, inverse = normalise(residual)
        gain_row = get(3)[...]
        out[0][...] = unit * gain_row + get(4)[...]
        put(0)
        grad = get(5)[...]
        out[5][0:1, :], out[5][1:2, :] = norm_sums(grad, unit)
        put(5)
        grad_residual = norm_back(grad, unit, inverse, gain_row)
        out[1][...] = grad_residual
        put(1)
        out[2][...] = grad_residual.astype(BF16)
        put(2)
        get(6)
        get(7)
        for start in range(0, inner, chunk):
            cols = slice(start, start + chunk)
            grad_hidden = dot_nt(out[2][...], get(6)[cols, :])
            out[3][:, cols] = (grad_hidden * get(7)[:, cols].astype(F32)).astype(BF16)
        put(3)
        out[4][...] = dot_nt(out[3][...], get(8)[...]).astype(BF16)
        put(4)

    return run(
        body,
        [normed, part_a, part_b, gain, bias, cotangent, w_out, slopes, w_in],
        [
            like((tokens, width), F32),
            like((tokens, width), F32),
            like((tokens, width), BF16),
            like((tokens, inner), BF16),
            like((tokens, width), BF16),
            like((2, width), F32),
        ],
        flops=4 * tokens * width * inner,
        name="feed_backward",
    )


def cross_backward(
    grad_in, part_a, part_b, normed, fwd_a, fwd_b, gain, wo, queries, keys, values, stats,
    segments, images, wq, dims,
):
    tokens, width = grad_in.shape
    inner = queries.shape[1]
    slots, patch_rows, pad = dims
    rows = tokens

    def body(get, out, put, extra):
        residual = get(3)[...] + (get(4)[...].astype(F32) + get(5)[...].astype(F32))
        unit, inverse = normalise(residual)
        grad = get(0)[...] + (get(1)[...].astype(F32) + get(2)[...].astype(F32))
        out[6][0:1, :], out[6][1:2, :] = norm_sums(grad, unit)
        put(6)
        grad_residual = norm_back(grad, unit, inverse, get(6)[...])
        out[0][...] = grad_residual
        put(0)
        out[1][...] = grad_residual.astype(BF16)
        put(1)
        grad_mixed = extra[0]
        grad_mixed[...] = dot_nt(out[1][...], get(7)[...]).astype(BF16)
        head = lax.axis_index("head")
        mask = cross_bias(column(get(12)[...]), get(13)[...], head, slots, patch_rows, pad)
        parts = [half_lanes(0), half_lanes(1)]
        for k in range(8, 12):
            get(k)
        for pair in range(inner // LANES):
            cols = slice(pair * LANES, (pair + 1) * LANES)
            grad_k, grad_v = 0.0, 0.0
            for block in range(tokens // rows):
                here = slice(block * rows, (block + 1) * rows)
                totals = [get(11)[here, 2 * pair + part : 2 * pair + part + 1] for part in range(2)]
                grad_q, more_k, more_v = attend_back(
                    get(8)[here, cols] * SCALE,
                    get(9)[:, cols],
                    get(10)[:, cols],
                    grad_mixed[here, cols],
                    mask[here],
                    totals,
                    parts,
                )
                out[2][here, cols] = grad_q.astype(BF16)
                grad_k, grad_v = grad_k + more_k, grad_v + more_v
            out[3][:, cols] = grad_k.astype(BF16)
            out[4][:, cols] = grad_v.astype(BF16)
        put(2)
        put(3)
        put(4)
        out[5][...] = dot_nt(out[2][...], get(14)[...]).astype(BF16)
        put(5)

    return run(
        body,
        [
            grad_in, part_a, part_b, normed, fwd_a, fwd_b, gain, wo, queries, keys, values, stats,
            segments, images, wq,
        ],
        [
            like((tokens, width), F32),
            like((tokens, width), BF16),
            like((tokens, inner), BF16),
            like((slots * pad, inner), BF16),
            like((slots * pad, inner), BF16),
            like((tokens, width), BF16),
            like((2, width), F32),
        ],
        scratch=[pltpu.VMEM((tokens, inner), BF16)],
        flops=4 * tokens * width * inner + 10 * tokens * slots * pad * inner,
        name="cross_backward",
    )


def self_backward(
    grad_in, part_a, part_b, text, fwd_a, fwd_b, gain, wo, projected, stats, segments, wq, wk, wv
):
    tokens, width = grad_in.shape
    inner = wq.shape[1]
    rows = tokens

    def body(get, out, put, extra):
        residual = get(3)[...].astype(F32) + (get(4)[...].astype(F32) + get(5)[...].astype(F32))
        unit, inverse = normalise(residual)
        grad = get(0)[...] + (get(1)[...].astype(F32) + get(2)[...].astype(F32))
        out[4][0:1, :], out[4][1:2, :] = norm_sums(grad, unit)
        put(4)
        grad_residual = norm_back(grad, unit, inverse, get(6)[...])
        out[0][...] = grad_residual
        put(0)
        out[1][...] = grad_residual.astype(BF16)
        put(1)
        grad_mixed, grad_keys, grad_values = extra
        grad_mixed[...] = dot_nt(out[1][...], get(7)[...]).astype(BF16)
        grad_keys[...] = jnp.zeros_like(grad_keys)
        grad_values[...] = jnp.zeros_like(grad_values)
        seg_row = get(10)[...]
        seg_col = column(seg_row)
        parts = [half_lanes(0), half_lanes(1)]
        get(8)
        get(9)
        for block in range(tokens // rows):
            first, size = window(block, tokens, rows)
            bias = self_bias(seg_col, seg_row, block, rows, first, size)
            here = slice(block * rows, (block + 1) * rows)
            there = slice(first, first + size)
            for pair in range(inner // LANES):
                cols = slice(pair * LANES, (pair + 1) * LANES)
                totals = [get(9)[here, 2 * pair + part : 2 * pair + part + 1] for part in range(2)]
                grad_q, grad_k, grad_v = attend_back(
                    get(8)[0, here, cols] * SCALE,
                    get(8)[1, there, cols],
                    get(8)[2, there, cols],
                    grad_mixed[here, cols],
                    bias,
                    totals,
                    parts,
                )
                out[2][here, cols] = grad_q.astype(BF16)
                grad_keys[there, cols] += grad_k
                grad_values[there, cols] += grad_v
        out[2][:, inner : 2 * inner] = grad_keys[...].astype(BF16)
        out[2][:, 2 * inner :] = grad_values[...].astype(BF16)
        put(2)
        total = 0.0
        for k in range(3):
            total = total + dot_nt(out[2][:, k * inner : (k + 1) * inner], get(11 + k)[...])
        out[3][...] = total.astype(BF16)
        put(3)

    return run(
        body,
        [
            grad_in, part_a, part_b, text, fwd_a, fwd_b, gain, wo, projected, stats, segments,
            wq, wk, wv,
        ],
        [
            like((tokens, width), F32),
            like((tokens, width), BF16),
            like((tokens, 3 * inner), BF16),
            like((tokens, width), BF16),
            like((2, width), F32),
        ],
        scratch=[
            pltpu.VMEM((tokens, inner), BF16),
            pltpu.VMEM((tokens, inner), F32),
            pltpu.VMEM((tokens, inner), F32),
        ],
        flops=8 * tokens * width * inner + 10 * tokens * 256 * inner,
        name="self_backward",
    )


def patch_backward(grad_keys, grad_values, wk, wv, dims):
    slots, patch_rows, pad = dims
    vis, inner = wk.shape
    width = vis // 2

    def body(get, out, put, extra):
        head = lax.axis_index("head")
        weights = [get(2), get(3)]
        grads = [get(0), get(1)]
        for k in range(2):
            first = pl.multiple_of((head if k == 0 else 1 - head) * width, width)
            left, right = (weights[j][pl.ds(first, width), :] for j in range(2))
            for slot in range(slots):
                rows = slice(slot * pad, (slot + 1) * pad)
                total = dot_nt(grads[0][rows, :], left) + dot_nt(grads[1][rows, :], right)
                out[k][slot_image(slot, slots, head)] = total[:patch_rows].astype(BF16)
            put(k)

    return run(
        body,
        [grad_keys, grad_values, wk, wv],
        [like((slots, patch_rows, width), BF16)] * 2,
        flops=4 * slots * pad * vis * inner,
        name="patch_backward",
    )


def offset_of(position, digits):
    count = len(digits)
    return sum(
        ((position >> (count - 1 - step)) & 1) << digit for step, digit in enumerate(digits)
    )


def weight_grads(inputs, blocks, streams, held, groups, columns, flops, name, chosen=None):
    chosen = streams if chosen is None else chosen
    bottoms = {}
    for k, stream in enumerate(streams):
        bottoms[stream] = sum(other.rows for other in streams[:k])
    outs = []
    for stream in chosen:
        outs += [like((stream.entries // 2 * stream.rows, columns), BF16)] * 2

    def body(get, out, put, scratch):
        me = lax.axis_index("dp") * lax.axis_size("stream") + lax.axis_index("stream")
        first = 0
        for block, (piece, product) in enumerate(blocks):
            whole = scratch[block]
            cuts = []
            for k, stream in enumerate(chosen):
                bottom = bottoms[stream]
                low = max(first, bottom)
                high = min(first + piece, bottom + stream.rows)
                if low < high:
                    cuts.append((k, stream, low, high))
            if cuts:
                product(get, whole)
            for k, stream, low, high in cuts:
                for position in range(stream.entries):
                    side, entry = divmod(position, stream.entries // 2)
                    source = (me ^ offset_of(position, stream.digits)) * piece + (low - first)
                    target = entry * stream.rows + low - bottoms[stream]
                    out[2 * k + side][target : target + high - low, :] = whole[
                        pl.ds(pl.multiple_of(source, 16), high - low), :
                    ]
            first += piece

    results = run(
        body,
        inputs,
        outs,
        scratch=[pltpu.VMEM((groups * piece, columns), BF16) for piece, _ in blocks],
        flops=flops,
        name=name,
    )
    for k, stream in enumerate(chosen):
        held += [results[2 * k], results[2 * k + 1]]
        stream.terms, stream.send = [(len(held) - 2, 0)], len(held) - 1


def product(left, right, first=None, size=None):
    def fill(get, whole):
        columns = get(right)[...] if first is None else get(right)[:, first : first + size]
        whole[...] = dot_tn(get(left)[...], columns).astype(BF16)

    return fill


def finish(streams, held, piece, vis_piece, blocks):
    columns = held[0].shape[1]
    used, places = [], {}
    for batch in streams.values():
        for stream in batch:
            for index, _ in stream.terms:
                if index not in places:
                    places[index] = len(used)
                    used.append(held[index])

    def body(get, out, put, scratch):
        def rows_of(batch, low, high):
            parts, bottom = [], 0
            for stream in batch:
                first, last = max(low, bottom) - bottom, min(high, bottom + stream.rows) - bottom
                if first < last:
                    total = 0.0
                    for index, row in stream.terms:
                        total = total + get(places[index])[row + first : row + last, :].astype(F32)
                    parts.append(total)
                bottom += stream.rows
            return parts[0] if len(parts) == 1 else jnp.concatenate(parts)

        for k in range(2 * blocks):
            out[k // blocks][:, k % blocks * columns : (k % blocks + 1) * columns] = rows_of(
                streams["ff"], k * piece, (k + 1) * piece
            )
        for k in range(2):
            out[2 + k][...] = rows_of(streams["cross"], k * piece, (k + 1) * piece)
            low = 2 * piece + k * vis_piece
            out[4 + k][...] = rows_of(streams["cross"], low, low + vis_piece)
        for k in range(4):
            out[6 + k][...] = rows_of(streams["self"], k * piece, (k + 1) * piece)
        vectors = rows_of(streams["self"], 4 * piece, 4 * piece + 16)
        for k in range(6):
            out[10 + k][...] = vectors[k, :piece]

    return run(
        body,
        used,
        [like((piece, blocks * columns), F32)] * 2
        + [like((piece, columns), F32)] * 2
        + [like((vis_piece, columns), F32)] * 2
        + [like((piece, columns), F32)] * 4
        + [like((piece,), F32)] * 6,
        name="finish",
    )


def project(left, right):
    return jnp.dot(left, right, preferred_element_type=F32)


def head_sum(partial_rows):
    return partial_rows, partner(partial_rows, "head", 0)


def body(
    text,
    patches,
    segment_ids,
    phrase_image,
    wq_self,
    wk_self,
    wv_self,
    wo_self,
    ln1_gain,
    ln1_bias,
    wq_cross,
    wk_cross,
    wv_cross,
    wo_cross,
    ln2_gain,
    ln2_bias,
    w_in,
    w_out,
    ln3_gain,
    ln3_bias,
    cotangent,
):
    slots, patch_rows, vis = patches.shape
    half = slots // 2
    pad = -(-patch_rows // 16) * 16
    dims = (slots, patch_rows, pad)
    tokens, width = text.shape
    inner = wq_self.shape[1]
    hidden_width = w_in.shape[1]
    groups = lax.axis_size("dp") * lax.axis_size("stream")
    head = lax.axis_index("head")
    row = lambda vector: vector.reshape(1, width)

    near = partner(lax.dynamic_slice_in_dim(patches, head * half, half, 0), "stream", 0)
    projected, attended, self_stats, part1 = self_forward(
        text, wq_self, wk_self, wv_self, wo_self, segment_ids, [wk_cross, wv_cross]
    )
    attended, near = lax.optimization_barrier((attended, near))
    other = partner(near, "head", 0)
    part1_a, part1_b = head_sum(part1)
    normed1, normed1_low, cross_queries = cross_queries_of(
        text, part1_a, part1_b, row(ln1_gain), row(ln1_bias), wq_cross
    )
    keys_values = cross_keys(near, 0, wk_cross, wv_cross, ())
    keys_cross, values_cross = cross_keys(other, 1, wk_cross, wv_cross, keys_values)
    cross_attended, cross_stats, part2 = cross_forward(
        cross_queries, keys_cross, values_cross, wo_cross, segment_ids, phrase_image, dims
    )
    part2_a, part2_b = head_sum(part2)
    normed2, normed2_low, hidden, slopes, part3 = feed_forward(
        normed1, part2_a, part2_b, row(ln2_gain), row(ln2_bias), w_in, w_out
    )
    part3_a, part3_b = head_sum(part3)
    output, grad_residual3, grad_three_low, grad_pre, part4, norm3 = feed_backward(
        normed2, part3_a, part3_b, row(ln3_gain), row(ln3_bias), cotangent, w_out, slopes, w_in
    )
    part4_a, part4_b = head_sum(part4)
    piece = width // groups
    fast = groups == 2**LINKS and piece % 16 == 0 and vis % (16 * groups) == 0
    order = Order()
    held, streams = Held(), {}
    if fast:
        streams = {name: [Stream(*stream) for stream in plan] for name, plan in PLAN.items()}
        everything = [stream for batch in streams.values() for stream in batch]
        blocks = hidden_width // inner
        links = {}
        for stream in streams["ff"]:
            links.setdefault(stream.steps[0], []).append(stream)
        for chosen in sorted(links.values(), key=lambda batch: -sum(part.rows for part in batch)):
            weight_grads(
                [order.after(grad_three_low), hidden, normed2_low, grad_pre],
                [(piece, product(0, 1, k * inner, inner)) for k in range(blocks)]
                + [(piece, product(2, 3, k * inner, inner)) for k in range(blocks)],
                streams["ff"],
                held,
                groups,
                inner,
                0,
                "ff_weight_grads",
                chosen,
            )
            away, _ = merge(chosen, 0, held, name="merge_0")
            order.passed(away)
    grad_residual2, grad_two_low, grad_cross_queries, grad_keys, grad_values, part5, norm2 = (
        cross_backward(
            order.after(grad_residual3), part4_a, part4_b, normed1, part2_a, part2_b,
            row(ln2_gain), wo_cross, cross_queries, keys_cross, values_cross, cross_stats,
            segment_ids, phrase_image, wq_cross, dims,
        )
    )
    part5_a, part5_b = head_sum(part5)
    if fast:
        def kv(which):
            def fill(get, whole):
                total = 0.0
                for slot in range(slots):
                    rows_in = get(4 + slot % 2)[slot // 2]
                    grads = get(6 + which)[slot * pad : slot * pad + patch_rows, :]
                    total = total + dot_tn(rows_in, grads)
                whole[...] = total.astype(BF16)

            return fill

        weight_grads(
            [grad_two_low, cross_attended, normed1_low, grad_cross_queries, near,
             other, grad_keys, grad_values],
            [
                (piece, product(0, 1)),
                (piece, product(2, 3)),
                (vis // groups, kv(0)),
                (vis // groups, kv(1)),
            ],
            streams["cross"],
            held,
            groups,
            inner,
            4 * tokens * width * inner + 4 * slots * pad * vis * inner,
            "cross_weight_grads",
        )
        away, _ = merge(streams["ff"] + streams["cross"], 1, held, name="merge_1")
        order.passed(away)
    grad_residual1, grad_one_low, grad_qkv, part6, norm1 = self_backward(
        order.after(grad_residual2), part5_a, part5_b, text, part1_a, part1_b, row(ln1_gain),
        wo_self, projected, self_stats, segment_ids, wq_self, wk_self, wv_self,
    )
    part6_a, part6_b = head_sum(part6)
    grad_keys, _ = lax.optimization_barrier((grad_keys, grad_qkv))
    patch_own, patch_away = patch_backward(grad_keys, grad_values, wk_cross, wv_cross, dims)
    patch_other = partner(patch_away, "head", 0)
    add_patches = (
        [patch_own, patch_other],
        [like(patch_own.shape, BF16)],
        lambda get, out: out[0].__setitem__(
            ..., (get(0)[...].astype(F32) + get(1)[...].astype(F32)).astype(BF16)
        ),
    )
    grad_text = grad_residual1 + (part6_a.astype(F32) + part6_b.astype(F32))
    if fast:
        def norms(get, whole):
            rows = jnp.concatenate([get(k)[...] for k in (4, 5, 6)] + [jnp.zeros((2, width), F32)])
            inside = lax.broadcasted_iota(jnp.int32, (8, inner), 1) < piece
            for group in range(groups):
                turned = pltpu.roll(rows, (width - group * piece) % width, 1)[:, :inner]
                entry = jnp.concatenate([jnp.where(inside, turned, 0.0), jnp.zeros((8, inner), F32)])
                whole[group * 16 : (group + 1) * 16, :] = entry.astype(BF16)

        weight_grads(
            [grad_one_low, attended, text, grad_qkv, norm1, norm2, norm3],
            [(piece, product(2, 3, k * inner, inner)) for k in range(3)]
            + [(piece, product(0, 1)), (16, norms)],
            streams["self"],
            held,
            groups,
            inner,
            8 * tokens * width * inner,
            "self_weight_grads",
        )
        grad_patches = None
        early = held.recent[0]
        held[early], patch_own, _ = lax.optimization_barrier((held[early], patch_own, held[-1]))
        for phase in range(2, PHASES):
            work = add_patches if phase == PATCH_PHASE else ((), (), None)
            if phase == PATCH_PHASE + 1:
                held[-1], grad_patches = lax.optimization_barrier((held[-1], grad_patches))
            away, more = merge(everything, phase, held, *work, name="merge_%d" % phase)
            if phase == PATCH_PHASE:
                grad_patches = partner(more[0], "stream", 0)
        grad_patches = grad_patches.astype(F32)
        shares = finish(streams, held, piece, vis // groups, blocks)
        own_w_out, own_w_in, cross_wo, cross_wq, cross_wk, cross_wv = shares[:6]
        self_wq, self_wk, self_wv, self_wo = shares[6:10]
        own_w_out, cross_wo, self_wo = own_w_out.T, cross_wo.T, self_wo.T
        own_norms = shares[10:]
    else:
        patch_sum = (patch_own.astype(F32) + patch_other.astype(F32)).astype(BF16)
        grad_patches = partner(patch_sum, "stream", 0).astype(F32)
        norm_grads = jnp.concatenate([norm1, norm2, norm3, jnp.zeros((2, width), F32)])

        def plain(left, right):
            grad = jnp.einsum("ta,tb->ab", left, right, preferred_element_type=F32)
            grad = grad.astype(BF16).reshape(groups, grad.shape[0] // groups, grad.shape[1])
            return scatter_sum_plain(grad)

        own_w_out = plain(grad_three_low, hidden).T
        own_w_in = plain(normed2_low, grad_pre)
        cross_wo = plain(grad_two_low, cross_attended).T
        cross_wq = plain(normed1_low, grad_cross_queries)
        far = jnp.stack([near, other], axis=1).reshape(slots, patch_rows, vis)
        far = jnp.pad(far, ((0, 0), (0, pad - patch_rows), (0, 0))).reshape(slots * pad, vis)
        cross_wk, cross_wv = plain(far, grad_keys), plain(far, grad_values)
        self_wq, self_wk, self_wv = jnp.split(plain(text, grad_qkv), 3, axis=1)
        self_wo = plain(grad_one_low, attended).T
        own_norms = scatter_sum_plain(
            norm_grads.reshape(8, groups, width // groups).swapaxes(0, 1).astype(BF16)
        )
    return (
        output,
        grad_text,
        grad_patches,
        self_wq,
        self_wk,
        self_wv,
        self_wo,
        own_norms[0],
        own_norms[1],
        cross_wq,
        cross_wk,
        cross_wv,
        cross_wo,
        own_norms[2],
        own_norms[3],
        own_w_in,
        own_w_out,
        own_norms[4],
        own_norms[5],
    )


def solution(mesh):
    in_specs = (
        P(("dp", "stream"), None),
        P(("dp", "stream"), None, None),
        P(("dp", "stream"), None),
        P(("dp", "stream"), None),
        P(None, "head"),
        P(None, "head"),
        P(None, "head"),
        P("head", None),
        P(),
        P(),
        P(None, "head"),
        P(None, "head"),
        P(None, "head"),
        P("head", None),
        P(),
        P(),
        P(None, "head"),
        P("head", None),
        P(),
        P(),
        P(("dp", "stream"), None),
    )
    out_specs = (
        P(("dp", "stream"), None),
        P(("dp", "stream"), None),
        P(("dp", "stream"), None, "head"),
        P(("dp", "stream"), "head"),
        P(("dp", "stream"), "head"),
        P(("dp", "stream"), "head"),
        P("head", ("dp", "stream")),
        P(("dp", "stream")),
        P(("dp", "stream")),
        P(("dp", "stream"), "head"),
        P(("dp", "stream"), "head"),
        P(("dp", "stream"), "head"),
        P("head", ("dp", "stream")),
        P(("dp", "stream")),
        P(("dp", "stream")),
        P(("dp", "stream"), "head"),
        P("head", ("dp", "stream")),
        P(("dp", "stream")),
        P(("dp", "stream")),
    )
    return jax.shard_map(body, mesh=mesh, in_specs=in_specs, out_specs=out_specs, check_vma=False)
```

```python
import jax
import jax.numpy as jnp
from jax import lax
from jax.experimental import pallas as pl
from jax.experimental.pallas import tpu as pltpu
from jax.sharding import PartitionSpec as P

HEAD_DIM = 64
LANES = 128
MAX_PHRASE = 48
EPSILON = 1e-12
NEGATIVE = -1e30
SCALE = HEAD_DIM ** (-0.5)
VMEM_LIMIT = 56 * 1024 * 1024
F32 = jnp.float32
BF16 = jnp.bfloat16


COSTS = {
    "self_forward": 0.8,
    "cross_queries": 0.1,
    "cross_keys": 0.3,
    "cross_forward": 6.2,
    "feed_forward": 3.3,
    "feed_backward": 3.3,
    "ff_weight_grads": 1.1,
    "cross_backward": 0.1,
    "cross_weight_grads": 3.3,
    "self_backward": 0.1,
    "self_weight_grads": 0.1,
    "patch_backward": 0.1,
}


def partner(value, axis, place):
    mask = 2**place
    pairs = [(source, source ^ mask) for source in range(lax.axis_size(axis))]
    return lax.ppermute(value, axis, pairs)


def group_bits():
    count = lax.axis_size("dp").bit_length() - 1
    return [("stream", 0)] + [("dp", place) for place in range(count)]


class Order:
    def __init__(self):
        self.last = None

    def after(self, value):
        if self.last is not None:
            value, _ = lax.optimization_barrier((value, self.last))
        return value

    def passed(self, value):
        self.last = value
        return value


LINKS = 4

PLAN = {
    "ff": ((48, ((0, 0), (1, 2), (2, 1), (3, 3))), (96, ((0, 0), (1, 2), (2, 3), (4, 1))), (128, ((0, 1), (1, 0), (2, 3), (4, 2))), (112, ((0, 2), (1, 3), (3, 1), (5, 0)))),
    "cross": ((48, ((1, 0), (2, 1), (3, 2), (4, 3))), (32, ((1, 0), (2, 2), (3, 3), (4, 1))), (96, ((1, 1), (2, 2), (3, 0), (4, 3))), (48, ((1, 1), (2, 0), (3, 3), (5, 2)))),
    "self": ((80, ((2, 0), (3, 1), (4, 3), (5, 2))), (32, ((2, 0), (3, 2), (4, 1), (5, 3))), (96, ((2, 1), (3, 0), (4, 2), (5, 3)))),
}
PHASES = 6
PATCH_PHASE = 4


class Stream:
    def __init__(self, rows, steps):
        self.rows, self.steps = rows, dict(steps)
        self.digits = [digit for _, digit in steps]
        self.entries = 2 ** len(steps)
        self.terms, self.send, self.sent = [], None, None


class Held(list):
    recent = ()
    phase = None


def gather_messages(streams, phase):
    messages = {}
    for stream in streams:
        if phase in stream.steps:
            pieces = messages.setdefault(stream.steps[phase], [])
            first = sum(rows for _, _, rows in pieces)
            pieces.append((stream, first, stream.entries // 2 * stream.rows))
    return messages


def start_messages(messages, arrays, held, phase):
    if held.phase != phase:
        held.phase, held.recent = phase, []
    for (digit, pieces), away in zip(sorted(messages.items()), arrays):
        axis, place = group_bits()[digit]
        held.recent.append(len(held))
        held.append(partner(away, axis, place))
        for stream, first, _ in pieces:
            stream.terms.append((len(held) - 1, first))
            stream.entries //= 2


def merge(streams, phase, held, extra_inputs=(), extra_outs=(), extra=None, name=None):
    messages = gather_messages(streams, phase)
    before = None
    for k in held.recent if held.phase != phase else ():
        if before is not None:
            held[k], _ = lax.optimization_barrier((held[k], held[before]))
        before = k
    if before is not None:
        for k, value in zip(
            held.recent, lax.optimization_barrier(tuple(held[k] for k in held.recent))
        ):
            held[k] = value
    used, places = [], {}

    def place(index):
        if index not in places:
            places[index] = len(used)
            used.append(held[index])
        return places[index]

    columns = held[0].shape[1]
    jobs, outs, aways = [], [], []
    for _, pieces in sorted(messages.items()):
        if len(pieces) == 1 and pieces[0][0].send is not None:
            aways.append(held[pieces[0][0].send])
            pieces[0][0].send = None
            continue
        aways.append(len(outs))
        for stream, first, rows in pieces:
            if stream.send is not None:
                sources = [(place(stream.send), 0)]
                stream.send = None
            else:
                sources = [(place(index), row + rows) for index, row in stream.terms]
            jobs.append((len(outs), first, rows, sources))
        outs.append(like((sum(rows for _, _, rows in pieces), columns), BF16))
    count = len(used)

    def body(get, out, put, scratch):
        for slot, first, rows, sources in jobs:
            parts = [get(k)[row : row + rows, :] for k, row in sources]
            if len(parts) > 1:
                total = parts[0].astype(F32)
                for part in parts[1:]:
                    total = total + part.astype(F32)
                parts = [total.astype(BF16)]
            out[slot][first : first + rows, :] = parts[0]
        if extra is not None:
            extra(lambda k: get(count + k), out[len(outs) :])

    results = []
    if outs or extra_outs:
        results = run(body, used + list(extra_inputs), outs + list(extra_outs), name=name)
    aways = [results[away] if isinstance(away, int) else away for away in aways]
    start_messages(messages, aways, held, phase)
    return aways, results[len(outs) :]


def scatter_sum_plain(grads):
    bits = group_bits()
    count = len(bits)
    grads = grads.reshape((2,) * count + grads.shape[1:])
    for step in range(count):
        axis, place = bits[step]
        dim = count - 1 - step
        mine = (lax.axis_index(axis) >> place) & 1
        away = lax.dynamic_index_in_dim(grads, 1 - mine, dim, keepdims=True)
        keep = lax.dynamic_index_in_dim(grads, mine, dim, keepdims=True)
        grads = keep.astype(F32) + partner(away, axis, place).astype(F32)
        if step < count - 1:
            grads = grads.astype(BF16)
    return grads.reshape(grads.shape[count:])


def run(body, inputs, outs, scratch=(), flops=0, aliases=None, name=None):
    n_in, n_out = len(inputs), len(outs)

    def kernel(*refs):
        ins, refs = refs[:n_in], refs[n_in:]
        body(lambda k: ins[k], refs[:n_out], lambda k: None, refs[n_out:])

    moved = sum(a.size * a.dtype.itemsize for a in inputs) + sum(
        a.size * a.dtype.itemsize for a in outs
    )
    return pl.pallas_call(
        kernel,
        name=name,
        out_shape=[jax.ShapeDtypeStruct(a.shape, a.dtype) for a in outs],
        in_specs=[pl.BlockSpec(memory_space=pltpu.VMEM)] * n_in,
        out_specs=[pl.BlockSpec(memory_space=pltpu.VMEM)] * n_out,
        scratch_shapes=list(scratch),
        input_output_aliases=aliases or {},
        compiler_params=pltpu.CompilerParams(vmem_limit_bytes=int(moved + 8 * 2**20 + sum(2 * 384 * 384 for _ in scratch))),
        cost_estimate=pl.CostEstimate(
            flops=int(1e9 * COSTS.get(name, 0.6)), bytes_accessed=1000, transcendentals=0
        ),
    )(*inputs)


def like(shape, dtype):
    return jax.ShapeDtypeStruct(shape, dtype)


def dot(left, right):
    return lax.dot_general(left, right, (((1,), (0,)), ((), ())), preferred_element_type=F32)


def dot_nt(left, right):
    return lax.dot_general(left, right, (((1,), (1,)), ((), ())), preferred_element_type=F32)


def dot_tn(left, right):
    return lax.dot_general(left, right, (((0,), (0,)), ((), ())), preferred_element_type=F32)


def normalise(rows):
    center = rows - jnp.mean(rows, axis=-1, keepdims=True)
    inverse = lax.rsqrt(jnp.mean(center * center, axis=-1, keepdims=True) + EPSILON)
    return center * inverse, inverse


def norm_back(grad, unit, inverse, gain):
    inner = grad * gain
    shift = jnp.mean(inner, axis=-1, keepdims=True)
    slope = jnp.mean(inner * unit, axis=-1, keepdims=True)
    return inverse * (inner - shift - unit * slope)


def norm_sums(grad, unit):
    return jnp.sum(grad * unit, axis=0, keepdims=True), jnp.sum(grad, axis=0, keepdims=True)


def column(row):
    wide = jnp.broadcast_to(row.astype(F32), (LANES, row.shape[1]))
    return jnp.transpose(wide)[:, :1].astype(jnp.int32)


def half_lanes(part):
    lane = lax.broadcasted_iota(jnp.int32, (1, LANES), 1)
    return (lane >= HEAD_DIM) if part else (lane < HEAD_DIM)


def window(block, tokens, rows):
    size = min(tokens, rows + 128)
    return min(max(block * rows - 64, 0), tokens - size), size


def self_bias(seg_col, seg_row, block, rows, first, size):
    same = seg_col[block * rows : (block + 1) * rows] == seg_row[:, first : first + size]
    return jnp.where(same, 0.0, NEGATIVE)


def cross_bias(seg_col, images_row, head, slots, patch_rows, patch_pad):
    phrases = images_row.shape[1]
    phrase = lax.broadcasted_iota(jnp.int32, (1, phrases), 1)
    image = jnp.sum(jnp.where(seg_col == phrase, images_row, 0), axis=1, keepdims=True)
    place = lax.broadcasted_iota(jnp.int32, (1, slots * patch_pad), 1)
    key_image = jnp.full((1, slots * patch_pad), -1, jnp.int32)
    for slot in range(slots):
        inside = (place >= slot * patch_pad) & (place < slot * patch_pad + patch_rows)
        key_image = jnp.where(inside, slot_image(slot, slots, head), key_image)
    return jnp.where(image == key_image, 0.0, NEGATIVE)


def slot_image(slot, slots, head):
    half = slots // 2
    return half * (head if slot % 2 == 0 else 1 - head) + slot // 2


def attend(queries, keys, values, bias, parts):
    mixed, totals = 0.0, []
    for part in range(2):
        scores = dot_nt(jnp.where(parts[part], queries, 0), keys) + bias
        largest = jnp.max(scores, axis=1, keepdims=True)
        exponent = jnp.exp(scores - largest)
        total = jnp.sum(exponent, axis=1, keepdims=True)
        picked = dot(exponent.astype(BF16), values) * (1.0 / total)
        mixed = picked if part == 0 else jnp.where(parts[1], picked, mixed)
        totals.append(largest + jnp.log(total))
    return mixed, totals


def attend_back(queries, keys, values, grad, bias, totals, parts):
    both = []
    for part in range(2):
        query = jnp.where(parts[part], queries, 0)
        grad_part = jnp.where(parts[part], grad, 0)
        probs = jnp.exp(dot_nt(query, keys) + bias - totals[part])
        grad_probs = dot_nt(grad_part, values)
        inner = jnp.sum(probs * grad_probs, axis=1, keepdims=True)
        grad_scores = (probs * (grad_probs - inner)).astype(BF16)
        both.append((query, grad_part, probs.astype(BF16), grad_scores))
    query, grad_part, probs, grad_scores = [
        jnp.concatenate([both[0][k], both[1][k]], axis=0) for k in range(4)
    ]
    keys = jnp.concatenate([jnp.where(parts[part], keys, 0) for part in range(2)], axis=0)
    grad_q = dot(jnp.concatenate([both[0][3], both[1][3]], axis=1), keys)
    return grad_q * SCALE, dot_tn(grad_scores, query), dot_tn(probs, grad_part)


def self_forward(text, wq, wk, wv, wo, segments, early):
    tokens, width = text.shape
    inner = wq.shape[1]
    rows = 128

    def body(get, out, put, extra):
        text_in = get(0)[...]
        projected = [dot(text_in, get(1 + k)[...]).astype(BF16) for k in range(3)]
        for k in range(3):
            out[0][k] = projected[k]
        put(0)
        seg_row = get(5)[...]
        seg_col = column(seg_row)
        parts = [half_lanes(0), half_lanes(1)]
        lane = lax.broadcasted_iota(jnp.int32, (1, LANES), 1)
        for block in range(tokens // rows):
            first, size = window(block, tokens, rows)
            bias = self_bias(seg_col, seg_row, block, rows, first, size)
            here = slice(block * rows, (block + 1) * rows)
            stats = jnp.zeros((rows, LANES), F32)
            for pair in range(inner // LANES):
                cols = slice(pair * LANES, (pair + 1) * LANES)
                mixed, totals = attend(
                    out[0][0, here, cols] * SCALE,
                    out[0][1, first : first + size, cols],
                    out[0][2, first : first + size, cols],
                    bias,
                    parts,
                )
                out[1][here, cols] = mixed.astype(BF16)
                for part in range(2):
                    stats = jnp.where(lane == 2 * pair + part, totals[part], stats)
            out[2][here, :] = stats
        put(1)
        put(2)
        out[3][...] = dot(out[1][...], get(4)[...]).astype(BF16)
        put(3)

    return run(
        body,
        [text, wq, wk, wv, wo, segments] + early,
        [
            like((3, tokens, inner), BF16),
            like((tokens, inner), BF16),
            like((tokens, LANES), F32),
            like((tokens, width), BF16),
        ],
        flops=2 * tokens * width * inner * 4 + 8 * tokens * 256 * inner,
        name="self_forward",
    )


def cross_keys(some, first, wk, wv, before):
    half, patch_rows, vis = some.shape
    slots = 2 * half
    pad = -(-patch_rows // 16) * 16
    inner = wk.shape[1]

    def body(get, out, put, extra):
        weights = [get(1), get(2)]
        for k in range(2):
            for slot in range(first, slots, 2):
                top, end = slot * pad, (slot + 1) * pad
                out[k][end - 16 : end, :] = jnp.zeros((16, inner), BF16)
                out[k][top : top + patch_rows, :] = dot(
                    get(0)[slot // 2], weights[k][...]
                ).astype(BF16)

    return run(
        body,
        [some, wk, wv] + list(before),
        [like((slots * pad, inner), BF16)] * 2,
        aliases={3 + k: k for k in range(len(before))},
        name="cross_keys",
    )


def cross_queries_of(text, part_a, part_b, gain, bias, wq):
    tokens, width = text.shape

    def body(get, out, put, extra):
        residual = get(0)[...].astype(F32) + (get(1)[...].astype(F32) + get(2)[...].astype(F32))
        unit, _ = normalise(residual)
        normed = unit * get(3)[...] + get(4)[...]
        out[0][...] = normed
        low = normed.astype(BF16)
        out[1][...] = low
        out[2][...] = dot(low, get(5)[...]).astype(BF16)

    return run(
        body,
        [text, part_a, part_b, gain, bias, wq],
        [
            like((tokens, width), F32),
            like((tokens, width), BF16),
            like((tokens, wq.shape[1]), BF16),
        ],
        flops=2 * tokens * width * wq.shape[1],
        name="cross_queries",
    )


def cross_forward(queries, keys, values, wo, segments, images, dims):
    tokens, inner = queries.shape
    width = wo.shape[1]
    slots, patch_rows, pad = dims
    rows = tokens

    def body(get, out, put, extra):
        head = lax.axis_index("head")
        mask = cross_bias(column(get(4)[...]), get(5)[...], head, slots, patch_rows, pad)
        parts = [half_lanes(0), half_lanes(1)]
        lane = lax.broadcasted_iota(jnp.int32, (1, LANES), 1)
        for block in range(tokens // rows):
            here = slice(block * rows, (block + 1) * rows)
            stats = jnp.zeros((rows, LANES), F32)
            for pair in range(inner // LANES):
                cols = slice(pair * LANES, (pair + 1) * LANES)
                mixed, totals = attend(
                    get(0)[here, cols] * SCALE,
                    get(1)[:, cols],
                    get(2)[:, cols],
                    mask[here],
                    parts,
                )
                out[0][here, cols] = mixed.astype(BF16)
                for part in range(2):
                    stats = jnp.where(lane == 2 * pair + part, totals[part], stats)
            out[1][here, :] = stats
        out[2][...] = dot(out[0][...], get(3)[...]).astype(BF16)

    return run(
        body,
        [queries, keys, values, wo, segments, images],
        [
            like((tokens, inner), BF16),
            like((tokens, LANES), F32),
            like((tokens, width), BF16),
        ],
        flops=2 * tokens * width * inner + 4 * tokens * slots * pad * inner,
        name="cross_forward",
    )


def feed_forward(normed, part_a, part_b, gain, bias, w_in, w_out):
    tokens, width = normed.shape
    inner = w_in.shape[1]
    chunk = 256

    def body(get, out, put, extra):
        residual = get(0)[...] + (get(1)[...].astype(F32) + get(2)[...].astype(F32))
        unit, _ = normalise(residual)
        normed_two = unit * get(3)[...] + get(4)[...]
        out[0][...] = normed_two
        put(0)
        out[1][...] = normed_two.astype(BF16)
        put(1)
        get(5)
        for start in range(0, inner, chunk):
            cols = slice(start, start + chunk)
            pre = dot(out[1][...], get(5)[:, cols])
            phi = 0.5 * (1.0 + lax.erf(pre * (0.5**0.5)))
            bell = jnp.exp(pre * pre * -0.5) * 0.3989422804014327
            out[2][:, cols] = (pre * phi).astype(BF16)
            out[3][:, cols] = (phi + pre * bell).astype(BF16)
        put(2)
        put(3)
        out[4][...] = dot(out[2][...], get(6)[...]).astype(BF16)
        put(4)

    return run(
        body,
        [normed, part_a, part_b, gain, bias, w_in, w_out],
        [
            like((tokens, width), F32),
            like((tokens, width), BF16),
            like((tokens, inner), BF16),
            like((tokens, inner), BF16),
            like((tokens, width), BF16),
        ],
        flops=4 * tokens * width * inner,
        name="feed_forward",
    )


def last_norm(normed, part_a, part_b, gain, bias):
    def body(get, out, put, extra):
        residual = get(0)[...] + (get(1)[...].astype(F32) + get(2)[...].astype(F32))
        out[0][...] = normalise(residual)[0] * get(3)[...] + get(4)[...]

    return run(
        body,
        [normed, part_a, part_b, gain, bias],
        [like(normed.shape, F32)],
        name="last_norm",
    )[0]


def feed_backward(normed, part_a, part_b, gain, cotangent, w_out, slopes, w_in):
    tokens, width = normed.shape
    inner = w_in.shape[1]
    chunk = 256

    def body(get, out, put, extra):
        residual = get(0)[...] + (get(1)[...].astype(F32) + get(2)[...].astype(F32))
        unit, inverse = normalise(residual)
        grad = get(4)[...]
        out[4][0:1, :], out[4][1:2, :] = norm_sums(grad, unit)
        grad_residual = norm_back(grad, unit, inverse, get(3)[...])
        out[0][...] = grad_residual
        out[1][...] = grad_residual.astype(BF16)
        for start in range(0, inner, chunk):
            cols = slice(start, start + chunk)
            grad_hidden = dot_nt(out[1][...], get(5)[cols, :])
            out[2][:, cols] = (grad_hidden * get(6)[:, cols].astype(F32)).astype(BF16)
        out[3][...] = dot_nt(out[2][...], get(7)[...]).astype(BF16)

    return run(
        body,
        [normed, part_a, part_b, gain, cotangent, w_out, slopes, w_in],
        [
            like((tokens, width), F32),
            like((tokens, width), BF16),
            like((tokens, inner), BF16),
            like((tokens, width), BF16),
            like((2, width), F32),
        ],
        flops=4 * tokens * width * inner,
        name="feed_backward",
    )


def cross_backward(
    grad_in, part_a, part_b, normed, fwd_a, fwd_b, gain, wo, queries, keys, values, stats,
    segments, images, wq, dims,
):
    tokens, width = grad_in.shape
    inner = queries.shape[1]
    slots, patch_rows, pad = dims
    rows = tokens

    def body(get, out, put, extra):
        residual = get(3)[...] + (get(4)[...].astype(F32) + get(5)[...].astype(F32))
        unit, inverse = normalise(residual)
        grad = get(0)[...] + (get(1)[...].astype(F32) + get(2)[...].astype(F32))
        out[6][0:1, :], out[6][1:2, :] = norm_sums(grad, unit)
        put(6)
        grad_residual = norm_back(grad, unit, inverse, get(6)[...])
        out[0][...] = grad_residual
        put(0)
        out[1][...] = grad_residual.astype(BF16)
        put(1)
        grad_mixed = extra[0]
        grad_mixed[...] = dot_nt(out[1][...], get(7)[...]).astype(BF16)
        head = lax.axis_index("head")
        mask = cross_bias(column(get(12)[...]), get(13)[...], head, slots, patch_rows, pad)
        parts = [half_lanes(0), half_lanes(1)]
        for k in range(8, 12):
            get(k)
        for pair in range(inner // LANES):
            cols = slice(pair * LANES, (pair + 1) * LANES)
            grad_k, grad_v = 0.0, 0.0
            for block in range(tokens // rows):
                here = slice(block * rows, (block + 1) * rows)
                totals = [get(11)[here, 2 * pair + part : 2 * pair + part + 1] for part in range(2)]
                grad_q, more_k, more_v = attend_back(
                    get(8)[here, cols] * SCALE,
                    get(9)[:, cols],
                    get(10)[:, cols],
                    grad_mixed[here, cols],
                    mask[here],
                    totals,
                    parts,
                )
                out[2][here, cols] = grad_q.astype(BF16)
                grad_k, grad_v = grad_k + more_k, grad_v + more_v
            out[3][:, cols] = grad_k.astype(BF16)
            out[4][:, cols] = grad_v.astype(BF16)
        put(2)
        put(3)
        put(4)
        out[5][...] = dot_nt(out[2][...], get(14)[...]).astype(BF16)
        put(5)

    return run(
        body,
        [
            grad_in, part_a, part_b, normed, fwd_a, fwd_b, gain, wo, queries, keys, values, stats,
            segments, images, wq,
        ],
        [
            like((tokens, width), F32),
            like((tokens, width), BF16),
            like((tokens, inner), BF16),
            like((slots * pad, inner), BF16),
            like((slots * pad, inner), BF16),
            like((tokens, width), BF16),
            like((2, width), F32),
        ],
        scratch=[pltpu.VMEM((tokens, inner), BF16)],
        flops=4 * tokens * width * inner + 10 * tokens * slots * pad * inner,
        name="cross_backward",
    )


def self_backward(
    grad_in, part_a, part_b, text, fwd_a, fwd_b, gain, wo, projected, stats, segments, wq, wk, wv
):
    tokens, width = grad_in.shape
    inner = wq.shape[1]
    rows = tokens

    def body(get, out, put, extra):
        residual = get(3)[...].astype(F32) + (get(4)[...].astype(F32) + get(5)[...].astype(F32))
        unit, inverse = normalise(residual)
        grad = get(0)[...] + (get(1)[...].astype(F32) + get(2)[...].astype(F32))
        out[4][0:1, :], out[4][1:2, :] = norm_sums(grad, unit)
        put(4)
        grad_residual = norm_back(grad, unit, inverse, get(6)[...])
        out[0][...] = grad_residual
        put(0)
        out[1][...] = grad_residual.astype(BF16)
        put(1)
        grad_mixed, grad_keys, grad_values = extra
        grad_mixed[...] = dot_nt(out[1][...], get(7)[...]).astype(BF16)
        grad_keys[...] = jnp.zeros_like(grad_keys)
        grad_values[...] = jnp.zeros_like(grad_values)
        seg_row = get(10)[...]
        seg_col = column(seg_row)
        parts = [half_lanes(0), half_lanes(1)]
        get(8)
        get(9)
        for block in range(tokens // rows):
            first, size = window(block, tokens, rows)
            bias = self_bias(seg_col, seg_row, block, rows, first, size)
            here = slice(block * rows, (block + 1) * rows)
            there = slice(first, first + size)
            for pair in range(inner // LANES):
                cols = slice(pair * LANES, (pair + 1) * LANES)
                totals = [get(9)[here, 2 * pair + part : 2 * pair + part + 1] for part in range(2)]
                grad_q, grad_k, grad_v = attend_back(
                    get(8)[0, here, cols] * SCALE,
                    get(8)[1, there, cols],
                    get(8)[2, there, cols],
                    grad_mixed[here, cols],
                    bias,
                    totals,
                    parts,
                )
                out[2][here, cols] = grad_q.astype(BF16)
                grad_keys[there, cols] += grad_k
                grad_values[there, cols] += grad_v
        out[2][:, inner : 2 * inner] = grad_keys[...].astype(BF16)
        out[2][:, 2 * inner :] = grad_values[...].astype(BF16)
        put(2)
        total = 0.0
        for k in range(3):
            total = total + dot_nt(out[2][:, k * inner : (k + 1) * inner], get(11 + k)[...])
        out[3][...] = total.astype(BF16)
        put(3)

    return run(
        body,
        [
            grad_in, part_a, part_b, text, fwd_a, fwd_b, gain, wo, projected, stats, segments,
            wq, wk, wv,
        ],
        [
            like((tokens, width), F32),
            like((tokens, width), BF16),
            like((tokens, 3 * inner), BF16),
            like((tokens, width), BF16),
            like((2, width), F32),
        ],
        scratch=[
            pltpu.VMEM((tokens, inner), BF16),
            pltpu.VMEM((tokens, inner), F32),
            pltpu.VMEM((tokens, inner), F32),
        ],
        flops=8 * tokens * width * inner + 10 * tokens * 256 * inner,
        name="self_backward",
    )


def patch_backward(grad_keys, grad_values, wk, wv, dims):
    slots, patch_rows, pad = dims
    vis, inner = wk.shape
    width = vis // 2

    def body(get, out, put, extra):
        head = lax.axis_index("head")
        weights = [get(2), get(3)]
        grads = [get(0), get(1)]
        for k in range(2):
            first = pl.multiple_of((head if k == 0 else 1 - head) * width, width)
            left, right = (weights[j][pl.ds(first, width), :] for j in range(2))
            for slot in range(slots):
                rows = slice(slot * pad, (slot + 1) * pad)
                total = dot_nt(grads[0][rows, :], left) + dot_nt(grads[1][rows, :], right)
                out[k][slot_image(slot, slots, head)] = total[:patch_rows].astype(BF16)
            put(k)

    return run(
        body,
        [grad_keys, grad_values, wk, wv],
        [like((slots, patch_rows, width), BF16)] * 2,
        flops=4 * slots * pad * vis * inner,
        name="patch_backward",
    )


def offset_of(position, digits):
    count = len(digits)
    return sum(
        ((position >> (count - 1 - step)) & 1) << digit for step, digit in enumerate(digits)
    )


def weight_grads(inputs, blocks, streams, held, groups, columns, flops, name, chosen=None):
    chosen = streams if chosen is None else chosen
    bottoms = {}
    for k, stream in enumerate(streams):
        bottoms[stream] = sum(other.rows for other in streams[:k])
    outs = []
    for stream in chosen:
        outs += [like((stream.entries // 2 * stream.rows, columns), BF16)] * 2

    def body(get, out, put, scratch):
        me = lax.axis_index("dp") * lax.axis_size("stream") + lax.axis_index("stream")
        first = 0
        for block, (piece, product) in enumerate(blocks):
            whole = scratch[block]
            cuts = []
            for k, stream in enumerate(chosen):
                bottom = bottoms[stream]
                low = max(first, bottom)
                high = min(first + piece, bottom + stream.rows)
                if low < high:
                    cuts.append((k, stream, low, high))
            if cuts:
                product(get, whole)
            for k, stream, low, high in cuts:
                for position in range(stream.entries):
                    side, entry = divmod(position, stream.entries // 2)
                    source = (me ^ offset_of(position, stream.digits)) * piece + (low - first)
                    target = entry * stream.rows + low - bottoms[stream]
                    out[2 * k + side][target : target + high - low, :] = whole[
                        pl.ds(pl.multiple_of(source, 16), high - low), :
                    ]
            first += piece

    results = run(
        body,
        inputs,
        outs,
        scratch=[pltpu.VMEM((groups * piece, columns), BF16) for piece, _ in blocks],
        flops=flops,
        name=name,
    )
    for k, stream in enumerate(chosen):
        held += [results[2 * k], results[2 * k + 1]]
        stream.terms, stream.send = [(len(held) - 2, 0)], len(held) - 1


def product(left, right, first=None, size=None):
    def fill(get, whole):
        columns = get(right)[...] if first is None else get(right)[:, first : first + size]
        whole[...] = dot_tn(get(left)[...], columns).astype(BF16)

    return fill


def finish(streams, held, piece, vis_piece, blocks):
    columns = held[0].shape[1]
    used, places = [], {}
    for batch in streams.values():
        for stream in batch:
            for index, _ in stream.terms:
                if index not in places:
                    places[index] = len(used)
                    used.append(held[index])

    def body(get, out, put, scratch):
        def rows_of(batch, low, high):
            parts, bottom = [], 0
            for stream in batch:
                first, last = max(low, bottom) - bottom, min(high, bottom + stream.rows) - bottom
                if first < last:
                    total = 0.0
                    for index, row in stream.terms:
                        total = total + get(places[index])[row + first : row + last, :].astype(F32)
                    parts.append(total)
                bottom += stream.rows
            return parts[0] if len(parts) == 1 else jnp.concatenate(parts)

        for k in range(2 * blocks):
            out[k // blocks][:, k % blocks * columns : (k % blocks + 1) * columns] = rows_of(
                streams["ff"], k * piece, (k + 1) * piece
            )
        for k in range(2):
            out[2 + k][...] = rows_of(streams["cross"], k * piece, (k + 1) * piece)
            low = 2 * piece + k * vis_piece
            out[4 + k][...] = rows_of(streams["cross"], low, low + vis_piece)
        for k in range(4):
            out[6 + k][...] = rows_of(streams["self"], k * piece, (k + 1) * piece)
        vectors = rows_of(streams["self"], 4 * piece, 4 * piece + 16)
        for k in range(6):
            out[10 + k][...] = vectors[k, :piece]

    return run(
        body,
        used,
        [like((piece, blocks * columns), F32)] * 2
        + [like((piece, columns), F32)] * 2
        + [like((vis_piece, columns), F32)] * 2
        + [like((piece, columns), F32)] * 4
        + [like((piece,), F32)] * 6,
        name="finish",
    )


def project(left, right):
    return jnp.dot(left, right, preferred_element_type=F32)


def head_sum(partial_rows):
    return partial_rows, partner(partial_rows, "head", 0)


def body(
    text,
    patches,
    segment_ids,
    phrase_image,
    wq_self,
    wk_self,
    wv_self,
    wo_self,
    ln1_gain,
    ln1_bias,
    wq_cross,
    wk_cross,
    wv_cross,
    wo_cross,
    ln2_gain,
    ln2_bias,
    w_in,
    w_out,
    ln3_gain,
    ln3_bias,
    cotangent,
):
    slots, patch_rows, vis = patches.shape
    half = slots // 2
    pad = -(-patch_rows // 16) * 16
    dims = (slots, patch_rows, pad)
    tokens, width = text.shape
    inner = wq_self.shape[1]
    hidden_width = w_in.shape[1]
    groups = lax.axis_size("dp") * lax.axis_size("stream")
    head = lax.axis_index("head")
    row = lambda vector: vector.reshape(1, width)

    near = partner(lax.dynamic_slice_in_dim(patches, head * half, half, 0), "stream", 0)
    projected, attended, self_stats, part1 = self_forward(
        text, wq_self, wk_self, wv_self, wo_self, segment_ids, [wk_cross, wv_cross]
    )
    attended, near = lax.optimization_barrier((attended, near))
    other = partner(near, "head", 0)
    part1_a, part1_b = head_sum(part1)
    normed1, normed1_low, cross_queries = cross_queries_of(
        text, part1_a, part1_b, row(ln1_gain), row(ln1_bias), wq_cross
    )
    keys_values = cross_keys(near, 0, wk_cross, wv_cross, ())
    keys_cross, values_cross = cross_keys(other, 1, wk_cross, wv_cross, keys_values)
    cross_attended, cross_stats, part2 = cross_forward(
        cross_queries, keys_cross, values_cross, wo_cross, segment_ids, phrase_image, dims
    )
    part2_a, part2_b = head_sum(part2)
    normed2, normed2_low, hidden, slopes, part3 = feed_forward(
        normed1, part2_a, part2_b, row(ln2_gain), row(ln2_bias), w_in, w_out
    )
    part3_a, part3_b = head_sum(part3)
    grad_residual3, grad_three_low, grad_pre, part4, norm3 = feed_backward(
        normed2, part3_a, part3_b, row(ln3_gain), cotangent, w_out, slopes, w_in
    )
    part4_a, part4_b = head_sum(part4)
    piece = width // groups
    fast = groups == 2**LINKS and piece % 16 == 0 and vis % (16 * groups) == 0
    order = Order()
    held, streams = Held(), {}
    if fast:
        streams = {name: [Stream(*stream) for stream in plan] for name, plan in PLAN.items()}
        everything = [stream for batch in streams.values() for stream in batch]
        blocks = hidden_width // inner
        links = {}
        for stream in streams["ff"]:
            links.setdefault(stream.steps[0], []).append(stream)
        for chosen in sorted(links.values(), key=lambda batch: -sum(part.rows for part in batch)):
            weight_grads(
                [order.after(grad_three_low), hidden, normed2_low, grad_pre],
                [(piece, product(0, 1, k * inner, inner)) for k in range(blocks)]
                + [(piece, product(2, 3, k * inner, inner)) for k in range(blocks)],
                streams["ff"],
                held,
                groups,
                inner,
                0,
                "ff_weight_grads",
                chosen,
            )
            away, _ = merge(chosen, 0, held, name="merge_0")
            order.passed(away)
    grad_residual2, grad_two_low, grad_cross_queries, grad_keys, grad_values, part5, norm2 = (
        cross_backward(
            order.after(grad_residual3), part4_a, part4_b, normed1, part2_a, part2_b,
            row(ln2_gain), wo_cross, cross_queries, keys_cross, values_cross, cross_stats,
            segment_ids, phrase_image, wq_cross, dims,
        )
    )
    part5_a, part5_b = head_sum(part5)
    if fast:
        def kv(which):
            def fill(get, whole):
                total = 0.0
                for slot in range(slots):
                    rows_in = get(4 + slot % 2)[slot // 2]
                    grads = get(6 + which)[slot * pad : slot * pad + patch_rows, :]
                    total = total + dot_tn(rows_in, grads)
                whole[...] = total.astype(BF16)

            return fill

        weight_grads(
            [grad_two_low, cross_attended, normed1_low, grad_cross_queries, near,
             other, grad_keys, grad_values],
            [
                (piece, product(0, 1)),
                (piece, product(2, 3)),
                (vis // groups, kv(0)),
                (vis // groups, kv(1)),
            ],
            streams["cross"],
            held,
            groups,
            inner,
            4 * tokens * width * inner + 4 * slots * pad * vis * inner,
            "cross_weight_grads",
        )
        late, _ = lax.optimization_barrier((normed2, held[-1]))
        output = last_norm(late, part3_a, part3_b, row(ln3_gain), row(ln3_bias))
        early = held.recent[0]
        held[early], output = lax.optimization_barrier((held[early], output))
        away, _ = merge(streams["ff"] + streams["cross"], 1, held, name="merge_1")
        order.passed(away)
    grad_residual1, grad_one_low, grad_qkv, part6, norm1 = self_backward(
        order.after(grad_residual2), part5_a, part5_b, text, part1_a, part1_b, row(ln1_gain),
        wo_self, projected, self_stats, segment_ids, wq_self, wk_self, wv_self,
    )
    part6_a, part6_b = head_sum(part6)
    grad_keys, _ = lax.optimization_barrier((grad_keys, grad_qkv))
    patch_own, patch_away = patch_backward(grad_keys, grad_values, wk_cross, wv_cross, dims)
    patch_other = partner(patch_away, "head", 0)
    add_patches = (
        [patch_own, patch_other],
        [like(patch_own.shape, BF16)],
        lambda get, out: out[0].__setitem__(
            ..., (get(0)[...].astype(F32) + get(1)[...].astype(F32)).astype(BF16)
        ),
    )
    grad_text = grad_residual1 + (part6_a.astype(F32) + part6_b.astype(F32))
    if fast:
        def norms(get, whole):
            rows = jnp.concatenate([get(k)[...] for k in (4, 5, 6)] + [jnp.zeros((2, width), F32)])
            inside = lax.broadcasted_iota(jnp.int32, (8, inner), 1) < piece
            for group in range(groups):
                turned = pltpu.roll(rows, (width - group * piece) % width, 1)[:, :inner]
                entry = jnp.concatenate([jnp.where(inside, turned, 0.0), jnp.zeros((8, inner), F32)])
                whole[group * 16 : (group + 1) * 16, :] = entry.astype(BF16)

        weight_grads(
            [grad_one_low, attended, text, grad_qkv, norm1, norm2, norm3],
            [(piece, product(2, 3, k * inner, inner)) for k in range(3)]
            + [(piece, product(0, 1)), (16, norms)],
            streams["self"],
            held,
            groups,
            inner,
            8 * tokens * width * inner,
            "self_weight_grads",
        )
        grad_patches = None
        early = held.recent[0]
        held[early], patch_own, _ = lax.optimization_barrier((held[early], patch_own, held[-1]))
        for phase in range(2, PHASES):
            work = add_patches if phase == PATCH_PHASE else ((), (), None)
            if phase == PATCH_PHASE + 1:
                held[-1], grad_patches = lax.optimization_barrier((held[-1], grad_patches))
            away, more = merge(everything, phase, held, *work, name="merge_%d" % phase)
            if phase == PATCH_PHASE:
                grad_patches = partner(more[0], "stream", 0)
        grad_patches = grad_patches.astype(F32)
        shares = finish(streams, held, piece, vis // groups, blocks)
        own_w_out, own_w_in, cross_wo, cross_wq, cross_wk, cross_wv = shares[:6]
        self_wq, self_wk, self_wv, self_wo = shares[6:10]
        own_w_out, cross_wo, self_wo = own_w_out.T, cross_wo.T, self_wo.T
        own_norms = shares[10:]
    else:
        patch_sum = (patch_own.astype(F32) + patch_other.astype(F32)).astype(BF16)
        grad_patches = partner(patch_sum, "stream", 0).astype(F32)
        norm_grads = jnp.concatenate([norm1, norm2, norm3, jnp.zeros((2, width), F32)])

        output = last_norm(normed2, part3_a, part3_b, row(ln3_gain), row(ln3_bias))

        def plain(left, right):
            grad = jnp.einsum("ta,tb->ab", left, right, preferred_element_type=F32)
            grad = grad.astype(BF16).reshape(groups, grad.shape[0] // groups, grad.shape[1])
            return scatter_sum_plain(grad)

        own_w_out = plain(grad_three_low, hidden).T
        own_w_in = plain(normed2_low, grad_pre)
        cross_wo = plain(grad_two_low, cross_attended).T
        cross_wq = plain(normed1_low, grad_cross_queries)
        far = jnp.stack([near, other], axis=1).reshape(slots, patch_rows, vis)
        far = jnp.pad(far, ((0, 0), (0, pad - patch_rows), (0, 0))).reshape(slots * pad, vis)
        cross_wk, cross_wv = plain(far, grad_keys), plain(far, grad_values)
        self_wq, self_wk, self_wv = jnp.split(plain(text, grad_qkv), 3, axis=1)
        self_wo = plain(grad_one_low, attended).T
        own_norms = scatter_sum_plain(
            norm_grads.reshape(8, groups, width // groups).swapaxes(0, 1).astype(BF16)
        )
    return (
        output,
        grad_text,
        grad_patches,
        self_wq,
        self_wk,
        self_wv,
        self_wo,
        own_norms[0],
        own_norms[1],
        cross_wq,
        cross_wk,
        cross_wv,
        cross_wo,
        own_norms[2],
        own_norms[3],
        own_w_in,
        own_w_out,
        own_norms[4],
        own_norms[5],
    )


def solution(mesh):
    in_specs = (
        P(("dp", "stream"), None),
        P(("dp", "stream"), None, None),
        P(("dp", "stream"), None),
        P(("dp", "stream"), None),
        P(None, "head"),
        P(None, "head"),
        P(None, "head"),
        P("head", None),
        P(),
        P(),
        P(None, "head"),
        P(None, "head"),
        P(None, "head"),
        P("head", None),
        P(),
        P(),
        P(None, "head"),
        P("head", None),
        P(),
        P(),
        P(("dp", "stream"), None),
    )
    out_specs = (
        P(("dp", "stream"), None),
        P(("dp", "stream"), None),
        P(("dp", "stream"), None, "head"),
        P(("dp", "stream"), "head"),
        P(("dp", "stream"), "head"),
        P(("dp", "stream"), "head"),
        P("head", ("dp", "stream")),
        P(("dp", "stream")),
        P(("dp", "stream")),
        P(("dp", "stream"), "head"),
        P(("dp", "stream"), "head"),
        P(("dp", "stream"), "head"),
        P("head", ("dp", "stream")),
        P(("dp", "stream")),
        P(("dp", "stream")),
        P(("dp", "stream"), "head"),
        P("head", ("dp", "stream")),
        P(("dp", "stream")),
        P(("dp", "stream")),
    )
    return jax.shard_map(body, mesh=mesh, in_specs=in_specs, out_specs=out_specs, check_vma=False)
```

```python
import jax
import jax.numpy as jnp
from jax import lax
from jax.experimental import pallas as pl
from jax.experimental.pallas import tpu as pltpu
from jax.sharding import PartitionSpec as P

HEAD_DIM = 64
LANES = 128
MAX_PHRASE = 48
EPSILON = 1e-12
NEGATIVE = -1e30
SCALE = HEAD_DIM ** (-0.5)
VMEM_LIMIT = 56 * 1024 * 1024
F32 = jnp.float32
BF16 = jnp.bfloat16


COSTS = {
    "self_forward": 0.8,
    "cross_queries": 0.1,
    "cross_keys": 0.3,
    "cross_forward": 6.2,
    "feed_forward": 3.3,
    "feed_backward": 3.3,
    "ff_weight_grads": 1.1,
    "cross_backward": 0.1,
    "cross_weight_grads": 3.3,
    "self_backward": 0.1,
    "self_weight_grads": 0.1,
    "patch_backward": 0.1,
}


def partner(value, axis, place):
    mask = 2**place
    pairs = [(source, source ^ mask) for source in range(lax.axis_size(axis))]
    return lax.ppermute(value, axis, pairs)


def group_bits():
    count = lax.axis_size("dp").bit_length() - 1
    return [("stream", 0)] + [("dp", place) for place in range(count)]


class Order:
    def __init__(self):
        self.last = None

    def after(self, value):
        if self.last is not None:
            value, _ = lax.optimization_barrier((value, self.last))
        return value

    def passed(self, value):
        self.last = value
        return value


LINKS = 4

PLAN = {
    "ff": ((48, ((0, 0), (1, 2), (2, 1), (3, 3))), (96, ((0, 0), (1, 2), (2, 3), (4, 1))), (128, ((0, 1), (1, 0), (2, 3), (4, 2))), (112, ((0, 2), (1, 3), (3, 1), (5, 0)))),
    "cross": ((48, ((1, 0), (2, 1), (3, 2), (4, 3))), (32, ((1, 0), (2, 2), (3, 3), (4, 1))), (96, ((1, 1), (2, 2), (3, 0), (4, 3))), (48, ((1, 1), (2, 0), (3, 3), (5, 2)))),
    "self": ((80, ((2, 0), (3, 1), (4, 3), (5, 2))), (32, ((2, 0), (3, 2), (4, 1), (5, 3))), (96, ((2, 1), (3, 0), (4, 2), (5, 3)))),
}
PHASES = 6
PATCH_PHASE = 4


class Stream:
    def __init__(self, rows, steps):
        self.rows, self.steps = rows, dict(steps)
        self.digits = [digit for _, digit in steps]
        self.entries = 2 ** len(steps)
        self.terms, self.send, self.sent = [], None, None


class Held(list):
    recent = ()
    phase = None


def gather_messages(streams, phase):
    messages = {}
    for stream in streams:
        if phase in stream.steps:
            pieces = messages.setdefault(stream.steps[phase], [])
            first = sum(rows for _, _, rows in pieces)
            pieces.append((stream, first, stream.entries // 2 * stream.rows))
    return messages


def start_messages(messages, arrays, held, phase):
    if held.phase != phase:
        held.phase, held.recent = phase, []
    for (digit, pieces), away in zip(sorted(messages.items()), arrays):
        axis, place = group_bits()[digit]
        held.recent.append(len(held))
        held.append(partner(away, axis, place))
        for stream, first, _ in pieces:
            stream.terms.append((len(held) - 1, first))
            stream.entries //= 2


def merge(streams, phase, held, extra_inputs=(), extra_outs=(), extra=None, name=None):
    messages = gather_messages(streams, phase)
    before = None
    for k in held.recent if held.phase != phase else ():
        if before is not None:
            held[k], _ = lax.optimization_barrier((held[k], held[before]))
        before = k
    if before is not None:
        for k, value in zip(
            held.recent, lax.optimization_barrier(tuple(held[k] for k in held.recent))
        ):
            held[k] = value
    used, places = [], {}

    def place(index):
        if index not in places:
            places[index] = len(used)
            used.append(held[index])
        return places[index]

    columns = held[0].shape[1]
    jobs, outs, aways = [], [], []
    for _, pieces in sorted(messages.items()):
        sources = {piece[0].send for piece in pieces}
        if len(sources) == 1 and None not in sources:
            aways.append(held[sources.pop()])
            for piece in pieces:
                piece[0].send = None
            continue
        aways.append(len(outs))
        for stream, first, rows in pieces:
            if stream.send is not None:
                sources = [(place(stream.send), 0)]
                stream.send = None
            else:
                sources = [(place(index), row + rows) for index, row in stream.terms]
            jobs.append((len(outs), first, rows, sources))
        outs.append(like((sum(rows for _, _, rows in pieces), columns), BF16))
    count = len(used)

    def body(get, out, put, scratch):
        for slot, first, rows, sources in jobs:
            parts = [get(k)[row : row + rows, :] for k, row in sources]
            if len(parts) > 1:
                total = parts[0].astype(F32)
                for part in parts[1:]:
                    total = total + part.astype(F32)
                parts = [total.astype(BF16)]
            out[slot][first : first + rows, :] = parts[0]
        if extra is not None:
            extra(lambda k: get(count + k), out[len(outs) :])

    results = []
    if outs or extra_outs:
        results = run(body, used + list(extra_inputs), outs + list(extra_outs), name=name)
    aways = [results[away] if isinstance(away, int) else away for away in aways]
    start_messages(messages, aways, held, phase)
    return aways, results[len(outs) :]


def scatter_sum_plain(grads):
    bits = group_bits()
    count = len(bits)
    grads = grads.reshape((2,) * count + grads.shape[1:])
    for step in range(count):
        axis, place = bits[step]
        dim = count - 1 - step
        mine = (lax.axis_index(axis) >> place) & 1
        away = lax.dynamic_index_in_dim(grads, 1 - mine, dim, keepdims=True)
        keep = lax.dynamic_index_in_dim(grads, mine, dim, keepdims=True)
        grads = keep.astype(F32) + partner(away, axis, place).astype(F32)
        if step < count - 1:
            grads = grads.astype(BF16)
    return grads.reshape(grads.shape[count:])


def run(body, inputs, outs, scratch=(), flops=0, aliases=None, name=None):
    n_in, n_out = len(inputs), len(outs)

    def kernel(*refs):
        ins, refs = refs[:n_in], refs[n_in:]
        body(lambda k: ins[k], refs[:n_out], lambda k: None, refs[n_out:])

    moved = sum(a.size * a.dtype.itemsize for a in inputs) + sum(
        a.size * a.dtype.itemsize for a in outs
    )
    return pl.pallas_call(
        kernel,
        name=name,
        out_shape=[jax.ShapeDtypeStruct(a.shape, a.dtype) for a in outs],
        in_specs=[pl.BlockSpec(memory_space=pltpu.VMEM)] * n_in,
        out_specs=[pl.BlockSpec(memory_space=pltpu.VMEM)] * n_out,
        scratch_shapes=list(scratch),
        input_output_aliases=aliases or {},
        compiler_params=pltpu.CompilerParams(vmem_limit_bytes=int(moved + 8 * 2**20 + sum(2 * 384 * 384 for _ in scratch))),
        cost_estimate=pl.CostEstimate(
            flops=int(1e9 * COSTS.get(name, 0.6)), bytes_accessed=1000, transcendentals=0
        ),
    )(*inputs)


def like(shape, dtype):
    return jax.ShapeDtypeStruct(shape, dtype)


def dot(left, right):
    return lax.dot_general(left, right, (((1,), (0,)), ((), ())), preferred_element_type=F32)


def dot_nt(left, right):
    return lax.dot_general(left, right, (((1,), (1,)), ((), ())), preferred_element_type=F32)


def dot_tn(left, right):
    return lax.dot_general(left, right, (((0,), (0,)), ((), ())), preferred_element_type=F32)


def normalise(rows):
    center = rows - jnp.mean(rows, axis=-1, keepdims=True)
    inverse = lax.rsqrt(jnp.mean(center * center, axis=-1, keepdims=True) + EPSILON)
    return center * inverse, inverse


def norm_back(grad, unit, inverse, gain):
    inner = grad * gain
    shift = jnp.mean(inner, axis=-1, keepdims=True)
    slope = jnp.mean(inner * unit, axis=-1, keepdims=True)
    return inverse * (inner - shift - unit * slope)


def norm_sums(grad, unit):
    return jnp.sum(grad * unit, axis=0, keepdims=True), jnp.sum(grad, axis=0, keepdims=True)


def column(row):
    wide = jnp.broadcast_to(row.astype(F32), (LANES, row.shape[1]))
    return jnp.transpose(wide)[:, :1].astype(jnp.int32)


def half_lanes(part):
    lane = lax.broadcasted_iota(jnp.int32, (1, LANES), 1)
    return (lane >= HEAD_DIM) if part else (lane < HEAD_DIM)


def window(block, tokens, rows):
    size = min(tokens, rows + 128)
    return min(max(block * rows - 64, 0), tokens - size), size


def self_bias(seg_col, seg_row, block, rows, first, size):
    same = seg_col[block * rows : (block + 1) * rows] == seg_row[:, first : first + size]
    return jnp.where(same, 0.0, NEGATIVE)


def cross_bias(seg_col, images_row, head, slots, patch_rows, patch_pad):
    phrases = images_row.shape[1]
    phrase = lax.broadcasted_iota(jnp.int32, (1, phrases), 1)
    image = jnp.sum(jnp.where(seg_col == phrase, images_row, 0), axis=1, keepdims=True)
    place = lax.broadcasted_iota(jnp.int32, (1, slots * patch_pad), 1)
    key_image = jnp.full((1, slots * patch_pad), -1, jnp.int32)
    for slot in range(slots):
        inside = (place >= slot * patch_pad) & (place < slot * patch_pad + patch_rows)
        key_image = jnp.where(inside, slot_image(slot, slots, head), key_image)
    return jnp.where(image == key_image, 0.0, NEGATIVE)


def slot_image(slot, slots, head):
    half = slots // 2
    return half * (head if slot % 2 == 0 else 1 - head) + slot // 2


def attend(queries, keys, values, bias, parts):
    mixed, totals = 0.0, []
    for part in range(2):
        scores = dot_nt(jnp.where(parts[part], queries, 0), keys) + bias
        largest = jnp.max(scores, axis=1, keepdims=True)
        exponent = jnp.exp(scores - largest)
        total = jnp.sum(exponent, axis=1, keepdims=True)
        picked = dot(exponent.astype(BF16), values) * (1.0 / total)
        mixed = picked if part == 0 else jnp.where(parts[1], picked, mixed)
        totals.append(largest + jnp.log(total))
    return mixed, totals


def attend_back(queries, keys, values, grad, bias, totals, parts):
    both = []
    for part in range(2):
        query = jnp.where(parts[part], queries, 0)
        grad_part = jnp.where(parts[part], grad, 0)
        probs = jnp.exp(dot_nt(query, keys) + bias - totals[part])
        grad_probs = dot_nt(grad_part, values)
        inner = jnp.sum(probs * grad_probs, axis=1, keepdims=True)
        grad_scores = (probs * (grad_probs - inner)).astype(BF16)
        both.append((query, grad_part, probs.astype(BF16), grad_scores))
    query, grad_part, probs, grad_scores = [
        jnp.concatenate([both[0][k], both[1][k]], axis=0) for k in range(4)
    ]
    keys = jnp.concatenate([jnp.where(parts[part], keys, 0) for part in range(2)], axis=0)
    grad_q = dot(jnp.concatenate([both[0][3], both[1][3]], axis=1), keys)
    return grad_q * SCALE, dot_tn(grad_scores, query), dot_tn(probs, grad_part)


def self_forward(text, wq, wk, wv, wo, segments, early):
    tokens, width = text.shape
    inner = wq.shape[1]
    rows = 128

    def body(get, out, put, extra):
        text_in = get(0)[...]
        projected = [dot(text_in, get(1 + k)[...]).astype(BF16) for k in range(3)]
        for k in range(3):
            out[0][k] = projected[k]
        put(0)
        seg_row = get(5)[...]
        seg_col = column(seg_row)
        parts = [half_lanes(0), half_lanes(1)]
        lane = lax.broadcasted_iota(jnp.int32, (1, LANES), 1)
        for block in range(tokens // rows):
            first, size = window(block, tokens, rows)
            bias = self_bias(seg_col, seg_row, block, rows, first, size)
            here = slice(block * rows, (block + 1) * rows)
            stats = jnp.zeros((rows, LANES), F32)
            for pair in range(inner // LANES):
                cols = slice(pair * LANES, (pair + 1) * LANES)
                mixed, totals = attend(
                    out[0][0, here, cols] * SCALE,
                    out[0][1, first : first + size, cols],
                    out[0][2, first : first + size, cols],
                    bias,
                    parts,
                )
                out[1][here, cols] = mixed.astype(BF16)
                for part in range(2):
                    stats = jnp.where(lane == 2 * pair + part, totals[part], stats)
            out[2][here, :] = stats
        put(1)
        put(2)
        out[3][...] = dot(out[1][...], get(4)[...]).astype(BF16)
        put(3)

    return run(
        body,
        [text, wq, wk, wv, wo, segments] + early,
        [
            like((3, tokens, inner), BF16),
            like((tokens, inner), BF16),
            like((tokens, LANES), F32),
            like((tokens, width), BF16),
        ],
        flops=2 * tokens * width * inner * 4 + 8 * tokens * 256 * inner,
        name="self_forward",
    )


def cross_keys(some, first, wk, wv, before):
    half, patch_rows, vis = some.shape
    slots = 2 * half
    pad = -(-patch_rows // 16) * 16
    inner = wk.shape[1]

    def body(get, out, put, extra):
        weights = [get(1), get(2)]
        for k in range(2):
            for slot in range(first, slots, 2):
                top, end = slot * pad, (slot + 1) * pad
                out[k][end - 16 : end, :] = jnp.zeros((16, inner), BF16)
                out[k][top : top + patch_rows, :] = dot(
                    get(0)[slot // 2], weights[k][...]
                ).astype(BF16)

    return run(
        body,
        [some, wk, wv] + list(before),
        [like((slots * pad, inner), BF16)] * 2,
        aliases={3 + k: k for k in range(len(before))},
        name="cross_keys",
    )


def cross_queries_of(text, part_a, part_b, gain, bias, wq):
    tokens, width = text.shape

    def body(get, out, put, extra):
        residual = get(0)[...].astype(F32) + (get(1)[...].astype(F32) + get(2)[...].astype(F32))
        unit, _ = normalise(residual)
        normed = unit * get(3)[...] + get(4)[...]
        out[0][...] = normed
        low = normed.astype(BF16)
        out[1][...] = low
        out[2][...] = dot(low, get(5)[...]).astype(BF16)

    return run(
        body,
        [text, part_a, part_b, gain, bias, wq],
        [
            like((tokens, width), F32),
            like((tokens, width), BF16),
            like((tokens, wq.shape[1]), BF16),
        ],
        flops=2 * tokens * width * wq.shape[1],
        name="cross_queries",
    )


def cross_forward(queries, keys, values, wo, segments, images, dims):
    tokens, inner = queries.shape
    width = wo.shape[1]
    slots, patch_rows, pad = dims
    rows = tokens

    def body(get, out, put, extra):
        head = lax.axis_index("head")
        mask = cross_bias(column(get(4)[...]), get(5)[...], head, slots, patch_rows, pad)
        parts = [half_lanes(0), half_lanes(1)]
        lane = lax.broadcasted_iota(jnp.int32, (1, LANES), 1)
        for block in range(tokens // rows):
            here = slice(block * rows, (block + 1) * rows)
            stats = jnp.zeros((rows, LANES), F32)
            for pair in range(inner // LANES):
                cols = slice(pair * LANES, (pair + 1) * LANES)
                mixed, totals = attend(
                    get(0)[here, cols] * SCALE,
                    get(1)[:, cols],
                    get(2)[:, cols],
                    mask[here],
                    parts,
                )
                out[0][here, cols] = mixed.astype(BF16)
                for part in range(2):
                    stats = jnp.where(lane == 2 * pair + part, totals[part], stats)
            out[1][here, :] = stats
        out[2][...] = dot(out[0][...], get(3)[...]).astype(BF16)

    return run(
        body,
        [queries, keys, values, wo, segments, images],
        [
            like((tokens, inner), BF16),
            like((tokens, LANES), F32),
            like((tokens, width), BF16),
        ],
        flops=2 * tokens * width * inner + 4 * tokens * slots * pad * inner,
        name="cross_forward",
    )


def feed_forward(normed, part_a, part_b, gain, bias, w_in, w_out):
    tokens, width = normed.shape
    inner = w_in.shape[1]
    chunk = 256

    def body(get, out, put, extra):
        residual = get(0)[...] + (get(1)[...].astype(F32) + get(2)[...].astype(F32))
        unit, _ = normalise(residual)
        normed_two = unit * get(3)[...] + get(4)[...]
        out[0][...] = normed_two
        put(0)
        out[1][...] = normed_two.astype(BF16)
        put(1)
        get(5)
        for start in range(0, inner, chunk):
            cols = slice(start, start + chunk)
            pre = dot(out[1][...], get(5)[:, cols])
            phi = 0.5 * (1.0 + lax.erf(pre * (0.5**0.5)))
            bell = jnp.exp(pre * pre * -0.5) * 0.3989422804014327
            out[2][:, cols] = (pre * phi).astype(BF16)
            out[3][:, cols] = (phi + pre * bell).astype(BF16)
        put(2)
        put(3)
        out[4][...] = dot(out[2][...], get(6)[...]).astype(BF16)
        put(4)

    return run(
        body,
        [normed, part_a, part_b, gain, bias, w_in, w_out],
        [
            like((tokens, width), F32),
            like((tokens, width), BF16),
            like((tokens, inner), BF16),
            like((tokens, inner), BF16),
            like((tokens, width), BF16),
        ],
        flops=4 * tokens * width * inner,
        name="feed_forward",
    )


def last_norm(normed, part_a, part_b, gain, bias):
    def body(get, out, put, extra):
        residual = get(0)[...] + (get(1)[...].astype(F32) + get(2)[...].astype(F32))
        out[0][...] = normalise(residual)[0] * get(3)[...] + get(4)[...]

    return run(
        body,
        [normed, part_a, part_b, gain, bias],
        [like(normed.shape, F32)],
        name="last_norm",
    )[0]


def feed_backward(normed, part_a, part_b, gain, cotangent, w_out, slopes, w_in):
    tokens, width = normed.shape
    inner = w_in.shape[1]
    chunk = 256

    def body(get, out, put, extra):
        residual = get(0)[...] + (get(1)[...].astype(F32) + get(2)[...].astype(F32))
        unit, inverse = normalise(residual)
        grad = get(4)[...]
        out[4][0:1, :], out[4][1:2, :] = norm_sums(grad, unit)
        grad_residual = norm_back(grad, unit, inverse, get(3)[...])
        out[0][...] = grad_residual
        out[1][...] = grad_residual.astype(BF16)
        for start in range(0, inner, chunk):
            cols = slice(start, start + chunk)
            grad_hidden = dot_nt(out[1][...], get(5)[cols, :])
            out[2][:, cols] = (grad_hidden * get(6)[:, cols].astype(F32)).astype(BF16)
        out[3][...] = dot_nt(out[2][...], get(7)[...]).astype(BF16)

    return run(
        body,
        [normed, part_a, part_b, gain, cotangent, w_out, slopes, w_in],
        [
            like((tokens, width), F32),
            like((tokens, width), BF16),
            like((tokens, inner), BF16),
            like((tokens, width), BF16),
            like((2, width), F32),
        ],
        flops=4 * tokens * width * inner,
        name="feed_backward",
    )


def cross_backward(
    grad_in, part_a, part_b, normed, fwd_a, fwd_b, gain, wo, queries, keys, values, stats,
    segments, images, wq, dims,
):
    tokens, width = grad_in.shape
    inner = queries.shape[1]
    slots, patch_rows, pad = dims
    rows = tokens

    def body(get, out, put, extra):
        residual = get(3)[...] + (get(4)[...].astype(F32) + get(5)[...].astype(F32))
        unit, inverse = normalise(residual)
        grad = get(0)[...] + (get(1)[...].astype(F32) + get(2)[...].astype(F32))
        out[6][0:1, :], out[6][1:2, :] = norm_sums(grad, unit)
        put(6)
        grad_residual = norm_back(grad, unit, inverse, get(6)[...])
        out[0][...] = grad_residual
        put(0)
        out[1][...] = grad_residual.astype(BF16)
        put(1)
        grad_mixed = extra[0]
        grad_mixed[...] = dot_nt(out[1][...], get(7)[...]).astype(BF16)
        head = lax.axis_index("head")
        mask = cross_bias(column(get(12)[...]), get(13)[...], head, slots, patch_rows, pad)
        parts = [half_lanes(0), half_lanes(1)]
        for k in range(8, 12):
            get(k)
        for pair in range(inner // LANES):
            cols = slice(pair * LANES, (pair + 1) * LANES)
            grad_k, grad_v = 0.0, 0.0
            for block in range(tokens // rows):
                here = slice(block * rows, (block + 1) * rows)
                totals = [get(11)[here, 2 * pair + part : 2 * pair + part + 1] for part in range(2)]
                grad_q, more_k, more_v = attend_back(
                    get(8)[here, cols] * SCALE,
                    get(9)[:, cols],
                    get(10)[:, cols],
                    grad_mixed[here, cols],
                    mask[here],
                    totals,
                    parts,
                )
                out[2][here, cols] = grad_q.astype(BF16)
                grad_k, grad_v = grad_k + more_k, grad_v + more_v
            out[3][:, cols] = grad_k.astype(BF16)
            out[4][:, cols] = grad_v.astype(BF16)
        put(2)
        put(3)
        put(4)
        out[5][...] = dot_nt(out[2][...], get(14)[...]).astype(BF16)
        put(5)

    return run(
        body,
        [
            grad_in, part_a, part_b, normed, fwd_a, fwd_b, gain, wo, queries, keys, values, stats,
            segments, images, wq,
        ],
        [
            like((tokens, width), F32),
            like((tokens, width), BF16),
            like((tokens, inner), BF16),
            like((slots * pad, inner), BF16),
            like((slots * pad, inner), BF16),
            like((tokens, width), BF16),
            like((2, width), F32),
        ],
        scratch=[pltpu.VMEM((tokens, inner), BF16)],
        flops=4 * tokens * width * inner + 10 * tokens * slots * pad * inner,
        name="cross_backward",
    )


def self_backward(
    grad_in, part_a, part_b, text, fwd_a, fwd_b, gain, wo, projected, stats, segments, wq, wk, wv
):
    tokens, width = grad_in.shape
    inner = wq.shape[1]
    rows = tokens

    def body(get, out, put, extra):
        residual = get(3)[...].astype(F32) + (get(4)[...].astype(F32) + get(5)[...].astype(F32))
        unit, inverse = normalise(residual)
        grad = get(0)[...] + (get(1)[...].astype(F32) + get(2)[...].astype(F32))
        out[4][0:1, :], out[4][1:2, :] = norm_sums(grad, unit)
        put(4)
        grad_residual = norm_back(grad, unit, inverse, get(6)[...])
        out[0][...] = grad_residual
        put(0)
        out[1][...] = grad_residual.astype(BF16)
        put(1)
        grad_mixed, grad_keys, grad_values = extra
        grad_mixed[...] = dot_nt(out[1][...], get(7)[...]).astype(BF16)
        grad_keys[...] = jnp.zeros_like(grad_keys)
        grad_values[...] = jnp.zeros_like(grad_values)
        seg_row = get(10)[...]
        seg_col = column(seg_row)
        parts = [half_lanes(0), half_lanes(1)]
        get(8)
        get(9)
        for block in range(tokens // rows):
            first, size = window(block, tokens, rows)
            bias = self_bias(seg_col, seg_row, block, rows, first, size)
            here = slice(block * rows, (block + 1) * rows)
            there = slice(first, first + size)
            for pair in range(inner // LANES):
                cols = slice(pair * LANES, (pair + 1) * LANES)
                totals = [get(9)[here, 2 * pair + part : 2 * pair + part + 1] for part in range(2)]
                grad_q, grad_k, grad_v = attend_back(
                    get(8)[0, here, cols] * SCALE,
                    get(8)[1, there, cols],
                    get(8)[2, there, cols],
                    grad_mixed[here, cols],
                    bias,
                    totals,
                    parts,
                )
                out[2][here, cols] = grad_q.astype(BF16)
                grad_keys[there, cols] += grad_k
                grad_values[there, cols] += grad_v
        out[2][:, inner : 2 * inner] = grad_keys[...].astype(BF16)
        out[2][:, 2 * inner :] = grad_values[...].astype(BF16)
        put(2)
        total = 0.0
        for k in range(3):
            total = total + dot_nt(out[2][:, k * inner : (k + 1) * inner], get(11 + k)[...])
        out[3][...] = total.astype(BF16)
        put(3)

    return run(
        body,
        [
            grad_in, part_a, part_b, text, fwd_a, fwd_b, gain, wo, projected, stats, segments,
            wq, wk, wv,
        ],
        [
            like((tokens, width), F32),
            like((tokens, width), BF16),
            like((tokens, 3 * inner), BF16),
            like((tokens, width), BF16),
            like((2, width), F32),
        ],
        scratch=[
            pltpu.VMEM((tokens, inner), BF16),
            pltpu.VMEM((tokens, inner), F32),
            pltpu.VMEM((tokens, inner), F32),
        ],
        flops=8 * tokens * width * inner + 10 * tokens * 256 * inner,
        name="self_backward",
    )


def patch_backward(grad_keys, grad_values, wk, wv, dims):
    slots, patch_rows, pad = dims
    vis, inner = wk.shape
    width = vis // 2

    def body(get, out, put, extra):
        head = lax.axis_index("head")
        weights = [get(2), get(3)]
        grads = [get(0), get(1)]
        for k in range(2):
            first = pl.multiple_of((head if k == 0 else 1 - head) * width, width)
            left, right = (weights[j][pl.ds(first, width), :] for j in range(2))
            for slot in range(slots):
                rows = slice(slot * pad, (slot + 1) * pad)
                total = dot_nt(grads[0][rows, :], left) + dot_nt(grads[1][rows, :], right)
                out[k][slot_image(slot, slots, head)] = total[:patch_rows].astype(BF16)
            put(k)

    return run(
        body,
        [grad_keys, grad_values, wk, wv],
        [like((slots, patch_rows, width), BF16)] * 2,
        flops=4 * slots * pad * vis * inner,
        name="patch_backward",
    )


def offset_of(position, digits):
    count = len(digits)
    return sum(
        ((position >> (count - 1 - step)) & 1) << digit for step, digit in enumerate(digits)
    )


def weight_grads(inputs, blocks, streams, held, groups, columns, flops, name, chosen=None):
    joint = chosen is not None
    chosen = streams if chosen is None else chosen
    bottoms = {}
    for k, stream in enumerate(streams):
        bottoms[stream] = sum(other.rows for other in streams[:k])
    outs, sends, total = [], [], 0
    for stream in chosen:
        rows = stream.entries // 2 * stream.rows
        outs.append(like((rows, columns), BF16))
        sends.append((len(chosen), total) if joint else (len(chosen) + len(sends), 0))
        total += rows
    if joint:
        outs.append(like((total, columns), BF16))
    else:
        outs += outs

    def body(get, out, put, scratch):
        me = lax.axis_index("dp") * lax.axis_size("stream") + lax.axis_index("stream")
        first = 0
        for block, (piece, product) in enumerate(blocks):
            whole = scratch[block]
            cuts = []
            for k, stream in enumerate(chosen):
                bottom = bottoms[stream]
                low = max(first, bottom)
                high = min(first + piece, bottom + stream.rows)
                if low < high:
                    cuts.append((k, stream, low, high))
            if cuts:
                product(get, whole)
            for k, stream, low, high in cuts:
                for position in range(stream.entries):
                    side, entry = divmod(position, stream.entries // 2)
                    source = (me ^ offset_of(position, stream.digits)) * piece + (low - first)
                    target = entry * stream.rows + low - bottoms[stream]
                    place, shift = sends[k] if side else (k, 0)
                    target += shift
                    out[place][target : target + high - low, :] = whole[
                        pl.ds(pl.multiple_of(source, 16), high - low), :
                    ]
            first += piece

    results = run(
        body,
        inputs,
        outs,
        scratch=[pltpu.VMEM((groups * piece, columns), BF16) for piece, _ in blocks],
        flops=flops,
        name=name,
    )
    base = len(held)
    held += results
    for k, stream in enumerate(chosen):
        stream.terms, stream.send = [(base + k, 0)], base + sends[k][0]


def product(left, right, first=None, size=None):
    def fill(get, whole):
        columns = get(right)[...] if first is None else get(right)[:, first : first + size]
        whole[...] = dot_tn(get(left)[...], columns).astype(BF16)

    return fill


def finish(streams, held, piece, vis_piece, blocks):
    columns = held[0].shape[1]
    used, places = [], {}
    for batch in streams.values():
        for stream in batch:
            for index, _ in stream.terms:
                if index not in places:
                    places[index] = len(used)
                    used.append(held[index])

    def body(get, out, put, scratch):
        def rows_of(batch, low, high):
            parts, bottom = [], 0
            for stream in batch:
                first, last = max(low, bottom) - bottom, min(high, bottom + stream.rows) - bottom
                if first < last:
                    total = 0.0
                    for index, row in stream.terms:
                        total = total + get(places[index])[row + first : row + last, :].astype(F32)
                    parts.append(total)
                bottom += stream.rows
            return parts[0] if len(parts) == 1 else jnp.concatenate(parts)

        for k in range(2 * blocks):
            out[k // blocks][:, k % blocks * columns : (k % blocks + 1) * columns] = rows_of(
                streams["ff"], k * piece, (k + 1) * piece
            )
        for k in range(2):
            out[2 + k][...] = rows_of(streams["cross"], k * piece, (k + 1) * piece)
            low = 2 * piece + k * vis_piece
            out[4 + k][...] = rows_of(streams["cross"], low, low + vis_piece)
        for k in range(4):
            out[6 + k][...] = rows_of(streams["self"], k * piece, (k + 1) * piece)
        vectors = rows_of(streams["self"], 4 * piece, 4 * piece + 16)
        for k in range(6):
            out[10 + k][...] = vectors[k, :piece]

    return run(
        body,
        used,
        [like((piece, blocks * columns), F32)] * 2
        + [like((piece, columns), F32)] * 2
        + [like((vis_piece, columns), F32)] * 2
        + [like((piece, columns), F32)] * 4
        + [like((piece,), F32)] * 6,
        name="finish",
    )


def project(left, right):
    return jnp.dot(left, right, preferred_element_type=F32)


def head_sum(partial_rows):
    return partial_rows, partner(partial_rows, "head", 0)


def body(
    text,
    patches,
    segment_ids,
    phrase_image,
    wq_self,
    wk_self,
    wv_self,
    wo_self,
    ln1_gain,
    ln1_bias,
    wq_cross,
    wk_cross,
    wv_cross,
    wo_cross,
    ln2_gain,
    ln2_bias,
    w_in,
    w_out,
    ln3_gain,
    ln3_bias,
    cotangent,
):
    slots, patch_rows, vis = patches.shape
    half = slots // 2
    pad = -(-patch_rows // 16) * 16
    dims = (slots, patch_rows, pad)
    tokens, width = text.shape
    inner = wq_self.shape[1]
    hidden_width = w_in.shape[1]
    groups = lax.axis_size("dp") * lax.axis_size("stream")
    head = lax.axis_index("head")
    row = lambda vector: vector.reshape(1, width)

    near = partner(lax.dynamic_slice_in_dim(patches, head * half, half, 0), "stream", 0)
    projected, attended, self_stats, part1 = self_forward(
        text, wq_self, wk_self, wv_self, wo_self, segment_ids, [wk_cross, wv_cross]
    )
    attended, near = lax.optimization_barrier((attended, near))
    other = partner(near, "head", 0)
    part1_a, part1_b = head_sum(part1)
    normed1, normed1_low, cross_queries = cross_queries_of(
        text, part1_a, part1_b, row(ln1_gain), row(ln1_bias), wq_cross
    )
    keys_values = cross_keys(near, 0, wk_cross, wv_cross, ())
    keys_cross, values_cross = cross_keys(other, 1, wk_cross, wv_cross, keys_values)
    cross_attended, cross_stats, part2 = cross_forward(
        cross_queries, keys_cross, values_cross, wo_cross, segment_ids, phrase_image, dims
    )
    part2_a, part2_b = head_sum(part2)
    normed2, normed2_low, hidden, slopes, part3 = feed_forward(
        normed1, part2_a, part2_b, row(ln2_gain), row(ln2_bias), w_in, w_out
    )
    part3_a, part3_b = head_sum(part3)
    grad_residual3, grad_three_low, grad_pre, part4, norm3 = feed_backward(
        normed2, part3_a, part3_b, row(ln3_gain), cotangent, w_out, slopes, w_in
    )
    part4_a, part4_b = head_sum(part4)
    piece = width // groups
    fast = groups == 2**LINKS and piece % 16 == 0 and vis % (16 * groups) == 0
    order = Order()
    held, streams = Held(), {}
    if fast:
        streams = {name: [Stream(*stream) for stream in plan] for name, plan in PLAN.items()}
        everything = [stream for batch in streams.values() for stream in batch]
        blocks = hidden_width // inner
        links = {}
        for stream in streams["ff"]:
            links.setdefault(stream.steps[0], []).append(stream)
        for chosen in sorted(links.values(), key=lambda batch: -sum(part.rows for part in batch)):
            weight_grads(
                [order.after(grad_three_low), hidden, normed2_low, grad_pre],
                [(piece, product(0, 1, k * inner, inner)) for k in range(blocks)]
                + [(piece, product(2, 3, k * inner, inner)) for k in range(blocks)],
                streams["ff"],
                held,
                groups,
                inner,
                0,
                "ff_weight_grads",
                chosen,
            )
            away, _ = merge(chosen, 0, held, name="merge_0")
            order.passed(away)
    grad_residual2, grad_two_low, grad_cross_queries, grad_keys, grad_values, part5, norm2 = (
        cross_backward(
            order.after(grad_residual3), part4_a, part4_b, normed1, part2_a, part2_b,
            row(ln2_gain), wo_cross, cross_queries, keys_cross, values_cross, cross_stats,
            segment_ids, phrase_image, wq_cross, dims,
        )
    )
    part5_a, part5_b = head_sum(part5)
    if fast:
        def kv(which):
            def fill(get, whole):
                total = 0.0
                for slot in range(slots):
                    rows_in = get(4 + slot % 2)[slot // 2]
                    grads = get(6 + which)[slot * pad : slot * pad + patch_rows, :]
                    total = total + dot_tn(rows_in, grads)
                whole[...] = total.astype(BF16)

            return fill

        weight_grads(
            [grad_two_low, cross_attended, normed1_low, grad_cross_queries, near,
             other, grad_keys, grad_values],
            [
                (piece, product(0, 1)),
                (piece, product(2, 3)),
                (vis // groups, kv(0)),
                (vis // groups, kv(1)),
            ],
            streams["cross"],
            held,
            groups,
            inner,
            4 * tokens * width * inner + 4 * slots * pad * vis * inner,
            "cross_weight_grads",
        )
        late, _ = lax.optimization_barrier((normed2, held[-1]))
        output = last_norm(late, part3_a, part3_b, row(ln3_gain), row(ln3_bias))
        early = held.recent[0]
        held[early], output = lax.optimization_barrier((held[early], output))
        away, _ = merge(streams["ff"] + streams["cross"], 1, held, name="merge_1")
        order.passed(away)
    grad_residual1, grad_one_low, grad_qkv, part6, norm1 = self_backward(
        order.after(grad_residual2), part5_a, part5_b, text, part1_a, part1_b, row(ln1_gain),
        wo_self, projected, self_stats, segment_ids, wq_self, wk_self, wv_self,
    )
    part6_a, part6_b = head_sum(part6)
    grad_keys, _ = lax.optimization_barrier((grad_keys, grad_qkv))
    patch_own, patch_away = patch_backward(grad_keys, grad_values, wk_cross, wv_cross, dims)
    patch_other = partner(patch_away, "head", 0)
    add_patches = (
        [patch_own, patch_other],
        [like(patch_own.shape, BF16)],
        lambda get, out: out[0].__setitem__(
            ..., (get(0)[...].astype(F32) + get(1)[...].astype(F32)).astype(BF16)
        ),
    )
    grad_text = grad_residual1 + (part6_a.astype(F32) + part6_b.astype(F32))
    if fast:
        def norms(get, whole):
            rows = jnp.concatenate([get(k)[...] for k in (4, 5, 6)] + [jnp.zeros((2, width), F32)])
            inside = lax.broadcasted_iota(jnp.int32, (8, inner), 1) < piece
            for group in range(groups):
                turned = pltpu.roll(rows, (width - group * piece) % width, 1)[:, :inner]
                entry = jnp.concatenate([jnp.where(inside, turned, 0.0), jnp.zeros((8, inner), F32)])
                whole[group * 16 : (group + 1) * 16, :] = entry.astype(BF16)

        weight_grads(
            [grad_one_low, attended, text, grad_qkv, norm1, norm2, norm3],
            [(piece, product(2, 3, k * inner, inner)) for k in range(3)]
            + [(piece, product(0, 1)), (16, norms)],
            streams["self"],
            held,
            groups,
            inner,
            8 * tokens * width * inner,
            "self_weight_grads",
        )
        grad_patches = None
        early = held.recent[0]
        held[early], patch_own, _ = lax.optimization_barrier((held[early], patch_own, held[-1]))
        for phase in range(2, PHASES):
            work = add_patches if phase == PATCH_PHASE else ((), (), None)
            if phase == PATCH_PHASE + 1:
                held[-1], grad_patches = lax.optimization_barrier((held[-1], grad_patches))
            away, more = merge(everything, phase, held, *work, name="merge_%d" % phase)
            if phase == PATCH_PHASE:
                grad_patches = partner(more[0], "stream", 0)
        grad_patches = grad_patches.astype(F32)
        shares = finish(streams, held, piece, vis // groups, blocks)
        own_w_out, own_w_in, cross_wo, cross_wq, cross_wk, cross_wv = shares[:6]
        self_wq, self_wk, self_wv, self_wo = shares[6:10]
        own_w_out, cross_wo, self_wo = own_w_out.T, cross_wo.T, self_wo.T
        own_norms = shares[10:]
    else:
        patch_sum = (patch_own.astype(F32) + patch_other.astype(F32)).astype(BF16)
        grad_patches = partner(patch_sum, "stream", 0).astype(F32)
        norm_grads = jnp.concatenate([norm1, norm2, norm3, jnp.zeros((2, width), F32)])

        output = last_norm(normed2, part3_a, part3_b, row(ln3_gain), row(ln3_bias))

        def plain(left, right):
            grad = jnp.einsum("ta,tb->ab", left, right, preferred_element_type=F32)
            grad = grad.astype(BF16).reshape(groups, grad.shape[0] // groups, grad.shape[1])
            return scatter_sum_plain(grad)

        own_w_out = plain(grad_three_low, hidden).T
        own_w_in = plain(normed2_low, grad_pre)
        cross_wo = plain(grad_two_low, cross_attended).T
        cross_wq = plain(normed1_low, grad_cross_queries)
        far = jnp.stack([near, other], axis=1).reshape(slots, patch_rows, vis)
        far = jnp.pad(far, ((0, 0), (0, pad - patch_rows), (0, 0))).reshape(slots * pad, vis)
        cross_wk, cross_wv = plain(far, grad_keys), plain(far, grad_values)
        self_wq, self_wk, self_wv = jnp.split(plain(text, grad_qkv), 3, axis=1)
        self_wo = plain(grad_one_low, attended).T
        own_norms = scatter_sum_plain(
            norm_grads.reshape(8, groups, width // groups).swapaxes(0, 1).astype(BF16)
        )
    return (
        output,
        grad_text,
        grad_patches,
        self_wq,
        self_wk,
        self_wv,
        self_wo,
        own_norms[0],
        own_norms[1],
        cross_wq,
        cross_wk,
        cross_wv,
        cross_wo,
        own_norms[2],
        own_norms[3],
        own_w_in,
        own_w_out,
        own_norms[4],
        own_norms[5],
    )


def solution(mesh):
    in_specs = (
        P(("dp", "stream"), None),
        P(("dp", "stream"), None, None),
        P(("dp", "stream"), None),
        P(("dp", "stream"), None),
        P(None, "head"),
        P(None, "head"),
        P(None, "head"),
        P("head", None),
        P(),
        P(),
        P(None, "head"),
        P(None, "head"),
        P(None, "head"),
        P("head", None),
        P(),
        P(),
        P(None, "head"),
        P("head", None),
        P(),
        P(),
        P(("dp", "stream"), None),
    )
    out_specs = (
        P(("dp", "stream"), None),
        P(("dp", "stream"), None),
        P(("dp", "stream"), None, "head"),
        P(("dp", "stream"), "head"),
        P(("dp", "stream"), "head"),
        P(("dp", "stream"), "head"),
        P("head", ("dp", "stream")),
        P(("dp", "stream")),
        P(("dp", "stream")),
        P(("dp", "stream"), "head"),
        P(("dp", "stream"), "head"),
        P(("dp", "stream"), "head"),
        P("head", ("dp", "stream")),
        P(("dp", "stream")),
        P(("dp", "stream")),
        P(("dp", "stream"), "head"),
        P("head", ("dp", "stream")),
        P(("dp", "stream")),
        P(("dp", "stream")),
    )
    return jax.shard_map(body, mesh=mesh, in_specs=in_specs, out_specs=out_specs, check_vma=False)
```
